256 devices in a mesh: layer: 4 (over x_hi, core), row: 32 (over z, y), col: 2 (over x_lo).
Axes of the slice: x: 4 (x_hi: 2, x_lo: 2; x = x_hi * 2 + x_lo), y: 4, z: 8, core: 2. Of those that a mesh axis runs over, the one named last changes fastest.
Arguments:
- density: float32 [5120, 5120], P(('row', 'col'))
- pattern: int32 [80, 4], replicated, may hold values from 0 to 79
Outputs:
- purified: float32 [5120, 5120], P(('row', 'col'))
The draws below stay inside these ranges and needn't reach their ends.
All inputs are finite; a program needn't handle non-finite values.
Results may differ from the reference program's by a relative error of at most 0.00013.
Values sent between devices are 32-bit elements; how exact they have to be, the bound alone decides.
No kernel may reach another device: no remote copies, remote signals or barrier semaphores. Data moves between devices by JAX's collectives and lax.ppermute only.
A program may use at most 64 MiB of HBM per device.

```python
import math
import jax
import jax.numpy as jnp
from jax import lax

BLOCK = 64
PER_ROW = 4
ORDER = 5120
BLOCKS = 80


def draw_density(key, part):
    key = jax.random.fold_in(key, 11)
    first_key = jax.random.fold_in(key, 0)
    noise = jax.random.normal(first_key, (ORDER, ORDER), jnp.float32)
    symmetric = noise + noise.T
    return symmetric * (1.06 / math.sqrt(2 * PER_ROW * BLOCK))


def set_ends(array, rng, low, high):
    longest = array.shape.index(max(array.shape))
    spots = []
    for shift in (0, 1):
        where = [jax.random.randint(jax.random.fold_in(rng, axis), (), 0, length) for axis, length in enumerate(array.shape)]
        where[longest] = (where[longest] + shift) % array.shape[longest]
        spots.append(tuple(where))
    return array.at[spots[0]].set(low).at[spots[1]].set(high)


def setup_inputs(seed: int = 0) -> dict:
    keys = jax.random.split(jax.random.key(seed), 3)
    return {
        "density": draw_density(jax.random.fold_in(keys[2], 71), 0),
        "pattern": set_ends(jax.random.randint(keys[1], (BLOCKS, PER_ROW), 0, BLOCKS), jax.random.fold_in(keys[1], 1), 0, BLOCKS - 1).astype(jnp.int32),
    }


def block_mask(pattern):
    count = pattern.shape[0]
    labels = jnp.arange(count, dtype=jnp.int32)
    listed = jnp.any(pattern[:, :, None] == labels[None, None, :], axis=1)
    diagonal_hit = labels[:, None] == labels[None, :]
    return (listed | listed.T | diagonal_hit).astype(jnp.float32)


def reference(density, pattern):
    table = block_mask(pattern)
    element_mask = jnp.repeat(jnp.repeat(table, BLOCK, axis=0), BLOCK, axis=1)
    masked = density * element_mask
    square = jnp.dot(masked, masked.T, precision=lax.Precision.HIGHEST, preferred_element_type=jnp.float32)
    filtered = element_mask * square
    update = 4.0 * masked - 3.0 * filtered
    product = jnp.dot(filtered, update.T, precision=lax.Precision.HIGHEST, preferred_element_type=jnp.float32)
    result = element_mask * product
    return 0.5 * (result + result.T)
```

```python
import jax
import jax.numpy as jnp
from jax import lax
from jax.experimental import pallas as pl
from jax.experimental.pallas import tpu as pltpu
from jax.sharding import PartitionSpec as P

BLOCK = 64
SLOTS = 4
PIECE = 16
PIECE_ROWS = 40
LANES = 128
I32 = jnp.int32
F32 = jnp.float32
BF16 = jnp.bfloat16


def ceil_to(value, unit):
    return -(-value // unit) * unit


def pack_kernel(where_ref, pattern_ref, density_ref, out_ref, buffer, sem):
    tile = where_ref[0]
    core = where_ref[1]
    rows = density_ref.shape[0]
    pieces = rows // PIECE
    tiles, half = out_ref.shape[0], out_ref.shape[1]
    lane = lax.broadcasted_iota(I32, (PIECE, LANES), 1)
    left = lane < BLOCK
    buffer[pieces * PIECE_ROWS :, :] = jnp.zeros(
        (buffer.shape[0] - pieces * PIECE_ROWS, LANES), F32
    )

    def chunk(piece, block):
        start = pl.multiple_of((block // 2) * LANES, LANES)
        return density_ref[piece * PIECE : (piece + 1) * PIECE, pl.ds(start, LANES)]

    for piece in range(pieces):
        block_row = (tile * pieces + piece) // (BLOCK // PIECE)
        for pair in range(SLOTS // 2):
            first = pattern_ref[2 * pair, block_row]
            second = pattern_ref[2 * pair + 1, block_row]
            a = chunk(piece, first)
            b = chunk(piece, second)
            a = jnp.where(first % 2 == 0, a, pltpu.roll(a, BLOCK, 1))
            b = jnp.where(second % 2 == 1, b, pltpu.roll(b, BLOCK, 1))
            base = piece * PIECE_ROWS + pair * PIECE
            buffer[base : base + PIECE, :] = jnp.where(left, a, b)
        d = chunk(piece, block_row)
        turned = pltpu.roll(d, BLOCK, 1)
        even = jnp.where(left[:8], d[:8], turned[8:])
        odd = jnp.where(left[:8], turned[:8], d[8:])
        base = piece * PIECE_ROWS + 2 * PIECE
        buffer[base : base + 8, :] = jnp.where(block_row % 2 == 0, even, odd)

    source = buffer.at[pl.ds(pl.multiple_of(core * half, 8), half), :]

    def start(index, carry):
        pltpu.make_async_copy(source, out_ref.at[index], sem).start()
        return carry

    def wait(index, carry):
        pltpu.make_async_copy(source, out_ref.at[index], sem).wait()
        return carry

    lax.fori_loop(0, tiles, start, 0)
    lax.fori_loop(0, tiles, wait, 0)


def table_kernel(
    where_ref, pattern_ref,
    meta, xa, xd, fd, fs, fn, pairs, pd, pf,
    loc, entry, chunk_at, names, degree, written, used,
):
    blocks = pattern_ref.shape[1]
    half_blocks = (blocks + 1) // 2
    tile = where_ref[0]
    pieces = where_ref[2]
    first_row = (tile * pieces) // (BLOCK // PIECE)
    last_row = (tile * pieces + pieces - 1) // (BLOCK // PIECE)

    def clear(ref, value, unroll=16):
        count = ref.shape[0] // unroll

        def body(i, carry):
            for u in range(unroll):
                ref[i * unroll + u] = value
            return carry

        lax.fori_loop(0, count, body, 0)

    clear(loc, -1)
    clear(entry, -1)
    clear(chunk_at, 0)
    clear(written, 0)
    clear(used, 0)

    def natural(a, carry):
        for s in range(SLOTS):
            b = pattern_ref[s, a]
            loc[a * blocks + b] = a * 16 + s * 2
        return carry

    lax.fori_loop(0, blocks, natural, 0)

    def transposed(a, carry):
        for s in range(SLOTS):
            b = pattern_ref[s, a]

            @pl.when(loc[b * blocks + a] < 0)
            def _():
                loc[b * blocks + a] = a * 16 + s * 2 + 1

        return carry

    lax.fori_loop(0, blocks, transposed, 0)

    def diagonal(a, carry):
        loc[a * blocks + a] = a * 16 + SLOTS * 2
        return carry

    lax.fori_loop(0, blocks, diagonal, 0)

    def mark(r):
        def body(c, carry):
            @pl.when(loc[r * blocks + c] >= 0)
            def _():
                used[c] = 1

            return carry

        lax.fori_loop(0, blocks, body, 0)

    mark(first_row)
    mark(last_row)

    def row_body(c, carry):
        def scan(state):
            def body(j, state):
                n_x, n_e, n_n, last = state
                here = loc[c * blocks + j]

                def found():
                    q = j // 2
                    fresh = (q != last).astype(I32)
                    index = n_e + fresh
                    xa[n_x] = here
                    xd[n_x] = index * 4 + (j % 2) * 2 + fresh
                    chunk_at[c * half_blocks + q] = index
                    names[c * blocks + n_n] = j
                    return n_x + 1, index, n_n + 1, q

                return lax.cond(here >= 0, found, lambda: state)

            n_x, n_e = state
            n_x, n_e, n_n, _ = lax.fori_loop(0, blocks, body, (n_x, n_e, 0, -1))
            degree[c] = n_n
            return n_x, n_e

        return lax.cond(used[c] > 0, lambda: scan(carry), lambda: carry)

    n_x, n_e = lax.fori_loop(0, blocks, row_body, (0, 0))
    meta[0] = n_x

    def filtered_of(r, state):
        def c_body(ci, state):
            c = names[r * blocks + ci]

            def k_body(ki, state):
                k = names[r * blocks + ki]

                def emit():
                    n_f, n_g = state
                    entry[c * blocks + k] = n_f
                    index = chunk_at[c * half_blocks + k // 2]
                    fresh = 1 - written[index]
                    written[index] = 1
                    fd[n_f] = index * 4 + (k % 2) * 2 + fresh
                    fs[n_f] = n_g

                    def j_body(ji, inner):
                        count, last = inner
                        j = names[c * blocks + ji]
                        q = j // 2
                        hit = (loc[k * blocks + j] >= 0) & (q != last)

                        def push():
                            pairs[n_g * 4 + count] = (
                                chunk_at[c * half_blocks + q] * 1024
                                + chunk_at[k * half_blocks + q]
                            )
                            return count + 1, q

                        return lax.cond(hit, push, lambda: inner)

                    count, _ = lax.fori_loop(0, degree[c], j_body, (0, -1))
                    for u in range(3):
                        pairs[n_g * 4 + count + u] = 0
                    groups = (count + 3) // 4
                    fn[n_f] = groups
                    return n_f + 1, n_g + groups

                need = (loc[c * blocks + k] >= 0) & (entry[c * blocks + k] < 0)
                return lax.cond(need, emit, lambda: state)

            return lax.fori_loop(0, degree[r], k_body, state)

        return lax.fori_loop(0, degree[r], c_body, state)

    state = filtered_of(first_row, (0, 0))
    n_f, _ = filtered_of(last_row, state)
    meta[1] = n_f

    def purified_of(r, which, n_p):
        def body(ci, n_p):
            c = names[r * blocks + ci]
            pd[n_p] = c * 2 + which
            pf[n_p] = entry[r * blocks + c]
            return n_p + 1

        return lax.fori_loop(0, degree[r], body, n_p)

    n_p = purified_of(first_row, 0, 0)
    meta[2] = n_p
    n_p = purified_of(last_row, 1, n_p)
    meta[3] = n_p

    def extent(r, at):
        start = chunk_at[r * half_blocks + names[r * blocks] // 2]
        stop = chunk_at[r * half_blocks + names[r * blocks + degree[r] - 1] // 2]
        meta[at] = start
        meta[at + 1] = stop + 1

    extent(first_row, 4)
    extent(last_row, 6)
    meta[8] = tile * pieces * PIECE - first_row * BLOCK
    meta[9] = where_ref[1]


def two_parts(value):
    high = value.astype(BF16)
    low = (value - high.astype(F32)).astype(BF16)
    return jnp.concatenate([high, low], axis=0)


def times(a, b):
    return lax.dot_general(
        a, b, (((1,), (1,)), ((), ())), preferred_element_type=F32
    )


def main_kernel(
    meta, xa, xd, fd, fs, fn, pairs, pd, pf, own_ref, other_ref, out_ref,
    gathered, blocks_m, blocks_f, mixed, result, sems,
):
    rows = out_ref.shape[0]
    half = own_ref.shape[1]
    pieces = rows // PIECE
    core = meta[9]
    copies = [
        pltpu.make_async_copy(
            own_ref,
            gathered.at[:, pl.ds(pl.multiple_of(core * half, 8), half), :],
            sems.at[0],
        ),
        pltpu.make_async_copy(
            other_ref,
            gathered.at[:, pl.ds(pl.multiple_of((1 - core) * half, 8), half), :],
            sems.at[1],
        ),
    ]
    for copy in copies:
        copy.start()
    right = lax.broadcasted_iota(I32, (BLOCK, LANES), 1) // BLOCK
    blocks_m[0] = jnp.zeros((2 * BLOCK, LANES), BF16)
    blocks_f[0] = jnp.zeros((2 * BLOCK, LANES), BF16)

    def clear(i, carry):
        start = pl.multiple_of(i * LANES, LANES)
        result[:, pl.ds(start, LANES)] = jnp.zeros((result.shape[0], LANES), F32)
        return carry

    lax.fori_loop(0, result.shape[1] // LANES, clear, 0)
    for copy in copies:
        copy.wait()

    def put(store, dest, value):
        index = dest // 4
        kept = jnp.where(right == (dest // 2) % 2, value, 0.0)
        new = two_parts(kept)
        fresh = dest % 2 == 1

        @pl.when(fresh)
        def _():
            store[index] = new

        @pl.when(jnp.logical_not(fresh))
        def _():
            store[index] = store[index] + new

    def expand(i, carry):
        code = xa[i]
        dest = xd[i]
        row = code // 16
        slot = (code // 2) % 8

        def piece_at(p):
            g = row * (BLOCK // PIECE) + p
            return g // pieces, (g % pieces) * PIECE_ROWS

        @pl.when(slot == SLOTS)
        def _():
            parts = []
            for p in range(BLOCK // PIECE):
                t, at = piece_at(p)
                x = gathered[t, pl.ds(pl.multiple_of(at + 2 * PIECE, 8), 8), :]
                turned = pltpu.roll(x, BLOCK, 1)
                parts.append(jnp.where(right[:8] == 0, x, turned))
                parts.append(jnp.where(right[:8] == 0, turned, x))
            put(blocks_m, dest, jnp.concatenate(parts, axis=0))

        @pl.when(slot < SLOTS)
        def _():
            parts = []
            for p in range(BLOCK // PIECE):
                t, at = piece_at(p)
                start = pl.multiple_of(at + (slot // 2) * PIECE, 8)
                parts.append(gathered[t, pl.ds(start, PIECE), :])
            x = jnp.concatenate(parts, axis=0)
            x = jnp.where(right == slot % 2, x, pltpu.roll(x, BLOCK, 1))

            @pl.when(code % 2 == 0)
            def _():
                put(blocks_m, dest, x)

            @pl.when(code % 2 == 1)
            def _():
                square = jnp.concatenate([x, x], axis=0).T
                put(blocks_m, dest, square[:BLOCK])

        return carry

    lax.fori_loop(0, meta[0], expand, 0)

    def fold(total):
        s = total[:BLOCK] + total[BLOCK:]
        return s + pltpu.roll(s, BLOCK, 1)

    zero = jnp.zeros((2 * BLOCK, LANES), F32)

    def filtered(i, carry):
        start = fs[i]

        def group(g, total):
            for u in range(4):
                code = pairs[(start + g) * 4 + u]
                total = total + times(blocks_m[code // 1024], blocks_m[code % 1024])
            return total

        total = lax.fori_loop(0, fn[i], group, zero)
        put(blocks_f, fd[i], fold(total))
        return carry

    lax.fori_loop(0, meta[1], filtered, 0)

    for which in range(2):
        first_chunk = meta[4 + 2 * which]

        def mix(i, carry):
            m = blocks_m[i].astype(F32)
            f = blocks_f[i].astype(F32)
            mixed[i - first_chunk] = two_parts(
                m[:BLOCK] + m[BLOCK:] - 1.5 * (f[:BLOCK] + f[BLOCK:])
            )
            return carry

        lax.fori_loop(first_chunk, meta[5 + 2 * which], mix, 0)
        mixed[mixed.shape[0] - 1] = jnp.zeros((2 * BLOCK, LANES), BF16)
        spare = mixed.shape[0] - 1

        def purified(i, carry):
            e = pf[i]
            start = fs[e]

            def group(g, total):
                for u in range(4):
                    code = pairs[(start + g) * 4 + u]
                    a = code // 1024
                    b = code % 1024
                    at = jnp.where(a == 0, spare, a - first_chunk)
                    total = total + times(blocks_f[a], blocks_m[b])
                    total = total + times(mixed[at], blocks_f[b])
                return total

            total = lax.fori_loop(0, fn[e], group, zero)
            c = pd[i] // 2
            lanes = pl.ds(pl.multiple_of((c // 2) * LANES, LANES), LANES)
            band = slice(which * BLOCK, (which + 1) * BLOCK)
            value = 2.0 * fold(total)
            result[band, lanes] = result[band, lanes] + jnp.where(
                right == c % 2, value, 0.0
            )
            return carry

        lo = meta[2] if which else 0
        hi = meta[3] if which else meta[2]
        lax.fori_loop(lo, hi, purified, 0)

    final = pltpu.make_async_copy(
        result.at[pl.ds(pl.multiple_of(meta[8], PIECE), rows), :], out_ref, sems.at[0]
    )
    final.start()
    final.wait()


def smem():
    return pl.BlockSpec(memory_space=pltpu.SMEM)


def make_pack(tiles, rows, width, half):
    pieces = rows // PIECE
    return pl.pallas_call(
        pack_kernel,
        out_shape=jax.ShapeDtypeStruct((tiles, half, LANES), F32),
        in_specs=[smem(), smem(), pl.BlockSpec(memory_space=pltpu.VMEM)],
        out_specs=pl.BlockSpec(memory_space=pl.ANY),
        scratch_shapes=[
            pltpu.VMEM((2 * half, LANES), F32),
            pltpu.SemaphoreType.DMA,
        ],
        compiler_params=pltpu.CompilerParams(vmem_limit_bytes=16 << 20),
        name="pack",
    )


def sizes(blocks):
    listed = blocks * (1 + 2 * SLOTS)
    triangles = blocks * (SLOTS * (SLOTS - 1) // 2 + SLOTS * SLOTS // 3 + 1)
    triples = ceil_to(4 * listed + 4 * blocks * SLOTS + 6 * triangles, 1024)
    return ceil_to(listed, 16), triples


def make_tables(blocks):
    listed, triples = sizes(blocks)
    shapes = [16, listed, listed, listed, listed, listed, triples, ceil_to(2 * blocks, 16), ceil_to(2 * blocks, 16)]
    square = ceil_to(blocks * blocks, 16)
    return pl.pallas_call(
        table_kernel,
        out_shape=[jax.ShapeDtypeStruct((n,), I32) for n in shapes],
        in_specs=[smem(), smem()],
        out_specs=[smem()] * len(shapes),
        scratch_shapes=[
            pltpu.SMEM((square,), I32),
            pltpu.SMEM((square,), I32),
            pltpu.SMEM((ceil_to(blocks * ((blocks + 1) // 2), 16),), I32),
            pltpu.SMEM((square,), I32),
            pltpu.SMEM((ceil_to(blocks, 16),), I32),
            pltpu.SMEM((ceil_to(listed + 1, 16),), I32),
            pltpu.SMEM((ceil_to(blocks, 16),), I32),
        ],
        name="tables",
    )


def make_main(tiles, rows, width, half):
    blocks = width // BLOCK
    listed, _ = sizes(blocks)
    return pl.pallas_call(
        main_kernel,
        out_shape=jax.ShapeDtypeStruct((rows, width), F32),
        in_specs=[smem()] * 9 + [pl.BlockSpec(memory_space=pl.ANY)] * 2,
        out_specs=pl.BlockSpec(memory_space=pl.ANY),
        scratch_shapes=[
            pltpu.VMEM((tiles, 2 * half, LANES), F32),
            pltpu.VMEM((listed + 1, 2 * BLOCK, LANES), BF16),
            pltpu.VMEM((listed + 1, 2 * BLOCK, LANES), BF16),
            pltpu.VMEM(((blocks + 1) // 2 + 1, 2 * BLOCK, LANES), BF16),
            pltpu.VMEM((2 * BLOCK, width), F32),
            pltpu.SemaphoreType.DMA((2,)),
        ],
        compiler_params=pltpu.CompilerParams(vmem_limit_bytes=61 << 20),
        name="purify",
    )


def local(density, pattern):
    rows, width = density.shape
    tiles = width // rows
    pieces = rows // PIECE
    half = ceil_to(pieces * PIECE_ROWS // 2, 8)
    tile = lax.axis_index("row") * lax.axis_size("col") + lax.axis_index("col")
    layers = lax.axis_size("layer")
    core = lax.axis_index("layer") % 2
    where = jnp.stack([tile, core, jnp.int32(pieces)]).astype(I32)
    listed = pattern.T
    sent = make_pack(tiles, rows, width, half)(where, listed, density)
    own = lax.all_to_all(sent, ("row", "col"), split_axis=0, concat_axis=0, tiled=True)
    tables = make_tables(width // BLOCK)(where, listed)
    other = lax.ppermute(own, "layer", [(i, i ^ 1) for i in range(layers)])
    return make_main(tiles, rows, width, half)(*tables, own, other)


def solution(mesh):
    in_specs = (P(("row", "col"), None), P())
    out_specs = P(("row", "col"), None)
    return jax.shard_map(local, mesh=mesh, in_specs=in_specs, out_specs=out_specs, check_vma=False)
```

```python
import jax
import jax.numpy as jnp
from jax import lax
from jax.experimental import pallas as pl
from jax.experimental.pallas import tpu as pltpu
from jax.sharding import PartitionSpec as P

BLOCK = 64
SLOTS = 4
PIECE = 16
TILE = 8
LANES = 128
PIECES = BLOCK // PIECE
PARTS = SLOTS + 1
QUARTERS = 4
UNROLL = 4
GROUP = 4
I32 = jnp.int32
F32 = jnp.float32
BF16 = jnp.bfloat16


def ceil_to(value, unit):
    return -(-value // unit) * unit


def pack_kernel(where_ref, pattern_ref, density_ref, out_ref, buffer, taken, sem):
    tile = where_ref[0]
    shift = where_ref[2]
    rows = density_ref.shape[0]
    pieces = rows // PIECE
    depth, share = out_ref.shape[0], out_ref.shape[1]
    left = lax.broadcasted_iota(I32, (PIECE, LANES), 1) < BLOCK
    count = buffer.shape[0]
    for v in range(pieces * PARTS, count):
        buffer[v] = jnp.zeros((TILE, LANES), F32)

    def chunk(piece, block):
        start = pl.multiple_of((block >> 1) * LANES, LANES)
        return density_ref[piece * PIECE : (piece + 1) * PIECE, pl.ds(start, LANES)]

    for piece in range(pieces):
        block_row = (tile * pieces + piece) >> 2
        for pair in range(SLOTS // 2):
            first = pattern_ref[2 * pair, block_row]
            second = pattern_ref[2 * pair + 1, block_row]
            a = chunk(piece, first)
            b = chunk(piece, second)
            a = jnp.where((first & 1) == 0, a, pltpu.roll(a, BLOCK, 1))
            b = jnp.where((second & 1) == 1, b, pltpu.roll(b, BLOCK, 1))
            both = jnp.where(left, a, b)
            buffer[piece * PARTS + 2 * pair] = both[:TILE]
            buffer[piece * PARTS + 2 * pair + 1] = both[TILE:]
        d = chunk(piece, block_row)
        turned = pltpu.roll(d, BLOCK, 1)
        even = jnp.where(left[:TILE], d[:TILE], turned[TILE:])
        odd = jnp.where(left[:TILE], turned[:TILE], d[TILE:])
        buffer[piece * PARTS + SLOTS] = jnp.where((block_row & 1) == 0, even, odd)

    for i in range(share // TILE):
        taken[i * TILE : (i + 1) * TILE, :] = buffer[shift + QUARTERS * i]
    copies = [
        pltpu.make_async_copy(taken, out_ref.at[index], sem) for index in range(depth)
    ]
    for copy in copies:
        copy.start()
    for copy in copies:
        copy.wait()


def relay_kernel(where_ref, got_ref, out_ref, buffer, sem):
    quarter = where_ref[3]
    depth, share = got_ref.shape[0], got_ref.shape[1]
    for z in range(depth):
        extra = sum(((quarter + QUARTERS * i) < z).astype(I32) for i in range(depth // QUARTERS))
        start = pl.multiple_of((z * (share // TILE - 1) + extra) * TILE, TILE)
        buffer[pl.ds(start, share), :] = got_ref[z]
    peers, length = out_ref.shape[0], out_ref.shape[1]
    copies = [
        pltpu.make_async_copy(buffer.at[:length], out_ref.at[index], sem)
        for index in range(peers)
    ]
    for copy in copies:
        copy.start()
    for copy in copies:
        copy.wait()


def table_kernel(
    where_ref, pattern_ref,
    meta, nat_at, nat_to, tra_at, tra_to, dia_at, dia_to, fa, fb, pairs, pp, mixl,
    cq, used, flag, names, ql, qn, entry, cnt,
    *, depth, across, length, spare, pieces,
):
    blocks = pattern_ref.shape[1]
    half = (blocks + 1) // 2
    tile = where_ref[0]
    low = (2 * across).bit_length() - 1
    scale = 65536 // pieces + 1
    assert all((g * scale) >> 16 == g // pieces for g in range(blocks * PIECES))
    share = length // TILE // depth
    row_0 = (tile * pieces) >> 2
    row_1 = (tile * pieces + pieces - 1) >> 2

    def each(lo, hi, body):
        def step(i, carry):
            body(i)
            return carry

        lax.fori_loop(lo, hi, step, 0)

    def clear(ref, start, count, value, unroll=8):
        def body(i):
            for u in range(unroll):
                ref[start + i * unroll + u] = value

        each(0, count // unroll, body)

    clear(used, 0, used.shape[0], 0)
    clear(flag, 0, flag.shape[0], 0)
    clear(entry, 0, entry.shape[0], 0)
    for i in range(16):
        cnt[i] = 0

    def neighbour(which, b):
        @pl.when(flag[which * blocks + b] == 0)
        def _():
            flag[which * blocks + b] = 1
            n = cnt[which]
            names[which * blocks + n] = b
            cnt[which] = n + 1

            @pl.when(used[b] == 0)
            def _():
                used[b] = 1
                qn[b] = 0
                clear(cq, b * half, half, 0, 8 if half % 8 == 0 else 1)

    neighbour(0, row_0)
    neighbour(1, row_1)
    for s in range(SLOTS):
        neighbour(0, pattern_ref[s, row_0])
        neighbour(1, pattern_ref[s, row_1])

    def incoming(a):
        for s in range(SLOTS):
            b = pattern_ref[s, a]

            @pl.when(b == row_0)
            def _():
                neighbour(0, a)

            @pl.when(b == row_1)
            def _():
                neighbour(1, a)

    each(0, blocks, incoming)

    def address(t, v):
        z = t >> low
        y = (t >> 1) & (across - 1)
        quarter = (v + z) & (QUARTERS - 1)
        before = z * share + sum(
            ((quarter + QUARTERS * i) < z).astype(I32) for i in range(depth // QUARTERS)
        )
        peer = y * 4 + (quarter >> 1) * 2 + (t & 1)
        return (
            ((quarter & 1) * (4 * across) + peer) * length + (before + (v >> 2)) * TILE
        )

    def split(g):
        t = (g * scale) >> 16
        return t, g - t * pieces

    def block_of(c, j, put):
        q = j >> 1
        bit = 1 << (j & 1)
        word = cq[c * half + q]

        @pl.when((word & bit) == 0)
        def _():
            @pl.when(word == 0)
            def _():
                index = cnt[2] + 1
                cnt[2] = index
                n = qn[c]
                ql[c * half + n] = q
                qn[c] = n + 1
                cq[c * half + q] = index * 4 + bit

            @pl.when(word != 0)
            def _():
                cq[c * half + q] = word + bit

            put((cq[c * half + q] >> 2) * 2 + (j & 1))

    def listed(a, s, at_ref, to_ref, counter, dest):
        n = cnt[counter]
        cnt[counter] = n + 1
        to_ref[n] = dest * 2 + s % 2
        for p in range(PIECES):
            t, g = split(a * PIECES + p)
            v = g * PARTS + (s // 2) * 2
            at_ref[n * 8 + 2 * p] = address(t, v)
            at_ref[n * 8 + 2 * p + 1] = address(t, v + 1)

    def edges(a):
        mine = used[a]
        for s in range(SLOTS):
            b = pattern_ref[s, a]

            @pl.when((mine > 0) & (a != b))
            def _():
                block_of(a, b, lambda dest: listed(a, s, nat_at, nat_to, 3, dest))

            @pl.when((used[b] > 0) & (a != b))
            def _():
                block_of(b, a, lambda dest: listed(a, s, tra_at, tra_to, 4, dest))

        @pl.when(mine > 0)
        def _():
            def put(dest):
                n = cnt[5]
                cnt[5] = n + 1
                dia_to[n] = dest
                for p in range(PIECES):
                    t, g = split(a * PIECES + p)
                    dia_at[n * 4 + p] = address(t, g * PARTS + SLOTS)

            block_of(a, a, put)

    each(0, blocks, edges)

    for i in range(GROUP):
        pairs[i] = 0
    cnt[8] = 1

    def filtered_of(which, r):
        def c_body(ci):
            c = names[which * blocks + ci]
            mixed = jnp.where(c == row_0, 1, jnp.where(c == row_1, half + 2, 0))
            chunks = qn[c]

            def k_body(ki):
                k = names[which * blocks + ki]
                word = cq[c * half + (k >> 1)]
                bit = 1 << (k & 1)
                dest = (word >> 2) * 2 + (k & 1)

                @pl.when(((word & bit) != 0) & (entry[dest] == 0))
                def _():
                    group = cnt[8]
                    base = group * GROUP

                    def chunk(i, count):
                        q = ql[c * half + i]
                        a = cq[c * half + q]
                        b = cq[k * half + q]
                        at = jnp.where(mixed > 0, mixed + i, 0)
                        pairs[base + count] = (at << 20) + ((a >> 2) << 10) + (b >> 2)
                        return count + (((a & b) & 3) != 0).astype(I32)

                    count = lax.fori_loop(0, chunks, chunk, 0)
                    for u in range(GROUP):
                        pairs[base + count + u] = 0
                    groups = (count + GROUP - 1) >> 2
                    cnt[8] = group + groups
                    span = group * 32 + groups
                    entry[dest] = span
                    code = dest * (1 << 17) + span

                    @pl.when(c == k)
                    def _():
                        n = cnt[6]
                        cnt[6] = n + 1
                        fa[n] = code

                    @pl.when(c != k)
                    def _():
                        n = cnt[7]
                        cnt[7] = n + 1
                        fb[n] = code

            each(0, cnt[which], k_body)

        each(0, cnt[which], c_body)

    filtered_of(0, row_0)
    filtered_of(1, row_1)

    cnt[9] = 2
    for which, r in ((0, row_0), (1, row_1)):

        def result(ci, which=which, r=r):
            c = names[which * blocks + ci]
            word = cq[r * half + (c >> 1)]
            span = entry[(word >> 2) * 2 + (c & 1)]
            code = (c * 2 + which) * (1 << 17) + span

            @pl.when(c == r)
            def _():
                pp[which] = code

            @pl.when(c != r)
            def _():
                n = cnt[9]
                cnt[9] = n + 1
                pp[n] = code

        each(0, cnt[which], result)
        at = which * (half + 1)
        mixl[at] = 0

        def mix(i, at=at, r=r):
            mixl[at + 1 + i] = cq[r * half + ql[r * half + i]] >> 2

        each(0, qn[r], mix)

    for u in range(UNROLL):
        nat_to[cnt[3] + u] = spare * 4
        tra_to[cnt[4] + u] = spare * 4
        dia_to[cnt[5] + u] = spare * 2
        for i in range(8):
            nat_at[(cnt[3] + u) * 8 + i] = 0
            tra_at[(cnt[4] + u) * 8 + i] = 0
        for i in range(4):
            dia_at[(cnt[5] + u) * 4 + i] = 0
        fa[cnt[6] + u] = spare * (1 << 18)
        fb[cnt[7] + u] = spare * (1 << 18)
        pp[cnt[9] + u] = 0

    for i in range(10):
        meta[i] = cnt[i]
    meta[10] = qn[row_0]
    meta[11] = qn[row_1]
    meta[12] = tile * pieces * PIECE - row_0 * BLOCK
    meta[13] = where_ref[1]


def two_parts(value):
    high = value.astype(BF16)
    low = (value - high.astype(F32)).astype(BF16)
    return jnp.concatenate([high, low], axis=0)


def times(lhs, rhs):
    return lax.dot_general(
        jnp.concatenate(lhs, axis=1),
        jnp.concatenate(rhs, axis=1),
        (((1,), (1,)), ((), ())),
        preferred_element_type=F32,
    )


def main_kernel(
    meta, nat_at, nat_to, tra_at, tra_to, dia_at, dia_to, fa, fb, pairs, pp, mixl,
    own_ref, other_ref, out_ref,
    gathered, blocks_m, blocks_f, mixed, result, sums, sems,
):
    rows = out_ref.shape[0]
    length = own_ref.shape[0] * own_ref.shape[1]
    peers, span = own_ref.shape[0], own_ref.shape[1]
    core = meta[13]
    copies = [
        pltpu.make_async_copy(own_ref, gathered.at[pl.ds(core * peers, peers)], sems.at[0]),
        pltpu.make_async_copy(
            other_ref, gathered.at[pl.ds((1 - core) * peers, peers)], sems.at[1]
        ),
    ]
    for copy in copies:
        copy.start()
    right = lax.broadcasted_iota(I32, (BLOCK, LANES), 1) // BLOCK
    none = jnp.zeros((2 * BLOCK, LANES), BF16)

    def each(lo, hi, body):
        def step(i, carry):
            body(i)
            return carry

        lax.fori_loop(lo, hi, step, 0)

    def clear(i):
        blocks_m[i] = none
        blocks_f[i] = none

    each(0, meta[2] + 1, clear)

    def clear_result(i):
        start = pl.multiple_of(i * LANES, LANES)
        result[:, pl.ds(start, LANES)] = jnp.zeros((result.shape[0], LANES), F32)

    each(0, result.shape[1] // LANES, clear_result)
    mixed[0] = none
    flat = gathered.reshape(2 * length, LANES)
    for copy in copies:
        copy.wait()

    def steps(count):
        return (count + UNROLL - 1) >> 2

    def rows_at(at_ref, n, count):
        return [
            flat[pl.ds(pl.multiple_of(at_ref[n * count + i], TILE), TILE), :]
            for i in range(count)
        ]

    def add(store, index, value):
        store[index] = store[index] + two_parts(value)

    def natural(i):
        for u in range(UNROLL):
            n = i * UNROLL + u
            to = nat_to[n]
            parity = (to >> 1) & 1
            x = jnp.concatenate(rows_at(nat_at, n, 8), axis=0)
            x = jnp.where((to & 1) == parity, x, pltpu.roll(x, BLOCK, 1))
            add(blocks_m, to >> 2, jnp.where(right == parity, x, 0.0))

    def transposed(i):
        for u in range(UNROLL):
            n = i * UNROLL + u
            to = tra_to[n]
            parity = (to >> 1) & 1
            x = jnp.concatenate(rows_at(tra_at, n, 8), axis=0).T
            x = jnp.where((to & 1) == 0, x[:BLOCK], x[BLOCK:])
            x = jnp.concatenate([x, x], axis=1)
            add(blocks_m, to >> 2, jnp.where(right == parity, x, 0.0))

    def diagonal(i):
        for u in range(UNROLL):
            n = i * UNROLL + u
            to = dia_to[n]
            parity = to & 1
            parts = []
            for x in rows_at(dia_at, n, 4):
                turned = pltpu.roll(x, BLOCK, 1)
                parts.append(jnp.where(right[:TILE] == 0, x, turned))
                parts.append(jnp.where(right[:TILE] == 0, turned, x))
            x = jnp.concatenate(parts, axis=0)
            add(blocks_m, to >> 1, jnp.where(right == parity, x, 0.0))

    each(0, steps(meta[3]), natural)
    each(0, steps(meta[4]), transposed)
    each(0, steps(meta[5]), diagonal)

    def fold(total):
        s = total[:BLOCK] + total[BLOCK:]
        return s + pltpu.roll(s, BLOCK, 1)

    def codes_of(word, g):
        n = word & 31
        group = jnp.where(g < n, ((word >> 5) & 4095) + g, 0)
        return [pairs[group * GROUP + u] for u in range(GROUP)]

    def filtered(list_ref, static):
        def product(word, groups):
            lhs, rhs = [], []
            for g in groups:
                for code in codes_of(word, g):
                    lhs.append(blocks_m[(code >> 10) & 1023])
                    rhs.append(blocks_m[code & 1023])
            return times(lhs, rhs)

        def body(i):
            words = [list_ref[i * UNROLL + u] for u in range(UNROLL)]
            for u in range(UNROLL):
                sums[u] = product(words[u], range(static))
            most = words[0] & 31
            for word in words[1:]:
                most = jnp.maximum(most, word & 31)

            def more(g):
                for u in range(UNROLL):
                    sums[u] = sums[u] + product(words[u], [g])

            each(static, most, more)
            for u in range(UNROLL):
                dest = words[u] >> 17
                value = fold(sums[u])
                add(blocks_f, dest >> 1, jnp.where(right == (dest & 1), value, 0.0))

        return body

    each(0, steps(meta[6]), filtered(fa, 3))
    each(0, steps(meta[7]), filtered(fb, 1))

    for which in range(2):
        start = which * (mixl.shape[0] // 2) + 1

        def mix(i, start=start):
            index = mixl[start + i]
            m = blocks_m[index].astype(F32)
            f = blocks_f[index].astype(F32)
            mixed[start + i] = two_parts(
                m[:BLOCK] + m[BLOCK:] - 1.5 * (f[:BLOCK] + f[BLOCK:])
            )

        each(0, meta[10 + which], mix)

    def purified(first, count, static, i):
        def product(word, groups):
            lhs, rhs = [], []
            for g in groups:
                for code in codes_of(word, g):
                    lhs += [blocks_f[(code >> 10) & 1023], mixed[code >> 20]]
                    rhs += [blocks_m[code & 1023], blocks_f[code & 1023]]
            return times(lhs, rhs)

        words = [pp[first + i * count + u] for u in range(count)]
        for u in range(count):
            sums[u] = product(words[u], range(static))
        most = words[0] & 31
        for word in words[1:]:
            most = jnp.maximum(most, word & 31)

        def more(g):
            for u in range(count):
                sums[u] = sums[u] + product(words[u], [g])

        each(static, most, more)
        for u in range(count):
            c = words[u] >> 18
            which = (words[u] >> 17) & 1
            lanes = pl.ds(pl.multiple_of((c >> 1) * LANES, LANES), LANES)
            band = pl.ds(pl.multiple_of(which * BLOCK, BLOCK), BLOCK)
            value = 2.0 * fold(sums[u])
            result[band, lanes] = result[band, lanes] + jnp.where(
                right == (c & 1), value, 0.0
            )

    purified(0, 2, 3, 0)
    each(0, steps(meta[9] - 2), lambda i: purified(2, UNROLL, 1, i))

    final = pltpu.make_async_copy(
        result.at[pl.ds(pl.multiple_of(meta[12], PIECE), rows), :], out_ref, sems.at[0]
    )
    final.start()
    final.wait()


def smem():
    return pl.BlockSpec(memory_space=pltpu.SMEM)


def make_pack(depth, rows, share):
    count = ceil_to(rows // PIECE * PARTS, QUARTERS)
    return pl.pallas_call(
        pack_kernel,
        out_shape=jax.ShapeDtypeStruct((depth, share, LANES), F32),
        in_specs=[smem(), smem(), pl.BlockSpec(memory_space=pltpu.VMEM)],
        out_specs=pl.BlockSpec(memory_space=pl.ANY),
        scratch_shapes=[
            pltpu.VMEM((count, TILE, LANES), F32),
            pltpu.VMEM((share, LANES), F32),
            pltpu.SemaphoreType.DMA,
        ],
        compiler_params=pltpu.CompilerParams(vmem_limit_bytes=16 << 20),
        name="pack",
    )


def make_relay(depth, share, peers, length):
    return pl.pallas_call(
        relay_kernel,
        out_shape=jax.ShapeDtypeStruct((peers, length, LANES), F32),
        in_specs=[smem(), pl.BlockSpec(memory_space=pltpu.VMEM)],
        out_specs=pl.BlockSpec(memory_space=pltpu.HBM),
        scratch_shapes=[
            pltpu.VMEM((length + TILE, LANES), F32),
            pltpu.SemaphoreType.DMA,
        ],
        compiler_params=pltpu.CompilerParams(vmem_limit_bytes=16 << 20),
        name="relay",
    )


def sizes(blocks):
    listed = blocks * (1 + 2 * SLOTS)
    triangles = blocks * (SLOTS * (SLOTS - 1) // 2 + SLOTS * SLOTS // 3 + 1)
    triples = ceil_to(4 * listed + 4 * blocks * SLOTS + 6 * triangles + 64, 1024)
    return listed, triples


def make_tables(blocks, depth, across, length, pieces):
    listed, triples = sizes(blocks)
    half = (blocks + 1) // 2
    edges = blocks * SLOTS + UNROLL
    diagonal = blocks + UNROLL
    shapes = [
        16, edges * 8, edges, edges * 8, edges, diagonal * 4, diagonal,
        diagonal, listed + UNROLL, triples, 2 * blocks + 2 + UNROLL, 2 * (half + 1),
    ]

    def kernel(*refs):
        table_kernel(*refs, depth=depth, across=across, length=length, spare=listed + 1, pieces=pieces)

    scratch = [
        blocks * half, ceil_to(blocks, 8), ceil_to(2 * blocks, 8), 2 * blocks,
        blocks * half, blocks, ceil_to(2 * (listed + 2), 8), 16,
    ]
    return pl.pallas_call(
        kernel,
        out_shape=[jax.ShapeDtypeStruct((n,), I32) for n in shapes],
        in_specs=[smem(), smem()],
        out_specs=[smem()] * len(shapes),
        scratch_shapes=[pltpu.SMEM((n,), I32) for n in scratch],
        compiler_params=pltpu.CompilerParams(vmem_limit_bytes=61 << 20),
        cost_estimate=pl.CostEstimate(
            flops=40_000_000_000, bytes_accessed=100_000_000, transcendentals=0
        ),
        name="tables",
    )


def make_main(rows, width, peers, length):
    blocks = width // BLOCK
    half = (blocks + 1) // 2
    listed, _ = sizes(blocks)
    return pl.pallas_call(
        main_kernel,
        out_shape=jax.ShapeDtypeStruct((rows, width), F32),
        in_specs=[smem()] * 12 + [pl.BlockSpec(memory_space=pltpu.HBM)] * 2,
        out_specs=pl.BlockSpec(memory_space=pl.ANY),
        scratch_shapes=[
            pltpu.VMEM((2 * peers, length, LANES), F32),
            pltpu.VMEM((listed + 2, 2 * BLOCK, LANES), BF16),
            pltpu.VMEM((listed + 2, 2 * BLOCK, LANES), BF16),
            pltpu.VMEM((2 * (half + 1), 2 * BLOCK, LANES), BF16),
            pltpu.VMEM((2 * BLOCK, width), F32),
            pltpu.VMEM((UNROLL, 2 * BLOCK, LANES), F32),
            pltpu.SemaphoreType.DMA((2,)),
        ],
        compiler_params=pltpu.CompilerParams(vmem_limit_bytes=61 << 20),
        name="purify",
    )


def local(density, pattern):
    rows, width = density.shape
    layers, lines, cols = (lax.axis_size(a) for a in ("layer", "row", "col"))
    across = 4
    depth = lines // across
    pieces = rows // PIECE
    share = ceil_to(pieces * PARTS, QUARTERS) // QUARTERS * TILE
    length = pieces * PARTS * depth // QUARTERS * TILE
    wide = layers // 2 * cols
    peers = across * wide
    line, col, layer = (lax.axis_index(a) for a in ("row", "col", "layer"))
    tile = line * cols + col
    z = line // across
    where = jnp.stack(
        [tile, layer % 2, (layer - z) % QUARTERS, layer]
    ).astype(I32)
    listed = pattern.T

    packed = make_pack(depth, rows, share)(where, listed, density)
    along = [[z * across + y for z in range(depth)] for y in range(across)]
    got = lax.all_to_all(
        packed, "row", split_axis=0, concat_axis=0, tiled=True, axis_index_groups=along
    )
    relayed = make_relay(depth, share, peers, length)(where, got)
    planes = [
        [
            ((x // cols * 2 + core) * lines + z * across + y) * cols + x % cols
            for y in range(across)
            for x in range(wide)
        ]
        for z in range(depth)
        for core in range(2)
    ]
    own = lax.all_to_all(
        relayed, ("layer", "row", "col"), split_axis=0, concat_axis=0, tiled=True,
        axis_index_groups=planes,
    )
    where, relayed = lax.optimization_barrier((where, relayed))
    tables = make_tables(width // BLOCK, depth, across, length, pieces)(where, listed)
    own, tables = lax.optimization_barrier((own, tables))
    other = lax.ppermute(own, "layer", [(i, i ^ 1) for i in range(layers)])
    return make_main(rows, width, peers, length)(*tables, own, other)


def solution(mesh):
    in_specs = (P(("row", "col"), None), P())
    out_specs = P(("row", "col"), None)
    return jax.shard_map(local, mesh=mesh, in_specs=in_specs, out_specs=out_specs, check_vma=False)
```

```python
import jax
import jax.numpy as jnp
from jax import lax
from jax.experimental import pallas as pl
from jax.experimental.pallas import tpu as pltpu
from jax.sharding import PartitionSpec as P

BLOCK = 64
SLOTS = 4
PIECE = 16
TILE = 8
LANES = 128
PIECES = BLOCK // PIECE
PARTS = SLOTS + 1
QUARTERS = 4
UNROLL = 4
GROUP = 4
I32 = jnp.int32
F32 = jnp.float32
BF16 = jnp.bfloat16


def ceil_to(value, unit):
    return -(-value // unit) * unit


def pack_kernel(where_ref, pattern_ref, density_ref, out_ref, buffer, taken, sem):
    tile = where_ref[0]
    shift = where_ref[2]
    rows = density_ref.shape[0]
    pieces = rows // PIECE
    depth, share = out_ref.shape[0], out_ref.shape[1]
    left = lax.broadcasted_iota(I32, (PIECE, LANES), 1) < BLOCK
    count = buffer.shape[0]
    for v in range(pieces * PARTS, count):
        buffer[v] = jnp.zeros((TILE, LANES), F32)

    def chunk(piece, block):
        start = pl.multiple_of((block >> 1) * LANES, LANES)
        return density_ref[piece * PIECE : (piece + 1) * PIECE, pl.ds(start, LANES)]

    for piece in range(pieces):
        block_row = (tile * pieces + piece) >> 2
        for pair in range(SLOTS // 2):
            first = pattern_ref[2 * pair, block_row]
            second = pattern_ref[2 * pair + 1, block_row]
            a = chunk(piece, first)
            b = chunk(piece, second)
            a = jnp.where((first & 1) == 0, a, pltpu.roll(a, BLOCK, 1))
            b = jnp.where((second & 1) == 1, b, pltpu.roll(b, BLOCK, 1))
            both = jnp.where(left, a, b)
            buffer[piece * PARTS + 2 * pair] = both[:TILE]
            buffer[piece * PARTS + 2 * pair + 1] = both[TILE:]
        d = chunk(piece, block_row)
        turned = pltpu.roll(d, BLOCK, 1)
        even = jnp.where(left[:TILE], d[:TILE], turned[TILE:])
        odd = jnp.where(left[:TILE], turned[:TILE], d[TILE:])
        buffer[piece * PARTS + SLOTS] = jnp.where((block_row & 1) == 0, even, odd)

    for i in range(share // TILE):
        taken[i * TILE : (i + 1) * TILE, :] = buffer[shift + QUARTERS * i]
    copies = [
        pltpu.make_async_copy(taken, out_ref.at[index], sem) for index in range(depth)
    ]
    for copy in copies:
        copy.start()
    for copy in copies:
        copy.wait()


def relay_kernel(where_ref, got_ref, out_ref, buffer, sem):
    quarter = where_ref[3]
    depth, share = got_ref.shape[0], got_ref.shape[1]
    for z in range(depth):
        extra = sum(((quarter + QUARTERS * i) < z).astype(I32) for i in range(depth // QUARTERS))
        start = pl.multiple_of((z * (share // TILE - 1) + extra) * TILE, TILE)
        buffer[pl.ds(start, share), :] = got_ref[z]
    peers, length = out_ref.shape[0], out_ref.shape[1]
    copies = [
        pltpu.make_async_copy(buffer.at[:length], out_ref.at[index], sem)
        for index in range(peers)
    ]
    for copy in copies:
        copy.start()
    for copy in copies:
        copy.wait()


def repeat_kernel(got_ref, out_ref, sem):
    copies = [
        pltpu.make_async_copy(got_ref, out_ref.at[index], sem)
        for index in range(out_ref.shape[0])
    ]
    for copy in copies:
        copy.start()
    for copy in copies:
        copy.wait()


class Part:
    def __init__(self, ref, start):
        self.ref, self.start = ref, start

    def __getitem__(self, i):
        return self.ref[self.start + i]

    def __setitem__(self, i, value):
        self.ref[self.start + i] = value


def parts_of(ref, lengths):
    parts, start = [], 0
    for length in lengths:
        parts.append(Part(ref, start))
        start += length
    return parts


def each(lo, hi, body):
    def step(i, carry):
        body(i)
        return carry

    lax.fori_loop(lo, hi, step, 0)


def clear(ref, start, count, value, unroll=8):
    def body(i):
        for u in range(unroll):
            ref[start + i * unroll + u] = value

    each(0, count // unroll, body)


def row_of(where_ref, pieces):
    first = where_ref[0] * pieces
    return jnp.where(where_ref[1] == 0, first >> 2, (first + pieces - 1) >> 2)


def neighbour_kernel(where_ref, pattern_ref, book, *, pieces):
    blocks = pattern_ref.shape[1]
    cnt, used, names = parts_of(book, book_lengths(blocks))
    r = row_of(where_ref, pieces)
    clear(book, 0, 16 + blocks, 0)

    def neighbour(b):
        @pl.when(used[b] == 0)
        def _():
            used[b] = 1
            n = cnt[0]
            names[n] = b
            cnt[0] = n + 1

    neighbour(r)
    for s in range(SLOTS):
        neighbour(pattern_ref[s, r])

    def incoming(a):
        hit = pattern_ref[0, a] == r
        for s in range(1, SLOTS):
            hit = hit | (pattern_ref[s, a] == r)

        @pl.when(hit)
        def _():
            neighbour(a)

    each(0, blocks, incoming)


def edge_kernel(
    where_ref, pattern_ref, book, lists, state,
    *, depth, across, length, spare, pieces,
):
    blocks = pattern_ref.shape[1]
    known, used, names = parts_of(book, book_lengths(blocks))
    meta, nat_at, nat_to, tra_at, tra_to, dia_at, dia_to = parts_of(lists, block_lengths(blocks))
    cnt, qn, cq, ql = parts_of(state, state_lengths(blocks))
    half = (blocks + 1) // 2
    low = (2 * across).bit_length() - 1
    scale = 65536 // pieces + 1
    assert all((g * scale) >> 16 == g // pieces for g in range(blocks * PIECES))
    share = length // TILE // depth
    clear(state, 0, 16, 0)

    def start(i):
        c = names[i]
        qn[c] = 0
        clear(state, 16 + blocks + c * half, half, 0, 8 if half % 8 == 0 else 1)

    each(0, known[0], start)

    def address(t, v):
        z = t >> low
        y = (t >> 1) & (across - 1)
        quarter = (v + z) & (QUARTERS - 1)
        before = z * share + sum(
            ((quarter + QUARTERS * i) < z).astype(I32) for i in range(depth // QUARTERS)
        )
        x = (quarter >> 1) * 2 + (t & 1)
        core = quarter & 1
        peer = jnp.where(core == 0, y * 4 + x, x * 4 + y)
        return (core * (4 * across) + peer) * length + (before + (v >> 2)) * TILE

    def split(g):
        t = (g * scale) >> 16
        return t, g - t * pieces

    def block_of(c, j, put):
        q = j >> 1
        bit = 1 << (j & 1)
        word = cq[c * half + q]

        @pl.when((word & bit) == 0)
        def _():
            fresh = word == 0
            index = jnp.where(fresh, cnt[2] + 1, word >> 2)
            cnt[2] = cnt[2] + fresh.astype(I32)
            n = qn[c]
            ql[c * half + jnp.where(fresh, n, half - 1)] = jnp.where(
                fresh, q, ql[c * half + half - 1]
            )
            qn[c] = n + fresh.astype(I32)
            cq[c * half + q] = jnp.where(fresh, index * 4, word) + bit
            put(index * 2 + (j & 1))

    def listed(a, s, at_ref, to_ref, counter, dest):
        n = cnt[counter]
        cnt[counter] = n + 1
        to_ref[n] = dest * 2 + s % 2
        for p in range(PIECES):
            t, g = split(a * PIECES + p)
            v = g * PARTS + (s // 2) * 2
            at_ref[n * 8 + 2 * p] = address(t, v)
            at_ref[n * 8 + 2 * p + 1] = address(t, v + 1)

    def edges(a):
        mine = used[a]
        ends = [pattern_ref[s, a] for s in range(SLOTS)]
        any_used = mine
        for b in ends:
            any_used = any_used | used[b]

        @pl.when(any_used > 0)
        def _():
            for s, b in enumerate(ends):

                @pl.when((mine > 0) & (a != b))
                def _():
                    block_of(a, b, lambda dest: listed(a, s, nat_at, nat_to, 3, dest))

                @pl.when((used[b] > 0) & (a != b))
                def _():
                    block_of(b, a, lambda dest: listed(a, s, tra_at, tra_to, 4, dest))

            @pl.when(mine > 0)
            def _():
                def put(dest):
                    n = cnt[5]
                    cnt[5] = n + 1
                    dia_to[n] = dest
                    for p in range(PIECES):
                        t, g = split(a * PIECES + p)
                        dia_at[n * 4 + p] = address(t, g * PARTS + SLOTS)

                block_of(a, a, put)

    each(0, blocks, edges)

    for u in range(UNROLL):
        nat_to[cnt[3] + u] = spare * 4
        tra_to[cnt[4] + u] = spare * 4
        dia_to[cnt[5] + u] = spare * 2
        for i in range(8):
            nat_at[(cnt[3] + u) * 8 + i] = 0
            tra_at[(cnt[4] + u) * 8 + i] = 0
        for i in range(4):
            dia_at[(cnt[5] + u) * 4 + i] = 0
    for i in range(6):
        meta[i] = cnt[i]
    meta[13] = where_ref[1]


def product_kernel(
    where_ref, book, state, lists, pairs, entry, cnt, *, blocks, spare, pieces
):
    known, _, names = parts_of(book, book_lengths(blocks))
    _, qn, cq, ql = parts_of(state, state_lengths(blocks))
    meta, fa, fb = parts_of(lists, product_lengths(blocks))
    half = (blocks + 1) // 2
    r = row_of(where_ref, pieces)
    for i in range(16):
        cnt[i] = 0
    cnt[0] = known[0]
    for i in range(GROUP):
        pairs[i] = 0
    cnt[8] = 1

    def c_body(ci):
        c = names[ci]
        chunks = qn[c]
        mine = c == r

        def k_body(ki):
            k = names[ki]
            word = cq[c * half + (k >> 1)]
            bit = 1 << (k & 1)
            dest = (word >> 2) * 2 + (k & 1)

            @pl.when((word & bit) != 0)
            def _():
                group = cnt[8]
                base = group * GROUP

                def chunk(i, count):
                    q = ql[c * half + i]
                    a = cq[c * half + q]
                    b = cq[k * half + q]
                    at = jnp.where(mine, 1 + i, 0)
                    pairs[base + count] = (at << 20) + ((a >> 2) << 10) + (b >> 2)
                    return count + (((a & b) & 3) != 0).astype(I32)

                count = lax.fori_loop(0, chunks, chunk, 0)
                for u in range(GROUP):
                    pairs[base + count + u] = 0
                groups = (count + GROUP - 1) >> 2
                cnt[8] = group + groups
                span = group * 32 + groups
                entry[dest] = span
                code = dest * (1 << 17) + span

                @pl.when(c == k)
                def _():
                    n = cnt[6]
                    cnt[6] = n + 1
                    fa[n] = code

                @pl.when(c != k)
                def _():
                    n = cnt[7]
                    cnt[7] = n + 1
                    fb[n] = code

        each(0, cnt[0], k_body)

    each(0, cnt[0], c_body)

    for u in range(UNROLL):
        fa[cnt[6] + u] = spare * (1 << 18)
        fb[cnt[7] + u] = spare * (1 << 18)
    meta[6] = cnt[6]
    meta[7] = cnt[7]


def result_kernel(where_ref, book, state, entry, lists, *, blocks, pieces):
    known, _, names = parts_of(book, book_lengths(blocks))
    _, qn, cq, ql = parts_of(state, state_lengths(blocks))
    meta, pp, mixl = parts_of(lists, result_lengths(blocks))
    half = (blocks + 1) // 2
    r = row_of(where_ref, pieces)

    def result(ci, n):
        c = names[ci]
        word = cq[r * half + (c >> 1)]
        code = c * (1 << 17) + entry[(word >> 2) * 2 + (c & 1)]
        pp[jnp.where(c == r, 0, n)] = code
        return jnp.where(c == r, n, n + 1)

    n = lax.fori_loop(0, known[0], result, 1)
    mixl[0] = 0

    def mix(i):
        mixl[1 + i] = cq[r * half + ql[r * half + i]] >> 2

    each(0, qn[r], mix)
    for u in range(UNROLL):
        pp[n + u] = 0
    meta[9] = n
    meta[10] = qn[r]


def two_parts(value):
    high = value.astype(BF16)
    low = (value - high.astype(F32)).astype(BF16)
    return jnp.concatenate([high, low], axis=0)


def times(lhs, rhs):
    return lax.dot_general(
        jnp.concatenate(lhs, axis=1),
        jnp.concatenate(rhs, axis=1),
        (((1,), (1,)), ((), ())),
        preferred_element_type=F32,
    )


def main_kernel(
    where_ref, block_lists, product_lists, pairs, result_lists, own_ref, other_ref, full_ref, result,
    gathered, blocks_m, blocks_f, mixed, sums, sems,
):
    blocks = result.shape[1] // BLOCK
    meta, nat_at, nat_to, tra_at, tra_to, dia_at, dia_to = parts_of(
        block_lists, block_lengths(blocks)
    )
    counts, fa, fb = parts_of(product_lists, product_lengths(blocks))
    extent, pp, mixl = parts_of(result_lists, result_lengths(blocks))
    length = own_ref.shape[0] * own_ref.shape[1]
    peers, span = own_ref.shape[0], own_ref.shape[1]
    core = meta[13]
    copies = [
        pltpu.make_async_copy(own_ref, gathered.at[pl.ds(core * peers, peers)], sems.at[0]),
        pltpu.make_async_copy(
            other_ref, gathered.at[pl.ds((1 - core) * peers, peers)], sems.at[1]
        ),
    ]
    for copy in copies:
        copy.start()
    right = lax.broadcasted_iota(I32, (BLOCK, LANES), 1) // BLOCK
    none = jnp.zeros((2 * BLOCK, LANES), BF16)

    def clear_blocks(i):
        blocks_m[i] = none
        blocks_f[i] = none

    each(0, meta[2] + 1, clear_blocks)

    def clear_result(i):
        start = pl.multiple_of(i * LANES, LANES)
        result[:, pl.ds(start, LANES)] = jnp.zeros((result.shape[0], LANES), F32)

    each(0, result.shape[1] // LANES, clear_result)
    mixed[0] = none
    flat = gathered.reshape(2 * length, LANES)
    for copy in copies:
        copy.wait()

    def steps(count):
        return (count + UNROLL - 1) >> 2

    def rows_at(at_ref, n, count):
        return [
            flat[pl.ds(pl.multiple_of(at_ref[n * count + i], TILE), TILE), :]
            for i in range(count)
        ]

    def add(store, index, value):
        store[index] = store[index] + two_parts(value)

    def natural(i):
        for u in range(UNROLL):
            n = i * UNROLL + u
            to = nat_to[n]
            parity = (to >> 1) & 1
            x = jnp.concatenate(rows_at(nat_at, n, 8), axis=0)
            x = jnp.where((to & 1) == parity, x, pltpu.roll(x, BLOCK, 1))
            add(blocks_m, to >> 2, jnp.where(right == parity, x, 0.0))

    def transposed(i):
        for u in range(UNROLL):
            n = i * UNROLL + u
            to = tra_to[n]
            parity = (to >> 1) & 1
            x = jnp.concatenate(rows_at(tra_at, n, 8), axis=0).T
            x = jnp.where((to & 1) == 0, x[:BLOCK], x[BLOCK:])
            x = jnp.concatenate([x, x], axis=1)
            add(blocks_m, to >> 2, jnp.where(right == parity, x, 0.0))

    def diagonal(i):
        for u in range(UNROLL):
            n = i * UNROLL + u
            to = dia_to[n]
            parity = to & 1
            parts = []
            for x in rows_at(dia_at, n, 4):
                turned = pltpu.roll(x, BLOCK, 1)
                parts.append(jnp.where(right[:TILE] == 0, x, turned))
                parts.append(jnp.where(right[:TILE] == 0, turned, x))
            x = jnp.concatenate(parts, axis=0)
            add(blocks_m, to >> 1, jnp.where(right == parity, x, 0.0))

    each(0, steps(meta[3]), natural)
    each(0, steps(meta[4]), transposed)
    each(0, steps(meta[5]), diagonal)

    def fold(total):
        s = total[:BLOCK] + total[BLOCK:]
        return s + pltpu.roll(s, BLOCK, 1)

    def codes_of(word, g):
        n = word & 31
        group = jnp.where(g < n, ((word >> 5) & 4095) + g, 0)
        return [pairs[group * GROUP + u] for u in range(GROUP)]

    def filtered(list_ref, static):
        def product(word, groups):
            lhs, rhs = [], []
            for g in groups:
                for code in codes_of(word, g):
                    lhs.append(blocks_m[(code >> 10) & 1023])
                    rhs.append(blocks_m[code & 1023])
            return times(lhs, rhs)

        def body(i):
            words = [list_ref[i * UNROLL + u] for u in range(UNROLL)]
            for u in range(UNROLL):
                sums[u] = product(words[u], range(static))
            most = words[0] & 31
            for word in words[1:]:
                most = jnp.maximum(most, word & 31)

            def more(g):
                for u in range(UNROLL):
                    sums[u] = sums[u] + product(words[u], [g])

            each(static, most, more)
            for u in range(UNROLL):
                dest = words[u] >> 17
                value = fold(sums[u])
                add(blocks_f, dest >> 1, jnp.where(right == (dest & 1), value, 0.0))

        return body

    each(0, steps(counts[6]), filtered(fa, 3))
    each(0, steps(counts[7]), filtered(fb, 1))

    def mix(i):
        index = mixl[1 + i]
        m = blocks_m[index].astype(F32)
        f = blocks_f[index].astype(F32)
        mixed[1 + i] = two_parts(
            m[:BLOCK] + m[BLOCK:] - 1.5 * (f[:BLOCK] + f[BLOCK:])
        )

    each(0, extent[10], mix)

    def purified(first, count, static, i):
        def product(word, groups):
            lhs, rhs = [], []
            for g in groups:
                for code in codes_of(word, g):
                    lhs += [blocks_f[(code >> 10) & 1023], mixed[code >> 20]]
                    rhs += [blocks_m[code & 1023], blocks_f[code & 1023]]
            return times(lhs, rhs)

        words = [pp[first + i * count + u] for u in range(count)]
        for u in range(count):
            sums[u] = product(words[u], range(static))
        most = words[0] & 31
        for word in words[1:]:
            most = jnp.maximum(most, word & 31)

        def more(g):
            for u in range(count):
                sums[u] = sums[u] + product(words[u], [g])

        each(static, most, more)
        for u in range(count):
            c = words[u] >> 17
            lanes = pl.ds(pl.multiple_of((c >> 1) * LANES, LANES), LANES)
            value = 2.0 * fold(sums[u])
            result[:, lanes] = result[:, lanes] + jnp.where(right == (c & 1), value, 0.0)

    purified(0, 1, 3, 0)
    each(0, steps(extent[9] - 1), lambda i: purified(1, UNROLL, 1, i))

    def act(source, target):
        copy = pltpu.make_async_copy(
            result.at[source, :], full_ref.at[target, :], sems.at[0]
        )
        copy.start()
        copy.wait()

    cases(where_ref, full_ref.shape[0], True, act)


def cases(where_ref, rows, mine, act):
    tile = where_ref[0]
    skip = tile * rows - ((tile * (rows // PIECE)) >> 2) * BLOCK
    for core in range(2):
        for cut in range(0, BLOCK, PIECE):
            if not 0 < rows - (BLOCK - cut) <= BLOCK:
                continue
            upper = (core == 0) == mine
            source = pl.ds(cut, BLOCK - cut) if upper else pl.ds(0, rows - BLOCK + cut)
            target = pl.ds(0, BLOCK - cut) if upper else pl.ds(BLOCK - cut, rows - BLOCK + cut)

            @pl.when((where_ref[1] == core) & (skip == cut))
            def _():
                act(source, target)


def assemble_kernel(where_ref, full_ref, other_ref, out_ref, sem):
    def act(source, target):
        copy = pltpu.make_async_copy(other_ref.at[source, :], out_ref.at[target, :], sem)
        copy.start()
        copy.wait()

    cases(where_ref, out_ref.shape[0], False, act)


def smem():
    return pl.BlockSpec(memory_space=pltpu.SMEM)


def make_pack(depth, rows, share):
    count = ceil_to(rows // PIECE * PARTS, QUARTERS)
    return pl.pallas_call(
        pack_kernel,
        out_shape=jax.ShapeDtypeStruct((depth, share, LANES), F32),
        in_specs=[smem(), smem(), pl.BlockSpec(memory_space=pltpu.VMEM)],
        out_specs=pl.BlockSpec(memory_space=pl.ANY),
        scratch_shapes=[
            pltpu.VMEM((count, TILE, LANES), F32),
            pltpu.VMEM((share, LANES), F32),
            pltpu.SemaphoreType.DMA,
        ],
        compiler_params=pltpu.CompilerParams(vmem_limit_bytes=16 << 20),
        name="pack",
    )


def make_relay(depth, share, peers, length):
    return pl.pallas_call(
        relay_kernel,
        out_shape=jax.ShapeDtypeStruct((peers, length, LANES), F32),
        in_specs=[smem(), pl.BlockSpec(memory_space=pltpu.VMEM)],
        out_specs=pl.BlockSpec(memory_space=pltpu.HBM),
        scratch_shapes=[
            pltpu.VMEM((length + TILE, LANES), F32),
            pltpu.SemaphoreType.DMA,
        ],
        compiler_params=pltpu.CompilerParams(vmem_limit_bytes=16 << 20),
        name="relay",
    )


def make_repeat(count, shape):
    return pl.pallas_call(
        repeat_kernel,
        out_shape=jax.ShapeDtypeStruct((count,) + shape, F32),
        in_specs=[pl.BlockSpec(memory_space=pltpu.VMEM)],
        out_specs=pl.BlockSpec(memory_space=pl.ANY),
        scratch_shapes=[pltpu.SemaphoreType.DMA],
        compiler_params=pltpu.CompilerParams(vmem_limit_bytes=16 << 20),
        name="repeat",
    )


def sizes(blocks):
    listed = blocks * (1 + 2 * SLOTS)
    triangles = blocks * (SLOTS * (SLOTS - 1) // 2 + SLOTS * SLOTS // 3 + 1)
    triples = ceil_to(4 * listed + 4 * blocks * SLOTS + 6 * triangles + 64, 1024)
    return listed, triples


def book_lengths(blocks):
    return [16, blocks, blocks]


def state_lengths(blocks):
    half = (blocks + 1) // 2
    return [16, blocks, blocks * half, blocks * half]


def block_lengths(blocks):
    edges = blocks * SLOTS + UNROLL
    diagonal = blocks + UNROLL
    return [16, edges * 8, edges, edges * 8, edges, diagonal * 4, diagonal]


def product_lengths(blocks):
    listed, _ = sizes(blocks)
    return [16, blocks + UNROLL, listed + UNROLL]


def result_lengths(blocks):
    return [16, blocks + 1 + UNROLL, (blocks + 1) // 2 + 1]


def scalars(lengths):
    return jax.ShapeDtypeStruct((ceil_to(sum(lengths), LANES),), I32)


def make_lists(kernel, name, inputs, outputs, scratch, **fixed):
    def body(*refs):
        kernel(*refs, **fixed)

    return pl.pallas_call(
        body,
        out_shape=outputs,
        in_specs=[smem()] * inputs,
        out_specs=[smem()] * len(outputs),
        scratch_shapes=[pltpu.SMEM((n,), I32) for n in scratch],
        compiler_params=pltpu.CompilerParams(vmem_limit_bytes=61 << 20),
        cost_estimate=pl.CostEstimate(
            flops=10_000_000_000, bytes_accessed=25_000_000, transcendentals=0
        ),
        name=name,
    )


def make_main(rows, width, peers, length):
    blocks = width // BLOCK
    half = (blocks + 1) // 2
    listed, _ = sizes(blocks)
    return pl.pallas_call(
        main_kernel,
        out_shape=[
            jax.ShapeDtypeStruct((rows, width), F32),
            jax.ShapeDtypeStruct((BLOCK, width), F32),
        ],
        in_specs=[smem()] * 5 + [pl.BlockSpec(memory_space=pl.ANY)] * 2,
        out_specs=[
            pl.BlockSpec(memory_space=pl.ANY),
            pl.BlockSpec(memory_space=pltpu.VMEM),
        ],
        scratch_shapes=[
            pltpu.VMEM((2 * peers, length, LANES), F32),
            pltpu.VMEM((listed + 2, 2 * BLOCK, LANES), BF16),
            pltpu.VMEM((listed + 2, 2 * BLOCK, LANES), BF16),
            pltpu.VMEM((half + 1, 2 * BLOCK, LANES), BF16),
            pltpu.VMEM((UNROLL, 2 * BLOCK, LANES), F32),
            pltpu.SemaphoreType.DMA((2,)),
        ],
        compiler_params=pltpu.CompilerParams(vmem_limit_bytes=58 << 20),
        name="purify",
    )


def make_assemble(rows, width):
    return pl.pallas_call(
        assemble_kernel,
        out_shape=jax.ShapeDtypeStruct((rows, width), F32),
        in_specs=[
            smem(), pl.BlockSpec(memory_space=pl.ANY), pl.BlockSpec(memory_space=pltpu.VMEM)
        ],
        out_specs=pl.BlockSpec(memory_space=pl.ANY),
        scratch_shapes=[pltpu.SemaphoreType.DMA],
        input_output_aliases={1: 0},
        compiler_params=pltpu.CompilerParams(vmem_limit_bytes=16 << 20),
        name="assemble",
    )


def local(density, pattern):
    rows, width = density.shape
    layers, lines, cols = (lax.axis_size(a) for a in ("layer", "row", "col"))
    across = 4
    depth = lines // across
    pieces = rows // PIECE
    share = ceil_to(pieces * PARTS, QUARTERS) // QUARTERS * TILE
    length = pieces * PARTS * depth // QUARTERS * TILE
    assert layers // 2 * cols == across
    peers = across * across
    line, col, layer = (lax.axis_index(a) for a in ("row", "col", "layer"))
    tile = line * cols + col
    z = line // across
    where = jnp.stack(
        [tile, layer % 2, (layer - z) % QUARTERS, layer]
    ).astype(I32)
    listed = pattern.T

    blocks = width // BLOCK
    count, triples = sizes(blocks)

    packed = make_pack(depth, rows, share)(where, listed, density)
    where, packed = lax.optimization_barrier((where, packed))
    (book,) = make_lists(
        neighbour_kernel, "neighbours", 2, [scalars(book_lengths(blocks))], [], pieces=pieces
    )(where, listed)
    along = [[z * across + y for z in range(depth)] for y in range(across)]
    got = lax.all_to_all(
        packed, "row", split_axis=0, concat_axis=0, tiled=True, axis_index_groups=along
    )
    got, book = lax.optimization_barrier((got, book))
    relayed = make_relay(depth, share, across, length)(where, got)

    def ring(core, z, fixed, over_x):
        places = [(i, fixed) if over_x else (fixed, i) for i in range(across)]
        return [
            ((x // cols * 2 + core) * lines + z * across + y) * cols + x % cols
            for x, y in places
        ]

    def rings(first):
        return [
            ring(core, z, fixed, (core == 0) == first)
            for core in range(2)
            for z in range(depth)
            for fixed in range(across)
        ]

    everywhere = ("layer", "row", "col")
    lined = lax.all_to_all(
        relayed, everywhere, split_axis=0, concat_axis=0, tiled=True, axis_index_groups=rings(True)
    )
    relayed = make_repeat(across, (across, length, LANES))(lined)
    own = lax.all_to_all(
        relayed, everywhere, split_axis=0, concat_axis=0, tiled=True, axis_index_groups=rings(False)
    )
    own = own.reshape(across * across, length, LANES)
    book, relayed = lax.optimization_barrier((book, relayed))
    block_lists, state = make_lists(
        edge_kernel, "edges", 3,
        [scalars(block_lengths(blocks)), scalars(state_lengths(blocks))], [],
        depth=depth, across=across, length=length, spare=count + 1, pieces=pieces,
    )(where, listed, book)
    product_lists, pairs, entry = make_lists(
        product_kernel, "products", 3,
        [scalars(product_lengths(blocks)), scalars([triples]), scalars([2 * (count + 2)])],
        [16], blocks=blocks, spare=count + 1, pieces=pieces,
    )(where, book, state)
    own, block_lists, product_lists, pairs, entry = lax.optimization_barrier(
        (own, block_lists, product_lists, pairs, entry)
    )
    cores = [(i, i ^ 1) for i in range(layers)]
    other = lax.ppermute(own, "layer", cores)
    (result_lists,) = make_lists(
        result_kernel, "results", 4, [scalars(result_lengths(blocks))], [],
        blocks=blocks, pieces=pieces,
    )(where, book, state, entry)
    full, band = make_main(rows, width, peers, length)(
        where, block_lists, product_lists, pairs, result_lists, own, other
    )
    return make_assemble(rows, width)(where, full, lax.ppermute(band, "layer", cores))


def solution(mesh):
    in_specs = (P(("row", "col"), None), P())
    out_specs = P(("row", "col"), None)
    return jax.shard_map(local, mesh=mesh, in_specs=in_specs, out_specs=out_specs, check_vma=False)
```

```python
import jax
import jax.numpy as jnp
from jax import lax
from jax.experimental import pallas as pl
from jax.experimental.pallas import tpu as pltpu
from jax.sharding import PartitionSpec as P

BLOCK = 64
SLOTS = 4
PIECE = 16
TILE = 8
LANES = 128
PIECES = BLOCK // PIECE
PARTS = SLOTS + 1
QUARTERS = 4
UNROLL = 4
GROUP = 4
I32 = jnp.int32
F32 = jnp.float32
BF16 = jnp.bfloat16


def ceil_to(value, unit):
    return -(-value // unit) * unit


def pack_kernel(where_ref, pattern_ref, density_ref, out_ref, buffer, taken, sem):
    tile = where_ref[0]
    shift = where_ref[2]
    rows = density_ref.shape[0]
    pieces = rows // PIECE
    depth, share = out_ref.shape[0], out_ref.shape[1]
    left = lax.broadcasted_iota(I32, (PIECE, LANES), 1) < BLOCK
    count = buffer.shape[0]
    for v in range(pieces * PARTS, count):
        buffer[v] = jnp.zeros((TILE, LANES), F32)

    def chunk(piece, block):
        start = pl.multiple_of((block >> 1) * LANES, LANES)
        return density_ref[piece * PIECE : (piece + 1) * PIECE, pl.ds(start, LANES)]

    for piece in range(pieces):
        block_row = (tile * pieces + piece) >> 2
        for pair in range(SLOTS // 2):
            first = pattern_ref[2 * pair, block_row]
            second = pattern_ref[2 * pair + 1, block_row]
            a = chunk(piece, first)
            b = chunk(piece, second)
            a = jnp.where((first & 1) == 0, a, pltpu.roll(a, BLOCK, 1))
            b = jnp.where((second & 1) == 1, b, pltpu.roll(b, BLOCK, 1))
            both = jnp.where(left, a, b)
            buffer[piece * PARTS + 2 * pair] = both[:TILE]
            buffer[piece * PARTS + 2 * pair + 1] = both[TILE:]
        d = chunk(piece, block_row)
        turned = pltpu.roll(d, BLOCK, 1)
        even = jnp.where(left[:TILE], d[:TILE], turned[TILE:])
        odd = jnp.where(left[:TILE], turned[:TILE], d[TILE:])
        buffer[piece * PARTS + SLOTS] = jnp.where((block_row & 1) == 0, even, odd)

    for i in range(share // TILE):
        taken[i * TILE : (i + 1) * TILE, :] = buffer[shift + QUARTERS * i]
    copies = [
        pltpu.make_async_copy(taken, out_ref.at[index], sem) for index in range(depth)
    ]
    for copy in copies:
        copy.start()
    for copy in copies:
        copy.wait()


def relay_kernel(where_ref, got_ref, out_ref, buffer, sem):
    quarter = where_ref[3]
    depth, share = got_ref.shape[0], got_ref.shape[1]
    for z in range(depth):
        extra = sum(((quarter + QUARTERS * i) < z).astype(I32) for i in range(depth // QUARTERS))
        start = pl.multiple_of((z * (share // TILE - 1) + extra) * TILE, TILE)
        buffer[pl.ds(start, share), :] = got_ref[z]
    peers, length = out_ref.shape[0], out_ref.shape[1]
    copies = [
        pltpu.make_async_copy(buffer.at[:length], out_ref.at[index], sem)
        for index in range(peers)
    ]
    for copy in copies:
        copy.start()
    for copy in copies:
        copy.wait()


class Part:
    def __init__(self, ref, start):
        self.ref, self.start = ref, start

    def __getitem__(self, i):
        return self.ref[self.start + i]

    def __setitem__(self, i, value):
        self.ref[self.start + i] = value


def parts_of(ref, lengths):
    parts, start = [], 0
    for length in lengths:
        parts.append(Part(ref, start))
        start += length
    return parts


def each(lo, hi, body):
    def step(i, carry):
        body(i)
        return carry

    lax.fori_loop(lo, hi, step, 0)


def clear(ref, start, count, value, unroll=8):
    def body(i):
        for u in range(unroll):
            ref[start + i * unroll + u] = value

    each(0, count // unroll, body)


def row_of(where_ref, pieces):
    first = where_ref[0] * pieces
    return jnp.where(where_ref[1] == 0, first >> 2, (first + pieces - 1) >> 2)


def neighbours_of(pattern_ref, r, cnt, used, names):
    blocks = pattern_ref.shape[1]

    def neighbour(b):
        @pl.when(used[b] == 0)
        def _():
            used[b] = 1
            n = cnt[0]
            names[n] = b
            cnt[0] = n + 1

    neighbour(r)
    for s in range(SLOTS):
        neighbour(pattern_ref[s, r])

    def incoming(a):
        hit = pattern_ref[0, a] == r
        for s in range(1, SLOTS):
            hit = hit | (pattern_ref[s, a] == r)

        @pl.when(hit)
        def _():
            neighbour(a)

    each(0, blocks, incoming)


def addressing(blocks, depth, across, length, pieces):
    low = (2 * across).bit_length() - 1
    scale = 65536 // pieces + 1
    assert all((g * scale) >> 16 == g // pieces for g in range(blocks * PIECES))
    share = length // TILE // depth

    def address(t, v):
        z = t >> low
        y = (t >> 1) & (across - 1)
        quarter = (v + z) & (QUARTERS - 1)
        before = z * share + sum(
            ((quarter + QUARTERS * i) < z).astype(I32) for i in range(depth // QUARTERS)
        )
        x = (quarter >> 1) * 2 + (t & 1)
        core = quarter & 1
        peer = jnp.where(core == 0, y * 4 + x, x * 4 + y)
        return (core * (4 * across) + peer) * length + (before + (v >> 2)) * TILE

    def split(g):
        t = (g * scale) >> 16
        return t, g - t * pieces

    def tiles_of(a, s, at_ref, n):
        for p in range(PIECES):
            t, g = split(a * PIECES + p)
            if s == SLOTS:
                at_ref[n * 4 + p] = address(t, g * PARTS + SLOTS)
            else:
                v = g * PARTS + (s // 2) * 2
                at_ref[n * 8 + 2 * p] = address(t, v)
                at_ref[n * 8 + 2 * p + 1] = address(t, v + 1)

    return tiles_of


def block_of(blocks, state, c, j, put):
    cnt, qn, cq, ql = parts_of(state, state_lengths(blocks))
    half = (blocks + 1) // 2
    q = j >> 1
    bit = 1 << (j & 1)
    word = cq[c * half + q]

    @pl.when((word & bit) == 0)
    def _():
        fresh = word == 0
        index = jnp.where(fresh, cnt[2] + 1, word >> 2)
        cnt[2] = cnt[2] + fresh.astype(I32)
        n = qn[c]
        ql[c * half + jnp.where(fresh, n, half - 1)] = jnp.where(
            fresh, q, ql[c * half + half - 1]
        )
        qn[c] = n + fresh.astype(I32)
        cq[c * half + q] = jnp.where(fresh, index * 4, word) + bit
        put(index * 2 + (j & 1))


def near_kernel(
    where_ref, pattern_ref, book, lists, state, *, depth, across, length, spare, pieces
):
    blocks = pattern_ref.shape[1]
    known, used, names = parts_of(book, book_lengths(blocks))
    meta, nat_at, nat_to, dia_at, dia_to = parts_of(lists, near_lengths(blocks))
    cnt, qn, _, _ = parts_of(state, state_lengths(blocks))
    half = (blocks + 1) // 2
    tiles_of = addressing(blocks, depth, across, length, pieces)
    clear(book, 0, 16 + blocks, 0)
    clear(state, 0, 16, 0)
    neighbours_of(pattern_ref, row_of(where_ref, pieces), known, used, names)

    def start(i):
        c = names[i]
        qn[c] = 0
        clear(state, 16 + blocks + c * half, half, 0, 8 if half % 8 == 0 else 1)

        def put_diagonal(dest):
            n = cnt[5]
            cnt[5] = n + 1
            dia_to[n] = dest
            tiles_of(c, SLOTS, dia_at, n)

        block_of(blocks, state, c, c, put_diagonal)
        for s in range(SLOTS):

            def put(dest):
                n = cnt[3]
                cnt[3] = n + 1
                nat_to[n] = dest * 2 + s % 2
                tiles_of(c, s, nat_at, n)

            block_of(blocks, state, c, pattern_ref[s, c], put)

    each(0, known[0], start)
    for u in range(UNROLL):
        nat_to[cnt[3] + u] = spare * 4
        dia_to[cnt[5] + u] = spare * 2
        for i in range(8):
            nat_at[(cnt[3] + u) * 8 + i] = 0
        for i in range(4):
            dia_at[(cnt[5] + u) * 4 + i] = 0
    meta[3] = cnt[3]
    meta[5] = cnt[5]
    meta[13] = where_ref[1]


def far_kernel(
    where_ref, pattern_ref, book, before, lists, state,
    *, depth, across, length, spare, pieces,
):
    blocks = pattern_ref.shape[1]
    known, used, names = parts_of(book, book_lengths(blocks))
    meta, tra_at, tra_to = parts_of(lists, far_lengths(blocks))
    _, qn_before, cq_before, ql_before = parts_of(before, state_lengths(blocks))
    cnt, qn, cq, ql = parts_of(state, state_lengths(blocks))
    half = (blocks + 1) // 2
    tiles_of = addressing(blocks, depth, across, length, pieces)
    clear(state, 0, 16, 0)
    cnt[2] = before[2]

    def copy(i):
        c = names[i]
        qn[c] = qn_before[c]
        unroll = 8 if half % 8 == 0 else 1

        def body(j):
            for u in range(unroll):
                at = c * half + j * unroll + u
                cq[at] = cq_before[at]
                ql[at] = ql_before[at]

        each(0, half // unroll, body)

    each(0, known[0], copy)

    def edges(a):
        ends = [pattern_ref[s, a] for s in range(SLOTS)]
        any_used = used[ends[0]]
        for b in ends[1:]:
            any_used = any_used | used[b]

        @pl.when(any_used > 0)
        def _():
            for s, b in enumerate(ends):

                @pl.when(used[b] > 0)
                def _():
                    def put(dest):
                        n = cnt[4]
                        cnt[4] = n + 1
                        tra_to[n] = dest * 2 + s % 2
                        tiles_of(a, s, tra_at, n)

                    block_of(blocks, state, b, a, put)

    each(0, blocks, edges)
    for u in range(UNROLL):
        tra_to[cnt[4] + u] = spare * 4
        for i in range(8):
            tra_at[(cnt[4] + u) * 8 + i] = 0
    meta[2] = cnt[2]
    meta[4] = cnt[4]


def product_kernel(
    where_ref, book, state, lists, pairs, entry, cnt, *, blocks, spare, pieces
):
    known, _, names = parts_of(book, book_lengths(blocks))
    _, qn, cq, ql = parts_of(state, state_lengths(blocks))
    meta, fa, fb = parts_of(lists, product_lengths(blocks))
    half = (blocks + 1) // 2
    r = row_of(where_ref, pieces)
    for i in range(16):
        cnt[i] = 0
    cnt[0] = known[0]
    for i in range(GROUP):
        pairs[i] = 0
    cnt[8] = 1

    def c_body(ci):
        c = names[ci]
        chunks = qn[c]
        mine = c == r

        def k_body(ki):
            k = names[ki]
            word = cq[c * half + (k >> 1)]
            bit = 1 << (k & 1)
            dest = (word >> 2) * 2 + (k & 1)

            @pl.when((word & bit) != 0)
            def _():
                group = cnt[8]
                base = group * GROUP

                def chunk(i, count):
                    q = ql[c * half + i]
                    a = cq[c * half + q]
                    b = cq[k * half + q]
                    at = jnp.where(mine, 1 + i, 0)
                    pairs[base + count] = (at << 20) + ((a >> 2) << 10) + (b >> 2)
                    return count + (((a & b) & 3) != 0).astype(I32)

                count = lax.fori_loop(0, chunks, chunk, 0)
                for u in range(GROUP):
                    pairs[base + count + u] = 0
                groups = (count + GROUP - 1) >> 2
                cnt[8] = group + groups
                span = group * 32 + groups
                entry[dest] = span
                code = dest * (1 << 17) + span

                @pl.when(c == k)
                def _():
                    n = cnt[6]
                    cnt[6] = n + 1
                    fa[n] = code

                @pl.when(c != k)
                def _():
                    n = cnt[7]
                    cnt[7] = n + 1
                    fb[n] = code

        each(0, cnt[0], k_body)

    each(0, cnt[0], c_body)

    for u in range(UNROLL):
        fa[cnt[6] + u] = spare * (1 << 18)
        fb[cnt[7] + u] = spare * (1 << 18)
    meta[6] = cnt[6]
    meta[7] = cnt[7]


def result_kernel(where_ref, book, state, entry, lists, *, blocks, pieces):
    known, _, names = parts_of(book, book_lengths(blocks))
    _, qn, cq, ql = parts_of(state, state_lengths(blocks))
    meta, pp, mixl = parts_of(lists, result_lengths(blocks))
    half = (blocks + 1) // 2
    r = row_of(where_ref, pieces)

    def result(ci, n):
        c = names[ci]
        word = cq[r * half + (c >> 1)]
        code = c * (1 << 17) + entry[(word >> 2) * 2 + (c & 1)]
        pp[jnp.where(c == r, 0, n)] = code
        return jnp.where(c == r, n, n + 1)

    n = lax.fori_loop(0, known[0], result, 1)
    mixl[0] = 0

    def mix(i):
        mixl[1 + i] = cq[r * half + ql[r * half + i]] >> 2

    each(0, qn[r], mix)
    for u in range(UNROLL):
        pp[n + u] = 0
    meta[9] = n
    meta[10] = qn[r]


def two_parts(value):
    high = value.astype(BF16)
    low = (value - high.astype(F32)).astype(BF16)
    return jnp.concatenate([high, low], axis=0)


def times(lhs, rhs):
    return lax.dot_general(
        jnp.concatenate(lhs, axis=1),
        jnp.concatenate(rhs, axis=1),
        (((1,), (1,)), ((), ())),
        preferred_element_type=F32,
    )


def main_kernel(
    where_ref, near_lists, far_lists, product_lists, pairs, result_lists,
    own_0, own_1, own_2, own_3, own_4, other_0, other_1, other_2, other_3, other_4,
    full_ref, result,
    gathered, blocks_m, blocks_f, mixed, sums, sems,
):
    blocks = result.shape[1] // BLOCK
    near, nat_at, nat_to, dia_at, dia_to = parts_of(near_lists, near_lengths(blocks))
    far, tra_at, tra_to = parts_of(far_lists, far_lengths(blocks))
    counts, fa, fb = parts_of(product_lists, product_lengths(blocks))
    extent, pp, mixl = parts_of(result_lists, result_lengths(blocks))
    core = where_ref[1]
    size = own_0.shape[0]
    half = own_3.shape[0]
    around = gathered.shape[0] // 2 // size

    def arrivals(refs, side, place, first):
        shifts = ((0, 0), (around - 1, 0), (1, 0), (2, 0), (2, half))
        return [
            pltpu.make_async_copy(
                ref,
                gathered.at[
                    pl.ds(
                        side * around * size + ((place + shift) & (around - 1)) * size + at,
                        ref.shape[0],
                    )
                ],
                sems.at[first + i],
            )
            for i, (ref, (shift, at)) in enumerate(zip(refs, shifts))
        ]

    y, x = where_ref[4], where_ref[5]
    copies = arrivals(
        (own_0, own_1, own_2, own_3, own_4), core, jnp.where(core == 0, y, x), 0
    ) + arrivals(
        (other_0, other_1, other_2, other_3, other_4), 1 - core, jnp.where(core == 0, x, y), 5
    )
    for copy in copies:
        copy.start()
    right = lax.broadcasted_iota(I32, (BLOCK, LANES), 1) // BLOCK
    none = jnp.zeros((2 * BLOCK, LANES), BF16)

    def clear_blocks(i):
        blocks_m[i] = none
        blocks_f[i] = none

    each(0, far[2] + 1, clear_blocks)

    def clear_result(i):
        start = pl.multiple_of(i * LANES, LANES)
        result[:, pl.ds(start, LANES)] = jnp.zeros((result.shape[0], LANES), F32)

    each(0, result.shape[1] // LANES, clear_result)
    mixed[0] = none
    flat = gathered.reshape(gathered.shape[0] * gathered.shape[1], LANES)
    for copy in copies:
        copy.wait()

    def steps(count):
        return (count + UNROLL - 1) >> 2

    def rows_at(at_ref, n, count):
        return [
            flat[pl.ds(pl.multiple_of(at_ref[n * count + i], TILE), TILE), :]
            for i in range(count)
        ]

    def add(store, index, value):
        store[index] = store[index] + two_parts(value)

    def natural(i):
        for u in range(UNROLL):
            n = i * UNROLL + u
            to = nat_to[n]
            parity = (to >> 1) & 1
            x = jnp.concatenate(rows_at(nat_at, n, 8), axis=0)
            x = jnp.where((to & 1) == parity, x, pltpu.roll(x, BLOCK, 1))
            add(blocks_m, to >> 2, jnp.where(right == parity, x, 0.0))

    def transposed(i):
        for u in range(UNROLL):
            n = i * UNROLL + u
            to = tra_to[n]
            parity = (to >> 1) & 1
            x = jnp.concatenate(rows_at(tra_at, n, 8), axis=0).T
            x = jnp.where((to & 1) == 0, x[:BLOCK], x[BLOCK:])
            x = jnp.concatenate([x, x], axis=1)
            add(blocks_m, to >> 2, jnp.where(right == parity, x, 0.0))

    def diagonal(i):
        for u in range(UNROLL):
            n = i * UNROLL + u
            to = dia_to[n]
            parity = to & 1
            parts = []
            for x in rows_at(dia_at, n, 4):
                turned = pltpu.roll(x, BLOCK, 1)
                parts.append(jnp.where(right[:TILE] == 0, x, turned))
                parts.append(jnp.where(right[:TILE] == 0, turned, x))
            x = jnp.concatenate(parts, axis=0)
            add(blocks_m, to >> 1, jnp.where(right == parity, x, 0.0))

    each(0, steps(near[3]), natural)
    each(0, steps(far[4]), transposed)
    each(0, steps(near[5]), diagonal)

    def fold(total):
        s = total[:BLOCK] + total[BLOCK:]
        return s + pltpu.roll(s, BLOCK, 1)

    def codes_of(word, g):
        n = word & 31
        group = jnp.where(g < n, ((word >> 5) & 4095) + g, 0)
        return [pairs[group * GROUP + u] for u in range(GROUP)]

    def filtered(list_ref, static):
        def product(word, groups):
            lhs, rhs = [], []
            for g in groups:
                for code in codes_of(word, g):
                    lhs.append(blocks_m[(code >> 10) & 1023])
                    rhs.append(blocks_m[code & 1023])
            return times(lhs, rhs)

        def body(i):
            words = [list_ref[i * UNROLL + u] for u in range(UNROLL)]
            for u in range(UNROLL):
                sums[u] = product(words[u], range(static))
            most = words[0] & 31
            for word in words[1:]:
                most = jnp.maximum(most, word & 31)

            def more(g):
                for u in range(UNROLL):
                    sums[u] = sums[u] + product(words[u], [g])

            each(static, most, more)
            for u in range(UNROLL):
                dest = words[u] >> 17
                value = fold(sums[u])
                add(blocks_f, dest >> 1, jnp.where(right == (dest & 1), value, 0.0))

        return body

    each(0, steps(counts[6]), filtered(fa, 3))
    each(0, steps(counts[7]), filtered(fb, 1))

    def mix(i):
        index = mixl[1 + i]
        m = blocks_m[index].astype(F32)
        f = blocks_f[index].astype(F32)
        mixed[1 + i] = two_parts(
            m[:BLOCK] + m[BLOCK:] - 1.5 * (f[:BLOCK] + f[BLOCK:])
        )

    each(0, extent[10], mix)

    def purified(first, count, static, i):
        def product(word, groups):
            lhs, rhs = [], []
            for g in groups:
                for code in codes_of(word, g):
                    lhs += [blocks_f[(code >> 10) & 1023], mixed[code >> 20]]
                    rhs += [blocks_m[code & 1023], blocks_f[code & 1023]]
            return times(lhs, rhs)

        words = [pp[first + i * count + u] for u in range(count)]
        for u in range(count):
            sums[u] = product(words[u], range(static))
        most = words[0] & 31
        for word in words[1:]:
            most = jnp.maximum(most, word & 31)

        def more(g):
            for u in range(count):
                sums[u] = sums[u] + product(words[u], [g])

        each(static, most, more)
        for u in range(count):
            c = words[u] >> 17
            lanes = pl.ds(pl.multiple_of((c >> 1) * LANES, LANES), LANES)
            value = 2.0 * fold(sums[u])
            result[:, lanes] = result[:, lanes] + jnp.where(right == (c & 1), value, 0.0)

    purified(0, 1, 3, 0)
    each(0, steps(extent[9] - 1), lambda i: purified(1, UNROLL, 1, i))

    def act(source, target):
        copy = pltpu.make_async_copy(
            result.at[source, :], full_ref.at[target, :], sems.at[0]
        )
        copy.start()
        copy.wait()

    cases(where_ref, full_ref.shape[0], True, act)


def cases(where_ref, rows, mine, act):
    tile = where_ref[0]
    skip = tile * rows - ((tile * (rows // PIECE)) >> 2) * BLOCK
    for core in range(2):
        for cut in range(0, BLOCK, PIECE):
            if not 0 < rows - (BLOCK - cut) <= BLOCK:
                continue
            upper = (core == 0) == mine
            source = pl.ds(cut, BLOCK - cut) if upper else pl.ds(0, rows - BLOCK + cut)
            target = pl.ds(0, BLOCK - cut) if upper else pl.ds(BLOCK - cut, rows - BLOCK + cut)

            @pl.when((where_ref[1] == core) & (skip == cut))
            def _():
                act(source, target)


def assemble_kernel(where_ref, full_ref, other_ref, out_ref, sem):
    def act(source, target):
        copy = pltpu.make_async_copy(other_ref.at[source, :], out_ref.at[target, :], sem)
        copy.start()
        copy.wait()

    cases(where_ref, out_ref.shape[0], False, act)


def smem():
    return pl.BlockSpec(memory_space=pltpu.SMEM)


def make_pack(depth, rows, share):
    count = ceil_to(rows // PIECE * PARTS, QUARTERS)
    return pl.pallas_call(
        pack_kernel,
        out_shape=jax.ShapeDtypeStruct((depth, share, LANES), F32),
        in_specs=[smem(), smem(), pl.BlockSpec(memory_space=pltpu.VMEM)],
        out_specs=pl.BlockSpec(memory_space=pl.ANY),
        scratch_shapes=[
            pltpu.VMEM((count, TILE, LANES), F32),
            pltpu.VMEM((share, LANES), F32),
            pltpu.SemaphoreType.DMA,
        ],
        compiler_params=pltpu.CompilerParams(vmem_limit_bytes=16 << 20),
        name="pack",
    )


def make_relay(depth, share, peers, length):
    return pl.pallas_call(
        relay_kernel,
        out_shape=jax.ShapeDtypeStruct((peers, length, LANES), F32),
        in_specs=[smem(), pl.BlockSpec(memory_space=pltpu.VMEM)],
        out_specs=pl.BlockSpec(memory_space=pltpu.HBM),
        scratch_shapes=[
            pltpu.VMEM((length + TILE, LANES), F32),
            pltpu.SemaphoreType.DMA,
        ],
        compiler_params=pltpu.CompilerParams(vmem_limit_bytes=16 << 20),
        name="relay",
    )


def sizes(blocks):
    listed = blocks * (1 + 2 * SLOTS)
    triangles = blocks * (SLOTS * (SLOTS - 1) // 2 + SLOTS * SLOTS // 3 + 1)
    triples = ceil_to(4 * listed + 4 * blocks * SLOTS + 6 * triangles + 64, 1024)
    return listed, triples


def book_lengths(blocks):
    return [16, blocks, blocks]


def state_lengths(blocks):
    half = (blocks + 1) // 2
    return [16, blocks, blocks * half, blocks * half]


def near_lengths(blocks):
    edges = blocks * SLOTS + UNROLL
    diagonal = blocks + UNROLL
    return [16, edges * 8, edges, diagonal * 4, diagonal]


def far_lengths(blocks):
    edges = blocks * SLOTS + UNROLL
    return [16, edges * 8, edges]


def product_lengths(blocks):
    listed, _ = sizes(blocks)
    return [16, blocks + UNROLL, listed + UNROLL]


def result_lengths(blocks):
    return [16, blocks + 1 + UNROLL, (blocks + 1) // 2 + 1]


def scalars(lengths):
    return jax.ShapeDtypeStruct((ceil_to(sum(lengths), LANES),), I32)


def make_lists(kernel, name, inputs, outputs, scratch, **fixed):
    def body(*refs):
        kernel(*refs, **fixed)

    return pl.pallas_call(
        body,
        out_shape=outputs,
        in_specs=[smem()] * inputs,
        out_specs=[smem()] * len(outputs),
        scratch_shapes=[pltpu.SMEM((n,), I32) for n in scratch],
        compiler_params=pltpu.CompilerParams(vmem_limit_bytes=61 << 20),
        cost_estimate=pl.CostEstimate(
            flops=10_000_000_000, bytes_accessed=25_000_000, transcendentals=0
        ),
        name=name,
    )


def make_main(rows, width, peers, length):
    blocks = width // BLOCK
    half = (blocks + 1) // 2
    listed, _ = sizes(blocks)
    return pl.pallas_call(
        main_kernel,
        out_shape=[
            jax.ShapeDtypeStruct((rows, width), F32),
            jax.ShapeDtypeStruct((BLOCK, width), F32),
        ],
        in_specs=[smem()] * 6 + [pl.BlockSpec(memory_space=pl.ANY)] * 10,
        out_specs=[
            pl.BlockSpec(memory_space=pl.ANY),
            pl.BlockSpec(memory_space=pltpu.VMEM),
        ],
        scratch_shapes=[
            pltpu.VMEM((2 * peers, length, LANES), F32),
            pltpu.VMEM((listed + 2, 2 * BLOCK, LANES), BF16),
            pltpu.VMEM((listed + 2, 2 * BLOCK, LANES), BF16),
            pltpu.VMEM((half + 1, 2 * BLOCK, LANES), BF16),
            pltpu.VMEM((UNROLL, 2 * BLOCK, LANES), F32),
            pltpu.SemaphoreType.DMA((10,)),
        ],
        compiler_params=pltpu.CompilerParams(vmem_limit_bytes=58 << 20),
        name="purify",
    )


def make_assemble(rows, width):
    return pl.pallas_call(
        assemble_kernel,
        out_shape=jax.ShapeDtypeStruct((rows, width), F32),
        in_specs=[
            smem(), pl.BlockSpec(memory_space=pl.ANY), pl.BlockSpec(memory_space=pltpu.VMEM)
        ],
        out_specs=pl.BlockSpec(memory_space=pl.ANY),
        scratch_shapes=[pltpu.SemaphoreType.DMA],
        input_output_aliases={1: 0},
        compiler_params=pltpu.CompilerParams(vmem_limit_bytes=16 << 20),
        name="assemble",
    )


def local(density, pattern):
    rows, width = density.shape
    layers, lines, cols = (lax.axis_size(a) for a in ("layer", "row", "col"))
    across = 4
    depth = lines // across
    pieces = rows // PIECE
    share = ceil_to(pieces * PARTS, QUARTERS) // QUARTERS * TILE
    length = pieces * PARTS * depth // QUARTERS * TILE
    assert layers // 2 * cols == across
    peers = across * across
    line, col, layer = (lax.axis_index(a) for a in ("row", "col", "layer"))
    tile = line * cols + col
    z = line // across
    where = jnp.stack(
        [tile, layer % 2, (layer - z) % QUARTERS, layer, line % across, layer // 2 * cols + col]
    ).astype(I32)
    listed = pattern.T

    blocks = width // BLOCK
    count, triples = sizes(blocks)

    packed = make_pack(depth, rows, share)(where, listed, density)
    where, packed = lax.optimization_barrier((where, packed))
    fixed = dict(depth=depth, across=across, length=length, spare=count + 1, pieces=pieces)
    book, near, state = make_lists(
        near_kernel, "near", 2,
        [scalars(f(blocks)) for f in (book_lengths, near_lengths, state_lengths)], [], **fixed,
    )(where, listed)
    along = [[z * across + y for z in range(depth)] for y in range(across)]
    got = lax.all_to_all(
        packed, "row", split_axis=0, concat_axis=0, tiled=True, axis_index_groups=along
    )
    got, book, near, state = lax.optimization_barrier((got, book, near, state))
    relayed = make_relay(depth, share, across, length)(where, got)

    def ring(core, z, fixed, over_x):
        places = [(i, fixed) if over_x else (fixed, i) for i in range(across)]
        return [
            ((x // cols * 2 + core) * lines + z * across + y) * cols + x % cols
            for x, y in places
        ]

    def rings(first):
        return [
            ring(core, z, fixed, (core == 0) == first)
            for core in range(2)
            for z in range(depth)
            for fixed in range(across)
        ]

    everywhere = ("layer", "row", "col")
    relayed, book, state = lax.optimization_barrier((relayed, book, state))
    mine = lax.all_to_all(
        relayed, everywhere, split_axis=0, concat_axis=0, tiled=True, axis_index_groups=rings(True)
    )
    far, state = make_lists(
        far_kernel, "far", 4,
        [scalars(far_lengths(blocks)), scalars(state_lengths(blocks))], [], **fixed,
    )(where, listed, book, state)
    mine, far, state = lax.optimization_barrier((mine, far, state))

    def turn(value, step):
        pairs = [
            (devices[i], devices[(i + step) % across])
            for devices in rings(False)
            for i in range(across)
        ]
        return lax.ppermute(value, everywhere, pairs)

    def swap(value):
        return lax.ppermute(value, "layer", [(i, i ^ 1) for i in range(layers)])

    middle = across // 2
    left, right = turn(mine, 1), turn(mine, -1)
    product_lists, pairs, entry = make_lists(
        product_kernel, "products", 3,
        [scalars(product_lengths(blocks)), scalars([triples]), scalars([2 * (count + 2)])],
        [16], blocks=blocks, spare=count + 1, pieces=pieces,
    )(where, book, state)
    left, right, product_lists, pairs, entry = lax.optimization_barrier(
        (left, right, product_lists, pairs, entry)
    )
    own = (mine, left, right, turn(left[:middle], 1), turn(right[middle:], -1))
    other = tuple(swap(part) for part in own)
    (result_lists,) = make_lists(
        result_kernel, "results", 4, [scalars(result_lengths(blocks))], [],
        blocks=blocks, pieces=pieces,
    )(where, book, state, entry)
    full, band = make_main(rows, width, peers, length)(
        where, near, far, product_lists, pairs, result_lists, *own, *other
    )
    return make_assemble(rows, width)(where, full, swap(band))


def solution(mesh):
    in_specs = (P(("row", "col"), None), P())
    out_specs = P(("row", "col"), None)
    return jax.shard_map(local, mesh=mesh, in_specs=in_specs, out_specs=out_specs, check_vma=False)
```

```python
import jax
import jax.numpy as jnp
from jax import lax
from jax.experimental import pallas as pl
from jax.experimental.pallas import tpu as pltpu
from jax.sharding import PartitionSpec as P

BLOCK = 64
SLOTS = 4
PIECE = 16
TILE = 8
LANES = 128
PIECES = BLOCK // PIECE
PARTS = SLOTS + 1
QUARTERS = 4
UNROLL = 4
GROUP = 4
START = 1024
I32 = jnp.int32
F32 = jnp.float32
BF16 = jnp.bfloat16


def ceil_to(value, unit):
    return -(-value // unit) * unit


def pack_kernel(where_ref, pattern_ref, density_ref, out_ref, staged, buffer, taken, sem, sems):
    tile = where_ref[0]
    shift = where_ref[2]
    rows = density_ref.shape[0]
    pieces = rows // PIECE
    depth, share = out_ref.shape[0], out_ref.shape[1]
    left = lax.broadcasted_iota(I32, (PIECE, LANES), 1) < BLOCK
    count = buffer.shape[0]
    for v in range(pieces * PARTS, count):
        buffer[v] = jnp.zeros((TILE, LANES), F32)

    loads = []
    for piece in range(pieces):
        block_row = (tile * pieces + piece) >> 2
        for s in range(PARTS):
            block = pattern_ref[s, block_row] if s < SLOTS else block_row
            start = pl.multiple_of((block >> 1) * LANES, LANES)
            at = piece * PARTS + s
            load = pltpu.make_async_copy(
                density_ref.at[piece * PIECE : (piece + 1) * PIECE, pl.ds(start, LANES)],
                staged.at[at],
                sems.at[at],
            )
            load.start()
            loads.append(load)
    for load in loads:
        load.wait()

    for piece in range(pieces):
        block_row = (tile * pieces + piece) >> 2
        for pair in range(SLOTS // 2):
            first = pattern_ref[2 * pair, block_row]
            second = pattern_ref[2 * pair + 1, block_row]
            a = staged[piece * PARTS + 2 * pair]
            b = staged[piece * PARTS + 2 * pair + 1]
            a = jnp.where((first & 1) == 0, a, pltpu.roll(a, BLOCK, 1))
            b = jnp.where((second & 1) == 1, b, pltpu.roll(b, BLOCK, 1))
            both = jnp.where(left, a, b)
            buffer[piece * PARTS + 2 * pair] = both[:TILE]
            buffer[piece * PARTS + 2 * pair + 1] = both[TILE:]
        d = staged[piece * PARTS + SLOTS]
        turned = pltpu.roll(d, BLOCK, 1)
        even = jnp.where(left[:TILE], d[:TILE], turned[TILE:])
        odd = jnp.where(left[:TILE], turned[:TILE], d[TILE:])
        buffer[piece * PARTS + SLOTS] = jnp.where((block_row & 1) == 0, even, odd)

    for i in range(share // TILE):
        taken[i * TILE : (i + 1) * TILE, :] = buffer[shift + QUARTERS * i]
    copies = [
        pltpu.make_async_copy(taken, out_ref.at[index], sem) for index in range(depth)
    ]
    for copy in copies:
        copy.start()
    for copy in copies:
        copy.wait()


def relay_kernel(where_ref, got_ref, out_ref, buffer, sem):
    quarter = where_ref[3]
    depth, share = got_ref.shape[0], got_ref.shape[1]
    for z in range(depth):
        extra = sum(((quarter + QUARTERS * i) < z).astype(I32) for i in range(depth // QUARTERS))
        start = pl.multiple_of((z * (share // TILE - 1) + extra) * TILE, TILE)
        buffer[pl.ds(start, share), :] = got_ref[z]
    peers, length = out_ref.shape[0], out_ref.shape[1]
    copies = [
        pltpu.make_async_copy(buffer.at[:length], out_ref.at[index], sem)
        for index in range(peers)
    ]
    for copy in copies:
        copy.start()
    for copy in copies:
        copy.wait()


class Part:
    def __init__(self, ref, start):
        self.ref, self.start = ref, start

    def __getitem__(self, i):
        return self.ref[self.start + i]

    def __setitem__(self, i, value):
        self.ref[self.start + i] = value


def parts_of(ref, lengths):
    parts, start = [], 0
    for length in lengths:
        parts.append(Part(ref, start))
        start += length
    return parts


def each(lo, hi, body):
    def step(i, carry):
        body(i)
        return carry

    lax.fori_loop(lo, hi, step, 0)


def clear(ref, start, count, value, unroll=8):
    def body(i):
        for u in range(unroll):
            ref[start + i * unroll + u] = value

    each(0, count // unroll, body)


def row_of(where_ref, pieces):
    first = where_ref[0] * pieces
    return jnp.where(where_ref[1] == 0, first >> 2, (first + pieces - 1) >> 2)


def neighbours_of(pattern_ref, r, cnt, used, names):
    blocks = pattern_ref.shape[1]

    def neighbour(b):
        @pl.when(used[b] == 0)
        def _():
            used[b] = 1
            n = cnt[0]
            names[n] = b
            cnt[0] = n + 1

    neighbour(r)
    for s in range(SLOTS):
        neighbour(pattern_ref[s, r])

    def incoming(a):
        hit = pattern_ref[0, a] == r
        for s in range(1, SLOTS):
            hit = hit | (pattern_ref[s, a] == r)

        @pl.when(hit)
        def _():
            neighbour(a)

    each(0, blocks, incoming)


def addressing(blocks, depth, across, length, pieces):
    low = (2 * across).bit_length() - 1
    scale = 65536 // pieces + 1
    assert all((g * scale) >> 16 == g // pieces for g in range(blocks * PIECES))
    share = length // TILE // depth

    def address(t, v):
        z = t >> low
        y = (t >> 1) & (across - 1)
        quarter = (v + z) & (QUARTERS - 1)
        before = z * share + sum(
            ((quarter + QUARTERS * i) < z).astype(I32) for i in range(depth // QUARTERS)
        )
        x = (quarter >> 1) * 2 + (t & 1)
        core = quarter & 1
        peer = jnp.where(core == 0, y * 4 + x, x * 4 + y)
        return (core * (4 * across) + peer) * length + (before + (v >> 2)) * TILE

    def split(g):
        t = (g * scale) >> 16
        return t, g - t * pieces

    def tiles_of(a, s, at_ref, n):
        for p in range(PIECES):
            t, g = split(a * PIECES + p)
            if s == SLOTS:
                at_ref[n * 4 + p] = address(t, g * PARTS + SLOTS)
            else:
                v = g * PARTS + (s // 2) * 2
                at_ref[n * 8 + 2 * p] = address(t, v)
                at_ref[n * 8 + 2 * p + 1] = address(t, v + 1)

    return tiles_of


def block_of(blocks, state, c, j, put):
    cnt, qn, cq, ql = parts_of(state, state_lengths(blocks))
    half = (blocks + 1) // 2
    q = j >> 1
    bit = 1 << (j & 1)
    word = cq[c * half + q]

    @pl.when((word & bit) == 0)
    def _():
        fresh = word == 0
        index = jnp.where(fresh, cnt[2] + 1, word >> 2)
        cnt[2] = cnt[2] + fresh.astype(I32)
        n = qn[c]
        ql[c * half + jnp.where(fresh, n, half - 1)] = jnp.where(
            fresh, q, ql[c * half + half - 1]
        )
        qn[c] = n + fresh.astype(I32)
        cq[c * half + q] = jnp.where(fresh, index * 4, word) + bit
        put(index * 2 + (j & 1))


def near_kernel(
    where_ref, pattern_ref, book, lists, state, *, depth, across, length, spare, pieces
):
    blocks = pattern_ref.shape[1]
    known, used, names = parts_of(book, book_lengths(blocks))
    meta, nat_at, nat_to, dia_at, dia_to = parts_of(lists, near_lengths(blocks))
    cnt, qn, _, _ = parts_of(state, state_lengths(blocks))
    half = (blocks + 1) // 2
    tiles_of = addressing(blocks, depth, across, length, pieces)
    clear(book, 0, 16 + blocks, 0)
    clear(state, 0, 16, 0)
    neighbours_of(pattern_ref, row_of(where_ref, pieces), known, used, names)

    def start(i):
        c = names[i]
        qn[c] = 0
        clear(state, 16 + blocks + c * half, half, 0, 8 if half % 8 == 0 else 1)

        def put_diagonal(dest):
            n = cnt[5]
            cnt[5] = n + 1
            dia_to[n] = dest
            tiles_of(c, SLOTS, dia_at, n)

        block_of(blocks, state, c, c, put_diagonal)
        for s in range(SLOTS):

            def put(dest):
                n = cnt[3]
                cnt[3] = n + 1
                nat_to[n] = dest * 2 + s % 2
                tiles_of(c, s, nat_at, n)

            block_of(blocks, state, c, pattern_ref[s, c], put)

    each(0, known[0], start)
    for u in range(UNROLL):
        nat_to[cnt[3] + u] = spare * 4
        dia_to[cnt[5] + u] = spare * 2
        for i in range(8):
            nat_at[(cnt[3] + u) * 8 + i] = 0
        for i in range(4):
            dia_at[(cnt[5] + u) * 4 + i] = 0
    meta[3] = cnt[3]
    meta[5] = cnt[5]
    meta[13] = where_ref[1]


def far_kernel(
    where_ref, pattern_ref, book, before, lists, state,
    *, depth, across, length, spare, pieces,
):
    blocks = pattern_ref.shape[1]
    known, used, names = parts_of(book, book_lengths(blocks))
    meta, tra_at, tra_to = parts_of(lists, far_lengths(blocks))
    _, qn_before, cq_before, ql_before = parts_of(before, state_lengths(blocks))
    cnt, qn, cq, ql = parts_of(state, state_lengths(blocks))
    half = (blocks + 1) // 2
    tiles_of = addressing(blocks, depth, across, length, pieces)
    clear(state, 0, 16, 0)
    cnt[2] = before[2]

    def copy(i):
        c = names[i]
        qn[c] = qn_before[c]
        unroll = 8 if half % 8 == 0 else 1

        def body(j):
            for u in range(unroll):
                at = c * half + j * unroll + u
                cq[at] = cq_before[at]
                ql[at] = ql_before[at]

        each(0, half // unroll, body)

    each(0, known[0], copy)

    def edges(a):
        ends = [pattern_ref[s, a] for s in range(SLOTS)]
        any_used = used[ends[0]]
        for b in ends[1:]:
            any_used = any_used | used[b]

        @pl.when(any_used > 0)
        def _():
            for s, b in enumerate(ends):

                @pl.when(used[b] > 0)
                def _():
                    def put(dest):
                        n = cnt[4]
                        cnt[4] = n + 1
                        tra_to[n] = dest * 2 + s % 2
                        tiles_of(a, s, tra_at, n)

                    block_of(blocks, state, b, a, put)

    each(0, blocks, edges)
    for u in range(UNROLL):
        tra_to[cnt[4] + u] = spare * 4
        for i in range(8):
            tra_at[(cnt[4] + u) * 8 + i] = 0
    meta[2] = cnt[2]
    meta[4] = cnt[4]


def move_used(source, target, used, sem):
    count = source.shape[0]

    def move(start, length):
        copy = pltpu.make_async_copy(
            source.at[pl.ds(start, length)], target.at[pl.ds(start, length)], sem
        )
        copy.start()
        copy.wait()

    move(0, min(START, count))

    @pl.when(used > START)
    def _():
        move(START, count - START)


def product_kernel(
    where_ref, book, state, lists, pairs_out, entry, cnt, pairs, sem, *, blocks, spare, pieces
):
    known, _, names = parts_of(book, book_lengths(blocks))
    _, qn, cq, ql = parts_of(state, state_lengths(blocks))
    meta, fa, fb = parts_of(lists, product_lengths(blocks))
    half = (blocks + 1) // 2
    r = row_of(where_ref, pieces)
    for i in range(16):
        cnt[i] = 0
    cnt[0] = known[0]
    for i in range(GROUP):
        pairs[i] = 0
    cnt[8] = 1

    def c_body(ci):
        c = names[ci]
        chunks = qn[c]
        mine = c == r

        def k_body(ki):
            k = names[ki]
            word = cq[c * half + (k >> 1)]
            bit = 1 << (k & 1)
            dest = (word >> 2) * 2 + (k & 1)

            @pl.when((word & bit) != 0)
            def _():
                group = cnt[8]
                base = group * GROUP

                def chunk(i, count):
                    q = ql[c * half + i]
                    a = cq[c * half + q]
                    b = cq[k * half + q]
                    at = jnp.where(mine, 1 + i, 0)
                    pairs[base + count] = (at << 20) + ((a >> 2) << 10) + (b >> 2)
                    return count + (((a & b) & 3) != 0).astype(I32)

                count = lax.fori_loop(0, chunks, chunk, 0)
                for u in range(GROUP):
                    pairs[base + count + u] = 0
                groups = (count + GROUP - 1) >> 2
                cnt[8] = group + groups
                span = group * 32 + groups
                entry[dest] = span
                code = dest * (1 << 17) + span

                @pl.when(c == k)
                def _():
                    n = cnt[6]
                    cnt[6] = n + 1
                    fa[n] = code

                @pl.when(c != k)
                def _():
                    n = cnt[7]
                    cnt[7] = n + 1
                    fb[n] = code

        each(0, cnt[0], k_body)

    each(0, cnt[0], c_body)

    for u in range(UNROLL):
        fa[cnt[6] + u] = spare * (1 << 18)
        fb[cnt[7] + u] = spare * (1 << 18)
    meta[6] = cnt[6]
    meta[7] = cnt[7]
    meta[8] = cnt[8]
    move_used(pairs, pairs_out, cnt[8] * GROUP, sem)


def result_kernel(where_ref, book, state, entry, lists, *, blocks, pieces):
    known, _, names = parts_of(book, book_lengths(blocks))
    _, qn, cq, ql = parts_of(state, state_lengths(blocks))
    meta, pp, mixl = parts_of(lists, result_lengths(blocks))
    half = (blocks + 1) // 2
    r = row_of(where_ref, pieces)

    def result(ci, n):
        c = names[ci]
        word = cq[r * half + (c >> 1)]
        code = c * (1 << 17) + entry[(word >> 2) * 2 + (c & 1)]
        pp[jnp.where(c == r, 0, n)] = code
        return jnp.where(c == r, n, n + 1)

    n = lax.fori_loop(0, known[0], result, 1)
    mixl[0] = 0

    def mix(i):
        mixl[1 + i] = cq[r * half + ql[r * half + i]] >> 2

    each(0, qn[r], mix)
    for u in range(UNROLL):
        pp[n + u] = 0
    meta[9] = n
    meta[10] = qn[r]


def two_parts(value):
    high = value.astype(BF16)
    low = (value - high.astype(F32)).astype(BF16)
    return jnp.concatenate([high, low], axis=0)


def times(lhs, rhs):
    return lax.dot_general(
        jnp.concatenate(lhs, axis=1),
        jnp.concatenate(rhs, axis=1),
        (((1,), (1,)), ((), ())),
        preferred_element_type=F32,
    )


def main_kernel(
    where_ref, near_lists, far_lists, product_lists, pairs_ref, result_lists,
    own_0, own_1, own_2, own_3, own_4, other_0, other_1, other_2, other_3, other_4,
    result,
    gathered, blocks_m, blocks_f, mixed, sums, sems, pairs, sem,
):
    blocks = result.shape[1] // BLOCK
    near, nat_at, nat_to, dia_at, dia_to = parts_of(near_lists, near_lengths(blocks))
    far, tra_at, tra_to = parts_of(far_lists, far_lengths(blocks))
    counts, fa, fb = parts_of(product_lists, product_lengths(blocks))
    extent, pp, mixl = parts_of(result_lists, result_lengths(blocks))
    core = where_ref[1]
    size = own_0.shape[0]
    half = own_3.shape[0]
    around = gathered.shape[0] // 2 // size

    def arrivals(refs, side, place, first):
        shifts = ((0, 0), (around - 1, 0), (1, 0), (2, 0), (2, half))
        return [
            pltpu.make_async_copy(
                ref,
                gathered.at[
                    pl.ds(
                        side * around * size + ((place + shift) & (around - 1)) * size + at,
                        ref.shape[0],
                    )
                ],
                sems.at[first + i],
            )
            for i, (ref, (shift, at)) in enumerate(zip(refs, shifts))
        ]

    y, x = where_ref[4], where_ref[5]
    copies = arrivals(
        (own_0, own_1, own_2, own_3, own_4), core, jnp.where(core == 0, y, x), 0
    ) + arrivals(
        (other_0, other_1, other_2, other_3, other_4), 1 - core, jnp.where(core == 0, x, y), 5
    )
    for copy in copies:
        copy.start()
    move_used(pairs_ref, pairs, counts[8] * GROUP, sem)
    right = lax.broadcasted_iota(I32, (BLOCK, LANES), 1) // BLOCK
    none = jnp.zeros((2 * BLOCK, LANES), BF16)

    def clear_blocks(i):
        blocks_m[i] = none
        blocks_f[i] = none

    each(0, far[2] + 1, clear_blocks)

    def clear_result(i):
        start = pl.multiple_of(i * LANES, LANES)
        result[:, pl.ds(start, LANES)] = jnp.zeros((result.shape[0], LANES), F32)

    each(0, result.shape[1] // LANES, clear_result)
    mixed[0] = none
    flat = gathered.reshape(gathered.shape[0] * gathered.shape[1], LANES)
    for copy in copies:
        copy.wait()

    def steps(count):
        return (count + UNROLL - 1) >> 2

    def rows_at(at_ref, n, count):
        return [
            flat[pl.ds(pl.multiple_of(at_ref[n * count + i], TILE), TILE), :]
            for i in range(count)
        ]

    def add(store, index, value):
        store[index] = store[index] + two_parts(value)

    def natural(i):
        for u in range(UNROLL):
            n = i * UNROLL + u
            to = nat_to[n]
            parity = (to >> 1) & 1
            x = jnp.concatenate(rows_at(nat_at, n, 8), axis=0)
            x = jnp.where((to & 1) == parity, x, pltpu.roll(x, BLOCK, 1))
            add(blocks_m, to >> 2, jnp.where(right == parity, x, 0.0))

    def transposed(i):
        for u in range(UNROLL):
            n = i * UNROLL + u
            to = tra_to[n]
            parity = (to >> 1) & 1
            x = jnp.concatenate(rows_at(tra_at, n, 8), axis=0).T
            x = jnp.where((to & 1) == 0, x[:BLOCK], x[BLOCK:])
            x = jnp.concatenate([x, x], axis=1)
            add(blocks_m, to >> 2, jnp.where(right == parity, x, 0.0))

    def diagonal(i):
        for u in range(UNROLL):
            n = i * UNROLL + u
            to = dia_to[n]
            parity = to & 1
            parts = []
            for x in rows_at(dia_at, n, 4):
                turned = pltpu.roll(x, BLOCK, 1)
                parts.append(jnp.where(right[:TILE] == 0, x, turned))
                parts.append(jnp.where(right[:TILE] == 0, turned, x))
            x = jnp.concatenate(parts, axis=0)
            add(blocks_m, to >> 1, jnp.where(right == parity, x, 0.0))

    each(0, steps(near[3]), natural)
    each(0, steps(far[4]), transposed)
    each(0, steps(near[5]), diagonal)

    def fold(total):
        s = total[:BLOCK] + total[BLOCK:]
        return s + pltpu.roll(s, BLOCK, 1)

    def codes_of(word, g):
        n = word & 31
        group = jnp.where(g < n, ((word >> 5) & 4095) + g, 0)
        return [pairs[group * GROUP + u] for u in range(GROUP)]

    def filtered(list_ref, static):
        def product(word, groups):
            lhs, rhs = [], []
            for g in groups:
                for code in codes_of(word, g):
                    lhs.append(blocks_m[(code >> 10) & 1023])
                    rhs.append(blocks_m[code & 1023])
            return times(lhs, rhs)

        def body(i):
            words = [list_ref[i * UNROLL + u] for u in range(UNROLL)]
            for u in range(UNROLL):
                sums[u] = product(words[u], range(static))
            most = words[0] & 31
            for word in words[1:]:
                most = jnp.maximum(most, word & 31)

            def more(g):
                for u in range(UNROLL):
                    sums[u] = sums[u] + product(words[u], [g])

            each(static, most, more)
            for u in range(UNROLL):
                dest = words[u] >> 17
                value = fold(sums[u])
                add(blocks_f, dest >> 1, jnp.where(right == (dest & 1), value, 0.0))

        return body

    each(0, steps(counts[6]), filtered(fa, 3))
    each(0, steps(counts[7]), filtered(fb, 1))

    def mix(i):
        index = mixl[1 + i]
        m = blocks_m[index].astype(F32)
        f = blocks_f[index].astype(F32)
        mixed[1 + i] = two_parts(
            m[:BLOCK] + m[BLOCK:] - 1.5 * (f[:BLOCK] + f[BLOCK:])
        )

    each(0, extent[10], mix)

    def purified(first, count, static, i):
        def product(word, groups):
            lhs, rhs = [], []
            for g in groups:
                for code in codes_of(word, g):
                    lhs += [blocks_f[(code >> 10) & 1023], mixed[code >> 20]]
                    rhs += [blocks_m[code & 1023], blocks_f[code & 1023]]
            return times(lhs, rhs)

        words = [pp[first + i * count + u] for u in range(count)]
        for u in range(count):
            sums[u] = product(words[u], range(static))
        most = words[0] & 31
        for word in words[1:]:
            most = jnp.maximum(most, word & 31)

        def more(g):
            for u in range(count):
                sums[u] = sums[u] + product(words[u], [g])

        each(static, most, more)
        for u in range(count):
            c = words[u] >> 17
            lanes = pl.ds(pl.multiple_of((c >> 1) * LANES, LANES), LANES)
            value = 2.0 * fold(sums[u])
            result[:, lanes] = result[:, lanes] + jnp.where(right == (c & 1), value, 0.0)

    purified(0, 1, 3, 0)
    each(0, steps(extent[9] - 1), lambda i: purified(1, UNROLL, 1, i))


def cases(where_ref, rows, mine, act):
    tile = where_ref[0]
    skip = tile * rows - ((tile * (rows // PIECE)) >> 2) * BLOCK
    for core in range(2):
        for cut in range(0, BLOCK, PIECE):
            if not 0 < rows - (BLOCK - cut) <= BLOCK:
                continue
            upper = (core == 0) == mine
            source = pl.ds(cut, BLOCK - cut) if upper else pl.ds(0, rows - BLOCK + cut)
            target = pl.ds(0, BLOCK - cut) if upper else pl.ds(BLOCK - cut, rows - BLOCK + cut)

            @pl.when((where_ref[1] == core) & (skip == cut))
            def _():
                act(source, target)


def place_kernel(where_ref, band_ref, out_ref, held, sem):
    load = pltpu.make_async_copy(band_ref, held, sem)
    load.start()
    load.wait()

    def act(source, target):
        copy = pltpu.make_async_copy(held.at[source, :], out_ref.at[target, :], sem)
        copy.start()
        copy.wait()

    cases(where_ref, out_ref.shape[0], True, act)


def assemble_kernel(where_ref, full_ref, other_ref, out_ref, sem):
    def act(source, target):
        copy = pltpu.make_async_copy(other_ref.at[source, :], out_ref.at[target, :], sem)
        copy.start()
        copy.wait()

    cases(where_ref, out_ref.shape[0], False, act)


def smem():
    return pl.BlockSpec(memory_space=pltpu.SMEM)


def make_pack(depth, rows, share):
    count = ceil_to(rows // PIECE * PARTS, QUARTERS)
    return pl.pallas_call(
        pack_kernel,
        out_shape=jax.ShapeDtypeStruct((depth, share, LANES), F32),
        in_specs=[smem(), smem(), pl.BlockSpec(memory_space=pltpu.HBM)],
        out_specs=pl.BlockSpec(memory_space=pl.ANY),
        scratch_shapes=[
            pltpu.VMEM((rows // PIECE * PARTS, PIECE, LANES), F32),
            pltpu.VMEM((count, TILE, LANES), F32),
            pltpu.VMEM((share, LANES), F32),
            pltpu.SemaphoreType.DMA,
            pltpu.SemaphoreType.DMA((rows // PIECE * PARTS,)),
        ],
        compiler_params=pltpu.CompilerParams(vmem_limit_bytes=61 << 20),
        name="pack",
    )


def make_relay(depth, share, peers, length):
    return pl.pallas_call(
        relay_kernel,
        out_shape=jax.ShapeDtypeStruct((peers, length, LANES), F32),
        in_specs=[smem(), pl.BlockSpec(memory_space=pltpu.VMEM)],
        out_specs=pl.BlockSpec(memory_space=pltpu.HBM),
        scratch_shapes=[
            pltpu.VMEM((length + TILE, LANES), F32),
            pltpu.SemaphoreType.DMA,
        ],
        compiler_params=pltpu.CompilerParams(vmem_limit_bytes=16 << 20),
        name="relay",
    )


def sizes(blocks):
    listed = blocks * (1 + 2 * SLOTS)
    triangles = blocks * (SLOTS * (SLOTS - 1) // 2 + SLOTS * SLOTS // 3 + 1)
    triples = ceil_to(4 * listed + 4 * blocks * SLOTS + 6 * triangles + 64, 1024)
    return listed, triples


def book_lengths(blocks):
    return [16, blocks, blocks]


def state_lengths(blocks):
    half = (blocks + 1) // 2
    return [16, blocks, blocks * half, blocks * half]


def near_lengths(blocks):
    edges = blocks * SLOTS + UNROLL
    diagonal = blocks + UNROLL
    return [16, edges * 8, edges, diagonal * 4, diagonal]


def far_lengths(blocks):
    edges = blocks * SLOTS + UNROLL
    return [16, edges * 8, edges]


def product_lengths(blocks):
    listed, _ = sizes(blocks)
    return [16, blocks + UNROLL, listed + UNROLL]


def result_lengths(blocks):
    return [16, blocks + 1 + UNROLL, (blocks + 1) // 2 + 1]


def scalars(lengths):
    return jax.ShapeDtypeStruct((ceil_to(sum(lengths), LANES),), I32)


def make_lists(kernel, name, inputs, outputs, scratch, outside=(), **fixed):
    def body(*refs):
        kernel(*refs, **fixed)

    return pl.pallas_call(
        body,
        out_shape=outputs,
        in_specs=[smem()] * inputs,
        out_specs=[
            pl.BlockSpec(memory_space=pltpu.HBM) if i in outside else smem()
            for i in range(len(outputs))
        ],
        scratch_shapes=[pltpu.SMEM((n,), I32) for n in scratch]
        + [pltpu.SemaphoreType.DMA] * len(outside),
        compiler_params=pltpu.CompilerParams(vmem_limit_bytes=61 << 20),
        cost_estimate=pl.CostEstimate(
            flops=10_000_000_000, bytes_accessed=25_000_000, transcendentals=0
        ),
        name=name,
    )


def make_main(width, peers, length):
    blocks = width // BLOCK
    half = (blocks + 1) // 2
    listed, triples = sizes(blocks)
    return pl.pallas_call(
        main_kernel,
        out_shape=jax.ShapeDtypeStruct((BLOCK, width), F32),
        in_specs=[smem()] * 4
        + [pl.BlockSpec(memory_space=pltpu.HBM), smem()]
        + [pl.BlockSpec(memory_space=pl.ANY)] * 10,
        out_specs=pl.BlockSpec(memory_space=pltpu.VMEM),
        scratch_shapes=[
            pltpu.VMEM((2 * peers, length, LANES), F32),
            pltpu.VMEM((listed + 2, 2 * BLOCK, LANES), BF16),
            pltpu.VMEM((listed + 2, 2 * BLOCK, LANES), BF16),
            pltpu.VMEM((half + 1, 2 * BLOCK, LANES), BF16),
            pltpu.VMEM((UNROLL, 2 * BLOCK, LANES), F32),
            pltpu.SemaphoreType.DMA((10,)),
            pltpu.SMEM((ceil_to(triples, LANES),), I32),
            pltpu.SemaphoreType.DMA,
        ],
        compiler_params=pltpu.CompilerParams(vmem_limit_bytes=58 << 20),
        name="purify",
    )


def make_place(rows, width):
    return pl.pallas_call(
        place_kernel,
        out_shape=jax.ShapeDtypeStruct((rows, width), F32),
        in_specs=[smem(), pl.BlockSpec(memory_space=pl.ANY)],
        out_specs=pl.BlockSpec(memory_space=pltpu.HBM),
        scratch_shapes=[pltpu.VMEM((BLOCK, width), F32), pltpu.SemaphoreType.DMA],
        compiler_params=pltpu.CompilerParams(vmem_limit_bytes=16 << 20),
        cost_estimate=pl.CostEstimate(
            flops=1_000_000_000, bytes_accessed=8_000_000, transcendentals=0
        ),
        name="place",
    )


def make_assemble(rows, width):
    return pl.pallas_call(
        assemble_kernel,
        out_shape=jax.ShapeDtypeStruct((rows, width), F32),
        in_specs=[
            smem(), pl.BlockSpec(memory_space=pl.ANY), pl.BlockSpec(memory_space=pltpu.VMEM)
        ],
        out_specs=pl.BlockSpec(memory_space=pl.ANY),
        scratch_shapes=[pltpu.SemaphoreType.DMA],
        input_output_aliases={1: 0},
        compiler_params=pltpu.CompilerParams(vmem_limit_bytes=16 << 20),
        name="assemble",
    )


def local(density, pattern):
    rows, width = density.shape
    layers, lines, cols = (lax.axis_size(a) for a in ("layer", "row", "col"))
    across = 4
    depth = lines // across
    pieces = rows // PIECE
    share = ceil_to(pieces * PARTS, QUARTERS) // QUARTERS * TILE
    length = pieces * PARTS * depth // QUARTERS * TILE
    assert layers // 2 * cols == across
    peers = across * across
    line, col, layer = (lax.axis_index(a) for a in ("row", "col", "layer"))
    tile = line * cols + col
    z = line // across
    where = jnp.stack(
        [tile, layer % 2, (layer - z) % QUARTERS, layer, line % across, layer // 2 * cols + col]
    ).astype(I32)
    listed = pattern.T

    blocks = width // BLOCK
    count, triples = sizes(blocks)

    packed = make_pack(depth, rows, share)(where, listed, density)
    where, packed = lax.optimization_barrier((where, packed))
    fixed = dict(depth=depth, across=across, length=length, spare=count + 1, pieces=pieces)
    book, near, state = make_lists(
        near_kernel, "near", 2,
        [scalars(f(blocks)) for f in (book_lengths, near_lengths, state_lengths)], [], **fixed,
    )(where, listed)
    along = [[z * across + y for z in range(depth)] for y in range(across)]
    got = lax.all_to_all(
        packed, "row", split_axis=0, concat_axis=0, tiled=True, axis_index_groups=along
    )
    got, book, near, state = lax.optimization_barrier((got, book, near, state))
    relayed = make_relay(depth, share, across, length)(where, got)

    def ring(core, z, fixed, over_x):
        places = [(i, fixed) if over_x else (fixed, i) for i in range(across)]
        return [
            ((x // cols * 2 + core) * lines + z * across + y) * cols + x % cols
            for x, y in places
        ]

    def rings(first):
        return [
            ring(core, z, fixed, (core == 0) == first)
            for core in range(2)
            for z in range(depth)
            for fixed in range(across)
        ]

    everywhere = ("layer", "row", "col")
    relayed, book, state = lax.optimization_barrier((relayed, book, state))
    mine = lax.all_to_all(
        relayed, everywhere, split_axis=0, concat_axis=0, tiled=True, axis_index_groups=rings(True)
    )
    far, state = make_lists(
        far_kernel, "far", 4,
        [scalars(far_lengths(blocks)), scalars(state_lengths(blocks))], [], **fixed,
    )(where, listed, book, state)
    mine, far, state = lax.optimization_barrier((mine, far, state))

    def turn(value, step):
        pairs = [
            (devices[i], devices[(i + step) % across])
            for devices in rings(False)
            for i in range(across)
        ]
        return lax.ppermute(value, everywhere, pairs)

    def swap(value):
        return lax.ppermute(value, "layer", [(i, i ^ 1) for i in range(layers)])

    middle = across // 2
    left, right = turn(mine, 1), turn(mine, -1)
    product_lists, pairs, entry = make_lists(
        product_kernel, "products", 3,
        [scalars(product_lengths(blocks)), scalars([triples]), scalars([2 * (count + 2)])],
        [16, ceil_to(triples, LANES)], outside=(1,),
        blocks=blocks, spare=count + 1, pieces=pieces,
    )(where, book, state)
    left, right, product_lists, pairs, entry = lax.optimization_barrier(
        (left, right, product_lists, pairs, entry)
    )
    own = (mine, left, right, turn(left[:middle], 1), turn(right[middle:], -1))
    other = tuple(swap(part) for part in own)
    (result_lists,) = make_lists(
        result_kernel, "results", 4, [scalars(result_lengths(blocks))], [],
        blocks=blocks, pieces=pieces,
    )(where, book, state, entry)
    band = make_main(width, peers, length)(
        where, near, far, product_lists, pairs, result_lists, *own, *other
    )
    full = make_place(rows, width)(where, band)
    return make_assemble(rows, width)(where, full, swap(band))


def solution(mesh):
    in_specs = (P(("row", "col"), None), P())
    out_specs = P(("row", "col"), None)
    return jax.shard_map(local, mesh=mesh, in_specs=in_specs, out_specs=out_specs, check_vma=False)
```

```python
import jax
import jax.numpy as jnp
from jax import lax
from jax.experimental import pallas as pl
from jax.experimental.pallas import tpu as pltpu
from jax.sharding import PartitionSpec as P

BLOCK = 64
SLOTS = 4
PIECE = 16
TILE = 8
LANES = 128
PIECES = BLOCK // PIECE
PARTS = SLOTS + 1
QUARTERS = 4
UNROLL = 4
GROUP = 4
START = 1024
I32 = jnp.int32
F32 = jnp.float32
BF16 = jnp.bfloat16


def ceil_to(value, unit):
    return -(-value // unit) * unit


def pack_kernel(where_ref, pattern_ref, density_ref, out_ref, buffer, taken, sem):
    tile = where_ref[0]
    shift = where_ref[2]
    rows = density_ref.shape[0]
    pieces = rows // PIECE
    depth, share = out_ref.shape[0], out_ref.shape[1]
    left = lax.broadcasted_iota(I32, (PIECE, LANES), 1) < BLOCK
    count = buffer.shape[0]
    for v in range(pieces * PARTS, count):
        buffer[v] = jnp.zeros((TILE, LANES), F32)

    def chunk(piece, block):
        start = pl.multiple_of((block >> 1) * LANES, LANES)
        return density_ref[piece * PIECE : (piece + 1) * PIECE, pl.ds(start, LANES)]

    for piece in range(pieces):
        block_row = (tile * pieces + piece) >> 2
        for pair in range(SLOTS // 2):
            first = pattern_ref[2 * pair, block_row]
            second = pattern_ref[2 * pair + 1, block_row]
            a = chunk(piece, first)
            b = chunk(piece, second)
            a = jnp.where((first & 1) == 0, a, pltpu.roll(a, BLOCK, 1))
            b = jnp.where((second & 1) == 1, b, pltpu.roll(b, BLOCK, 1))
            both = jnp.where(left, a, b)
            buffer[piece * PARTS + 2 * pair] = both[:TILE]
            buffer[piece * PARTS + 2 * pair + 1] = both[TILE:]
        d = chunk(piece, block_row)
        turned = pltpu.roll(d, BLOCK, 1)
        even = jnp.where(left[:TILE], d[:TILE], turned[TILE:])
        odd = jnp.where(left[:TILE], turned[:TILE], d[TILE:])
        buffer[piece * PARTS + SLOTS] = jnp.where((block_row & 1) == 0, even, odd)

    for i in range(share // TILE):
        taken[i * TILE : (i + 1) * TILE, :] = buffer[shift + QUARTERS * i]
    copies = [
        pltpu.make_async_copy(taken, out_ref.at[index], sem) for index in range(depth)
    ]
    for copy in copies:
        copy.start()
    for copy in copies:
        copy.wait()


def relay_kernel(where_ref, got_ref, out_ref, buffer, sem):
    quarter = where_ref[3]
    depth, share = got_ref.shape[0], got_ref.shape[1]
    for z in range(depth):
        extra = sum(((quarter + QUARTERS * i) < z).astype(I32) for i in range(depth // QUARTERS))
        start = pl.multiple_of((z * (share // TILE - 1) + extra) * TILE, TILE)
        buffer[pl.ds(start, share), :] = got_ref[z]
    peers, length = out_ref.shape[0], out_ref.shape[1]
    copies = [
        pltpu.make_async_copy(buffer.at[:length], out_ref.at[index], sem)
        for index in range(peers)
    ]
    for copy in copies:
        copy.start()
    for copy in copies:
        copy.wait()


class Part:
    def __init__(self, ref, start):
        self.ref, self.start = ref, start

    def __getitem__(self, i):
        return self.ref[self.start + i]

    def __setitem__(self, i, value):
        self.ref[self.start + i] = value


def parts_of(ref, lengths):
    parts, start = [], 0
    for length in lengths:
        parts.append(Part(ref, start))
        start += length
    return parts


def each(lo, hi, body):
    def step(i, carry):
        body(i)
        return carry

    lax.fori_loop(lo, hi, step, 0)


def clear(ref, start, count, value, unroll=8):
    def body(i):
        for u in range(unroll):
            ref[start + i * unroll + u] = value

    each(0, count // unroll, body)


def row_of(where_ref, pieces):
    first = where_ref[0] * pieces
    return jnp.where(where_ref[1] == 0, first >> 2, (first + pieces - 1) >> 2)


def neighbours_of(pattern_ref, r, cnt, used, names):
    blocks = pattern_ref.shape[1]

    def neighbour(b):
        @pl.when(used[b] == 0)
        def _():
            used[b] = 1
            n = cnt[0]
            names[n] = b
            cnt[0] = n + 1

    neighbour(r)
    for s in range(SLOTS):
        neighbour(pattern_ref[s, r])

    def incoming(a):
        hit = pattern_ref[0, a] == r
        for s in range(1, SLOTS):
            hit = hit | (pattern_ref[s, a] == r)

        @pl.when(hit)
        def _():
            neighbour(a)

    each(0, blocks, incoming)


def addressing(blocks, depth, across, length, pieces):
    low = (2 * across).bit_length() - 1
    scale = 65536 // pieces + 1
    assert all((g * scale) >> 16 == g // pieces for g in range(blocks * PIECES))
    share = length // TILE // depth

    def address(t, v):
        z = t >> low
        y = (t >> 1) & (across - 1)
        quarter = (v + z) & (QUARTERS - 1)
        before = z * share + sum(
            ((quarter + QUARTERS * i) < z).astype(I32) for i in range(depth // QUARTERS)
        )
        x = (quarter >> 1) * 2 + (t & 1)
        core = quarter & 1
        peer = jnp.where(core == 0, y * 4 + x, x * 4 + y)
        return (core * (4 * across) + peer) * length + (before + (v >> 2)) * TILE

    def split(g):
        t = (g * scale) >> 16
        return t, g - t * pieces

    def tiles_of(a, s, at_ref, n):
        for p in range(PIECES):
            t, g = split(a * PIECES + p)
            if s == SLOTS:
                at_ref[n * 4 + p] = address(t, g * PARTS + SLOTS)
            else:
                v = g * PARTS + (s // 2) * 2
                at_ref[n * 8 + 2 * p] = address(t, v)
                at_ref[n * 8 + 2 * p + 1] = address(t, v + 1)

    return tiles_of


def block_of(blocks, state, c, j, put):
    cnt, qn, cq, ql = parts_of(state, state_lengths(blocks))
    half = (blocks + 1) // 2
    q = j >> 1
    bit = 1 << (j & 1)
    word = cq[c * half + q]

    @pl.when((word & bit) == 0)
    def _():
        fresh = word == 0
        index = jnp.where(fresh, cnt[2] + 1, word >> 2)
        cnt[2] = cnt[2] + fresh.astype(I32)
        n = qn[c]
        ql[c * half + jnp.where(fresh, n, half - 1)] = jnp.where(
            fresh, q, ql[c * half + half - 1]
        )
        qn[c] = n + fresh.astype(I32)
        cq[c * half + q] = jnp.where(fresh, index * 4, word) + bit
        put(index * 2 + (j & 1))


def near_kernel(
    where_ref, pattern_ref, book, lists, state, *, depth, across, length, spare, pieces
):
    blocks = pattern_ref.shape[1]
    known, used, names = parts_of(book, book_lengths(blocks))
    meta, nat_at, nat_to, dia_at, dia_to = parts_of(lists, near_lengths(blocks))
    cnt, qn, _, _ = parts_of(state, state_lengths(blocks))
    half = (blocks + 1) // 2
    tiles_of = addressing(blocks, depth, across, length, pieces)
    clear(book, 0, 16 + blocks, 0)
    clear(state, 0, 16, 0)
    neighbours_of(pattern_ref, row_of(where_ref, pieces), known, used, names)

    def start(i):
        c = names[i]
        qn[c] = 0
        clear(state, 16 + blocks + c * half, half, 0, 8 if half % 8 == 0 else 1)

        def put_diagonal(dest):
            n = cnt[5]
            cnt[5] = n + 1
            dia_to[n] = dest
            tiles_of(c, SLOTS, dia_at, n)

        block_of(blocks, state, c, c, put_diagonal)
        for s in range(SLOTS):

            def put(dest):
                n = cnt[3]
                cnt[3] = n + 1
                nat_to[n] = dest * 2 + s % 2
                tiles_of(c, s, nat_at, n)

            block_of(blocks, state, c, pattern_ref[s, c], put)

    each(0, known[0], start)
    for u in range(UNROLL):
        nat_to[cnt[3] + u] = spare * 4
        dia_to[cnt[5] + u] = spare * 2
        for i in range(8):
            nat_at[(cnt[3] + u) * 8 + i] = 0
        for i in range(4):
            dia_at[(cnt[5] + u) * 4 + i] = 0
    meta[3] = cnt[3]
    meta[5] = cnt[5]
    meta[13] = where_ref[1]


def far_kernel(
    where_ref, pattern_ref, book, before, lists, state,
    *, depth, across, length, spare, pieces,
):
    blocks = pattern_ref.shape[1]
    known, used, names = parts_of(book, book_lengths(blocks))
    meta, tra_at, tra_to = parts_of(lists, far_lengths(blocks))
    _, qn_before, cq_before, ql_before = parts_of(before, state_lengths(blocks))
    cnt, qn, cq, ql = parts_of(state, state_lengths(blocks))
    half = (blocks + 1) // 2
    tiles_of = addressing(blocks, depth, across, length, pieces)
    clear(state, 0, 16, 0)
    cnt[2] = before[2]

    def copy(i):
        c = names[i]
        qn[c] = qn_before[c]
        unroll = 8 if half % 8 == 0 else 1

        def body(j):
            for u in range(unroll):
                at = c * half + j * unroll + u
                cq[at] = cq_before[at]
                ql[at] = ql_before[at]

        each(0, half // unroll, body)

    each(0, known[0], copy)

    def edges(a):
        ends = [pattern_ref[s, a] for s in range(SLOTS)]
        any_used = used[ends[0]]
        for b in ends[1:]:
            any_used = any_used | used[b]

        @pl.when(any_used > 0)
        def _():
            for s, b in enumerate(ends):

                @pl.when(used[b] > 0)
                def _():
                    def put(dest):
                        n = cnt[4]
                        cnt[4] = n + 1
                        tra_to[n] = dest * 2 + s % 2
                        tiles_of(a, s, tra_at, n)

                    block_of(blocks, state, b, a, put)

    each(0, blocks, edges)
    for u in range(UNROLL):
        tra_to[cnt[4] + u] = spare * 4
        for i in range(8):
            tra_at[(cnt[4] + u) * 8 + i] = 0
    meta[2] = cnt[2]
    meta[4] = cnt[4]


def move_used(source, target, used, sem):
    count = source.shape[0]

    def move(start, length):
        copy = pltpu.make_async_copy(
            source.at[pl.ds(start, length)], target.at[pl.ds(start, length)], sem
        )
        copy.start()
        copy.wait()

    move(0, min(START, count))

    @pl.when(used > START)
    def _():
        move(START, count - START)


def product_kernel(
    where_ref, book, state, lists, pairs_out, entry, cnt, pairs, sem, *, blocks, spare, pieces
):
    known, _, names = parts_of(book, book_lengths(blocks))
    _, qn, cq, ql = parts_of(state, state_lengths(blocks))
    meta, fa, fb = parts_of(lists, product_lengths(blocks))
    half = (blocks + 1) // 2
    r = row_of(where_ref, pieces)
    for i in range(16):
        cnt[i] = 0
    cnt[0] = known[0]
    for i in range(GROUP):
        pairs[i] = 0
    cnt[8] = 1

    def c_body(ci):
        c = names[ci]
        chunks = qn[c]
        mine = c == r

        def k_body(ki):
            k = names[ki]
            word = cq[c * half + (k >> 1)]
            bit = 1 << (k & 1)
            dest = (word >> 2) * 2 + (k & 1)

            @pl.when((word & bit) != 0)
            def _():
                group = cnt[8]
                base = group * GROUP

                def chunk(i, count):
                    q = ql[c * half + i]
                    a = cq[c * half + q]
                    b = cq[k * half + q]
                    at = jnp.where(mine, 1 + i, 0)
                    pairs[base + count] = (at << 20) + ((a >> 2) << 10) + (b >> 2)
                    return count + (((a & b) & 3) != 0).astype(I32)

                count = lax.fori_loop(0, chunks, chunk, 0)
                for u in range(GROUP):
                    pairs[base + count + u] = 0
                groups = (count + GROUP - 1) >> 2
                cnt[8] = group + groups
                span = group * 32 + groups
                entry[dest] = span
                code = dest * (1 << 17) + span

                @pl.when(c == k)
                def _():
                    n = cnt[6]
                    cnt[6] = n + 1
                    fa[n] = code

                @pl.when(c != k)
                def _():
                    n = cnt[7]
                    cnt[7] = n + 1
                    fb[n] = code

        each(0, cnt[0], k_body)

    each(0, cnt[0], c_body)

    for u in range(UNROLL):
        fa[cnt[6] + u] = spare * (1 << 18)
        fb[cnt[7] + u] = spare * (1 << 18)
    meta[6] = cnt[6]
    meta[7] = cnt[7]
    meta[8] = cnt[8]
    move_used(pairs, pairs_out, cnt[8] * GROUP, sem)


def result_kernel(where_ref, book, state, entry, lists, *, blocks, pieces):
    known, _, names = parts_of(book, book_lengths(blocks))
    _, qn, cq, ql = parts_of(state, state_lengths(blocks))
    meta, pp, mixl = parts_of(lists, result_lengths(blocks))
    half = (blocks + 1) // 2
    r = row_of(where_ref, pieces)

    def result(ci, n):
        c = names[ci]
        word = cq[r * half + (c >> 1)]
        code = c * (1 << 17) + entry[(word >> 2) * 2 + (c & 1)]
        pp[jnp.where(c == r, 0, n)] = code
        return jnp.where(c == r, n, n + 1)

    n = lax.fori_loop(0, known[0], result, 1)
    mixl[0] = 0

    def mix(i):
        mixl[1 + i] = cq[r * half + ql[r * half + i]] >> 2

    each(0, qn[r], mix)
    for u in range(UNROLL):
        pp[n + u] = 0
    meta[9] = n
    meta[10] = qn[r]


def two_parts(value):
    high = value.astype(BF16)
    low = (value - high.astype(F32)).astype(BF16)
    return jnp.concatenate([high, low], axis=0)


def times(lhs, rhs):
    return lax.dot_general(
        jnp.concatenate(lhs, axis=1),
        jnp.concatenate(rhs, axis=1),
        (((1,), (1,)), ((), ())),
        preferred_element_type=F32,
    )


def main_kernel(
    where_ref, near_lists, far_lists, product_lists, pairs_ref, result_lists,
    own_0, own_1, own_2, own_3, own_4, other_0, other_1, other_2, other_3, other_4,
    result,
    gathered, blocks_m, blocks_f, mixed, sums, sems, pairs, sem,
):
    blocks = result.shape[1] // BLOCK
    near, nat_at, nat_to, dia_at, dia_to = parts_of(near_lists, near_lengths(blocks))
    far, tra_at, tra_to = parts_of(far_lists, far_lengths(blocks))
    counts, fa, fb = parts_of(product_lists, product_lengths(blocks))
    extent, pp, mixl = parts_of(result_lists, result_lengths(blocks))
    core = where_ref[1]
    size = own_0.shape[0]
    half = own_3.shape[0]
    around = gathered.shape[0] // 2 // size

    def arrivals(refs, side, place, first):
        shifts = ((0, 0), (around - 1, 0), (1, 0), (2, 0), (2, half))
        return [
            pltpu.make_async_copy(
                ref,
                gathered.at[
                    pl.ds(
                        side * around * size + ((place + shift) & (around - 1)) * size + at,
                        ref.shape[0],
                    )
                ],
                sems.at[first + i],
            )
            for i, (ref, (shift, at)) in enumerate(zip(refs, shifts))
        ]

    y, x = where_ref[4], where_ref[5]
    copies = arrivals(
        (own_0, own_1, own_2, own_3, own_4), core, jnp.where(core == 0, y, x), 0
    ) + arrivals(
        (other_0, other_1, other_2, other_3, other_4), 1 - core, jnp.where(core == 0, x, y), 5
    )
    for copy in copies:
        copy.start()
    move_used(pairs_ref, pairs, counts[8] * GROUP, sem)
    right = lax.broadcasted_iota(I32, (BLOCK, LANES), 1) // BLOCK
    none = jnp.zeros((2 * BLOCK, LANES), BF16)

    def clear_blocks(i):
        blocks_m[i] = none
        blocks_f[i] = none

    each(0, far[2] + 1, clear_blocks)

    def clear_result(i):
        start = pl.multiple_of(i * LANES, LANES)
        result[:, pl.ds(start, LANES)] = jnp.zeros((result.shape[0], LANES), F32)

    each(0, result.shape[1] // LANES, clear_result)
    mixed[0] = none
    flat = gathered.reshape(gathered.shape[0] * gathered.shape[1], LANES)
    for copy in copies:
        copy.wait()

    def steps(count):
        return (count + UNROLL - 1) >> 2

    def rows_at(at_ref, n, count):
        return [
            flat[pl.ds(pl.multiple_of(at_ref[n * count + i], TILE), TILE), :]
            for i in range(count)
        ]

    def add(store, index, value):
        store[index] = store[index] + two_parts(value)

    def natural(i):
        for u in range(UNROLL):
            n = i * UNROLL + u
            to = nat_to[n]
            parity = (to >> 1) & 1
            x = jnp.concatenate(rows_at(nat_at, n, 8), axis=0)
            x = jnp.where((to & 1) == parity, x, pltpu.roll(x, BLOCK, 1))
            add(blocks_m, to >> 2, jnp.where(right == parity, x, 0.0))

    def transposed(i):
        for u in range(UNROLL):
            n = i * UNROLL + u
            to = tra_to[n]
            parity = (to >> 1) & 1
            x = jnp.concatenate(rows_at(tra_at, n, 8), axis=0).T
            x = jnp.where((to & 1) == 0, x[:BLOCK], x[BLOCK:])
            x = jnp.concatenate([x, x], axis=1)
            add(blocks_m, to >> 2, jnp.where(right == parity, x, 0.0))

    def diagonal(i):
        for u in range(UNROLL):
            n = i * UNROLL + u
            to = dia_to[n]
            parity = to & 1
            parts = []
            for x in rows_at(dia_at, n, 4):
                turned = pltpu.roll(x, BLOCK, 1)
                parts.append(jnp.where(right[:TILE] == 0, x, turned))
                parts.append(jnp.where(right[:TILE] == 0, turned, x))
            x = jnp.concatenate(parts, axis=0)
            add(blocks_m, to >> 1, jnp.where(right == parity, x, 0.0))

    each(0, steps(near[3]), natural)
    each(0, steps(far[4]), transposed)
    each(0, steps(near[5]), diagonal)

    def fold(total):
        s = total[:BLOCK] + total[BLOCK:]
        return s + pltpu.roll(s, BLOCK, 1)

    def codes_of(word, g):
        n = word & 31
        group = jnp.where(g < n, ((word >> 5) & 4095) + g, 0)
        return [pairs[group * GROUP + u] for u in range(GROUP)]

    def filtered(list_ref, static):
        def product(word, groups):
            lhs, rhs = [], []
            for g in groups:
                for code in codes_of(word, g):
                    lhs.append(blocks_m[(code >> 10) & 1023])
                    rhs.append(blocks_m[code & 1023])
            return times(lhs, rhs)

        def body(i):
            words = [list_ref[i * UNROLL + u] for u in range(UNROLL)]
            for u in range(UNROLL):
                sums[u] = product(words[u], range(static))
            most = words[0] & 31
            for word in words[1:]:
                most = jnp.maximum(most, word & 31)

            def more(g):
                for u in range(UNROLL):
                    sums[u] = sums[u] + product(words[u], [g])

            each(static, most, more)
            for u in range(UNROLL):
                dest = words[u] >> 17
                value = fold(sums[u])
                add(blocks_f, dest >> 1, jnp.where(right == (dest & 1), value, 0.0))

        return body

    each(0, steps(counts[6]), filtered(fa, 3))
    each(0, steps(counts[7]), filtered(fb, 1))

    def mix(i):
        index = mixl[1 + i]
        m = blocks_m[index].astype(F32)
        f = blocks_f[index].astype(F32)
        mixed[1 + i] = two_parts(
            m[:BLOCK] + m[BLOCK:] - 1.5 * (f[:BLOCK] + f[BLOCK:])
        )

    each(0, extent[10], mix)

    def purified(first, count, static, i):
        def product(word, groups):
            lhs, rhs = [], []
            for g in groups:
                for code in codes_of(word, g):
                    lhs += [blocks_f[(code >> 10) & 1023], mixed[code >> 20]]
                    rhs += [blocks_m[code & 1023], blocks_f[code & 1023]]
            return times(lhs, rhs)

        words = [pp[first + i * count + u] for u in range(count)]
        for u in range(count):
            sums[u] = product(words[u], range(static))
        most = words[0] & 31
        for word in words[1:]:
            most = jnp.maximum(most, word & 31)

        def more(g):
            for u in range(count):
                sums[u] = sums[u] + product(words[u], [g])

        each(static, most, more)
        for u in range(count):
            c = words[u] >> 17
            lanes = pl.ds(pl.multiple_of((c >> 1) * LANES, LANES), LANES)
            value = 2.0 * fold(sums[u])
            result[:, lanes] = result[:, lanes] + jnp.where(right == (c & 1), value, 0.0)

    purified(0, 1, 3, 0)
    each(0, steps(extent[9] - 1), lambda i: purified(1, UNROLL, 1, i))


def cases(where_ref, rows, mine, act):
    tile = where_ref[0]
    skip = tile * rows - ((tile * (rows // PIECE)) >> 2) * BLOCK
    for core in range(2):
        for cut in range(0, BLOCK, PIECE):
            if not 0 < rows - (BLOCK - cut) <= BLOCK:
                continue
            upper = (core == 0) == mine
            source = pl.ds(cut, BLOCK - cut) if upper else pl.ds(0, rows - BLOCK + cut)
            target = pl.ds(0, BLOCK - cut) if upper else pl.ds(BLOCK - cut, rows - BLOCK + cut)

            @pl.when((where_ref[1] == core) & (skip == cut))
            def _():
                act(source, target)


def place_kernel(where_ref, band_ref, out_ref, held, sem):
    load = pltpu.make_async_copy(band_ref, held, sem)
    load.start()
    load.wait()

    def act(source, target):
        copy = pltpu.make_async_copy(held.at[source, :], out_ref.at[target, :], sem)
        copy.start()
        copy.wait()

    cases(where_ref, out_ref.shape[0], True, act)


def assemble_kernel(where_ref, full_ref, other_ref, out_ref, sem):
    def act(source, target):
        copy = pltpu.make_async_copy(other_ref.at[source, :], out_ref.at[target, :], sem)
        copy.start()
        copy.wait()

    cases(where_ref, out_ref.shape[0], False, act)


def smem():
    return pl.BlockSpec(memory_space=pltpu.SMEM)


def make_pack(depth, rows, share):
    count = ceil_to(rows // PIECE * PARTS, QUARTERS)
    return pl.pallas_call(
        pack_kernel,
        out_shape=jax.ShapeDtypeStruct((depth, share, LANES), F32),
        in_specs=[smem(), smem(), pl.BlockSpec(memory_space=pltpu.VMEM)],
        out_specs=pl.BlockSpec(memory_space=pl.ANY),
        scratch_shapes=[
            pltpu.VMEM((count, TILE, LANES), F32),
            pltpu.VMEM((share, LANES), F32),
            pltpu.SemaphoreType.DMA,
        ],
        compiler_params=pltpu.CompilerParams(vmem_limit_bytes=16 << 20),
        name="pack",
    )


def make_relay(depth, share, peers, length):
    return pl.pallas_call(
        relay_kernel,
        out_shape=jax.ShapeDtypeStruct((peers, length, LANES), F32),
        in_specs=[smem(), pl.BlockSpec(memory_space=pltpu.VMEM)],
        out_specs=pl.BlockSpec(memory_space=pltpu.HBM),
        scratch_shapes=[
            pltpu.VMEM((length + TILE, LANES), F32),
            pltpu.SemaphoreType.DMA,
        ],
        compiler_params=pltpu.CompilerParams(vmem_limit_bytes=16 << 20),
        name="relay",
    )


def sizes(blocks):
    listed = blocks * (1 + 2 * SLOTS)
    triangles = blocks * (SLOTS * (SLOTS - 1) // 2 + SLOTS * SLOTS // 3 + 1)
    triples = ceil_to(4 * listed + 4 * blocks * SLOTS + 6 * triangles + 64, 1024)
    return listed, triples


def book_lengths(blocks):
    return [16, blocks, blocks]


def state_lengths(blocks):
    half = (blocks + 1) // 2
    return [16, blocks, blocks * half, blocks * half]


def near_lengths(blocks):
    edges = blocks * SLOTS + UNROLL
    diagonal = blocks + UNROLL
    return [16, edges * 8, edges, diagonal * 4, diagonal]


def far_lengths(blocks):
    edges = blocks * SLOTS + UNROLL
    return [16, edges * 8, edges]


def product_lengths(blocks):
    listed, _ = sizes(blocks)
    return [16, blocks + UNROLL, listed + UNROLL]


def result_lengths(blocks):
    return [16, blocks + 1 + UNROLL, (blocks + 1) // 2 + 1]


def scalars(lengths):
    return jax.ShapeDtypeStruct((ceil_to(sum(lengths), LANES),), I32)


def make_lists(kernel, name, inputs, outputs, scratch, outside=(), **fixed):
    def body(*refs):
        kernel(*refs, **fixed)

    return pl.pallas_call(
        body,
        out_shape=outputs,
        in_specs=[smem()] * inputs,
        out_specs=[
            pl.BlockSpec(memory_space=pltpu.HBM) if i in outside else smem()
            for i in range(len(outputs))
        ],
        scratch_shapes=[pltpu.SMEM((n,), I32) for n in scratch]
        + [pltpu.SemaphoreType.DMA] * len(outside),
        compiler_params=pltpu.CompilerParams(vmem_limit_bytes=61 << 20),
        cost_estimate=pl.CostEstimate(
            flops=10_000_000_000, bytes_accessed=25_000_000, transcendentals=0
        ),
        name=name,
    )


def make_main(width, peers, length):
    blocks = width // BLOCK
    half = (blocks + 1) // 2
    listed, triples = sizes(blocks)
    return pl.pallas_call(
        main_kernel,
        out_shape=jax.ShapeDtypeStruct((BLOCK, width), F32),
        in_specs=[smem()] * 4
        + [pl.BlockSpec(memory_space=pltpu.HBM), smem()]
        + [pl.BlockSpec(memory_space=pl.ANY)] * 10,
        out_specs=pl.BlockSpec(memory_space=pltpu.VMEM),
        scratch_shapes=[
            pltpu.VMEM((2 * peers, length, LANES), F32),
            pltpu.VMEM((listed + 2, 2 * BLOCK, LANES), BF16),
            pltpu.VMEM((listed + 2, 2 * BLOCK, LANES), BF16),
            pltpu.VMEM((half + 1, 2 * BLOCK, LANES), BF16),
            pltpu.VMEM((UNROLL, 2 * BLOCK, LANES), F32),
            pltpu.SemaphoreType.DMA((10,)),
            pltpu.SMEM((ceil_to(triples, LANES),), I32),
            pltpu.SemaphoreType.DMA,
        ],
        compiler_params=pltpu.CompilerParams(vmem_limit_bytes=58 << 20),
        name="purify",
    )


def make_place(rows, width):
    return pl.pallas_call(
        place_kernel,
        out_shape=jax.ShapeDtypeStruct((rows, width), F32),
        in_specs=[smem(), pl.BlockSpec(memory_space=pl.ANY)],
        out_specs=pl.BlockSpec(memory_space=pltpu.HBM),
        scratch_shapes=[pltpu.VMEM((BLOCK, width), F32), pltpu.SemaphoreType.DMA],
        compiler_params=pltpu.CompilerParams(vmem_limit_bytes=16 << 20),
        cost_estimate=pl.CostEstimate(
            flops=1_000_000_000, bytes_accessed=8_000_000, transcendentals=0
        ),
        name="place",
    )


def make_assemble(rows, width):
    return pl.pallas_call(
        assemble_kernel,
        out_shape=jax.ShapeDtypeStruct((rows, width), F32),
        in_specs=[
            smem(), pl.BlockSpec(memory_space=pl.ANY), pl.BlockSpec(memory_space=pltpu.VMEM)
        ],
        out_specs=pl.BlockSpec(memory_space=pl.ANY),
        scratch_shapes=[pltpu.SemaphoreType.DMA],
        input_output_aliases={1: 0},
        compiler_params=pltpu.CompilerParams(vmem_limit_bytes=16 << 20),
        name="assemble",
    )


def local(density, pattern):
    rows, width = density.shape
    layers, lines, cols = (lax.axis_size(a) for a in ("layer", "row", "col"))
    across = 4
    depth = lines // across
    pieces = rows // PIECE
    share = ceil_to(pieces * PARTS, QUARTERS) // QUARTERS * TILE
    length = pieces * PARTS * depth // QUARTERS * TILE
    assert layers // 2 * cols == across
    peers = across * across
    line, col, layer = (lax.axis_index(a) for a in ("row", "col", "layer"))
    tile = line * cols + col
    z = line // across
    where = jnp.stack(
        [tile, layer % 2, (layer - z) % QUARTERS, layer, line % across, layer // 2 * cols + col]
    ).astype(I32)
    listed = pattern.T

    blocks = width // BLOCK
    count, triples = sizes(blocks)

    packed = make_pack(depth, rows, share)(where, listed, density)
    where, packed = lax.optimization_barrier((where, packed))
    fixed = dict(depth=depth, across=across, length=length, spare=count + 1, pieces=pieces)
    book, near, state = make_lists(
        near_kernel, "near", 2,
        [scalars(f(blocks)) for f in (book_lengths, near_lengths, state_lengths)], [], **fixed,
    )(where, listed)
    along = [[z * across + y for z in range(depth)] for y in range(across)]
    got = lax.all_to_all(
        packed, "row", split_axis=0, concat_axis=0, tiled=True, axis_index_groups=along
    )
    got, book, near, state = lax.optimization_barrier((got, book, near, state))
    relayed = make_relay(depth, share, across, length)(where, got)

    def ring(core, z, fixed, over_x):
        places = [(i, fixed) if over_x else (fixed, i) for i in range(across)]
        return [
            ((x // cols * 2 + core) * lines + z * across + y) * cols + x % cols
            for x, y in places
        ]

    def rings(first):
        return [
            ring(core, z, fixed, (core == 0) == first)
            for core in range(2)
            for z in range(depth)
            for fixed in range(across)
        ]

    everywhere = ("layer", "row", "col")
    relayed, book, state = lax.optimization_barrier((relayed, book, state))
    mine = lax.all_to_all(
        relayed, everywhere, split_axis=0, concat_axis=0, tiled=True, axis_index_groups=rings(True)
    )
    far, state = make_lists(
        far_kernel, "far", 4,
        [scalars(far_lengths(blocks)), scalars(state_lengths(blocks))], [], **fixed,
    )(where, listed, book, state)
    mine, far, state = lax.optimization_barrier((mine, far, state))

    def turn(value, step):
        pairs = [
            (devices[i], devices[(i + step) % across])
            for devices in rings(False)
            for i in range(across)
        ]
        return lax.ppermute(value, everywhere, pairs)

    def swap(value):
        return lax.ppermute(value, "layer", [(i, i ^ 1) for i in range(layers)])

    middle = across // 2
    left, right = turn(mine, 1), turn(mine, -1)
    product_lists, pairs, entry = make_lists(
        product_kernel, "products", 3,
        [scalars(product_lengths(blocks)), scalars([triples]), scalars([2 * (count + 2)])],
        [16, ceil_to(triples, LANES)], outside=(1,),
        blocks=blocks, spare=count + 1, pieces=pieces,
    )(where, book, state)
    left, right, product_lists, pairs, entry = lax.optimization_barrier(
        (left, right, product_lists, pairs, entry)
    )
    own = (mine, left, right, turn(left[:middle], 1), turn(right[middle:], -1))
    other = tuple(swap(part) for part in own)
    (result_lists,) = make_lists(
        result_kernel, "results", 4, [scalars(result_lengths(blocks))], [],
        blocks=blocks, pieces=pieces,
    )(where, book, state, entry)
    band = make_main(width, peers, length)(
        where, near, far, product_lists, pairs, result_lists, *own, *other
    )
    full = make_place(rows, width)(where, band)
    return make_assemble(rows, width)(where, full, swap(band))


def solution(mesh):
    in_specs = (P(("row", "col"), None), P())
    out_specs = P(("row", "col"), None)
    return jax.shard_map(local, mesh=mesh, in_specs=in_specs, out_specs=out_specs, check_vma=False)
```

```python
import jax
import jax.numpy as jnp
from jax import lax
from jax.experimental import pallas as pl
from jax.experimental.pallas import tpu as pltpu
from jax.sharding import PartitionSpec as P

BLOCK = 64
SLOTS = 4
PIECE = 16
TILE = 8
LANES = 128
PIECES = BLOCK // PIECE
PARTS = SLOTS + 1
QUARTERS = 4
UNROLL = 4
GROUP = 4
START = 1024
I32 = jnp.int32
F32 = jnp.float32
BF16 = jnp.bfloat16


def ceil_to(value, unit):
    return -(-value // unit) * unit


def pack_kernel(where_ref, pattern_ref, density_ref, out_ref, buffer, taken, sem):
    tile = where_ref[0]
    shift = where_ref[2]
    rows = density_ref.shape[0]
    pieces = rows // PIECE
    depth, share = out_ref.shape[0], out_ref.shape[1]
    left = lax.broadcasted_iota(I32, (PIECE, LANES), 1) < BLOCK
    count = buffer.shape[0]
    for v in range(pieces * PARTS, count):
        buffer[v] = jnp.zeros((TILE, LANES), F32)

    def chunk(piece, block):
        start = pl.multiple_of((block >> 1) * LANES, LANES)
        return density_ref[piece * PIECE : (piece + 1) * PIECE, pl.ds(start, LANES)]

    for piece in range(pieces):
        block_row = (tile * pieces + piece) >> 2
        for pair in range(SLOTS // 2):
            first = pattern_ref[2 * pair, block_row]
            second = pattern_ref[2 * pair + 1, block_row]
            a = chunk(piece, first)
            b = chunk(piece, second)
            a = jnp.where((first & 1) == 0, a, pltpu.roll(a, BLOCK, 1))
            b = jnp.where((second & 1) == 1, b, pltpu.roll(b, BLOCK, 1))
            both = jnp.where(left, a, b)
            buffer[piece * PARTS + 2 * pair] = both[:TILE]
            buffer[piece * PARTS + 2 * pair + 1] = both[TILE:]
        d = chunk(piece, block_row)
        turned = pltpu.roll(d, BLOCK, 1)
        even = jnp.where(left[:TILE], d[:TILE], turned[TILE:])
        odd = jnp.where(left[:TILE], turned[:TILE], d[TILE:])
        buffer[piece * PARTS + SLOTS] = jnp.where((block_row & 1) == 0, even, odd)

    for i in range(share // TILE):
        taken[i * TILE : (i + 1) * TILE, :] = buffer[shift + QUARTERS * i]
    copies = [
        pltpu.make_async_copy(taken, out_ref.at[index], sem) for index in range(depth)
    ]
    for copy in copies:
        copy.start()
    for copy in copies:
        copy.wait()


def relay_kernel(where_ref, got_ref, out_ref, buffer, sem):
    quarter = where_ref[3]
    depth, share = got_ref.shape[0], got_ref.shape[1]
    for z in range(depth):
        extra = sum(((quarter + QUARTERS * i) < z).astype(I32) for i in range(depth // QUARTERS))
        start = pl.multiple_of((z * (share // TILE - 1) + extra) * TILE, TILE)
        buffer[pl.ds(start, share), :] = got_ref[z]
    peers, length = out_ref.shape[0], out_ref.shape[1]
    copies = [
        pltpu.make_async_copy(buffer.at[:length], out_ref.at[index], sem)
        for index in range(peers)
    ]
    for copy in copies:
        copy.start()
    for copy in copies:
        copy.wait()


class Part:
    def __init__(self, ref, start):
        self.ref, self.start = ref, start

    def __getitem__(self, i):
        return self.ref[self.start + i]

    def __setitem__(self, i, value):
        self.ref[self.start + i] = value


def parts_of(ref, lengths):
    parts, start = [], 0
    for length in lengths:
        parts.append(Part(ref, start))
        start += length
    return parts


def each(lo, hi, body):
    def step(i, carry):
        body(i)
        return carry

    lax.fori_loop(lo, hi, step, 0)


def clear(ref, start, count, value, unroll=8):
    def body(i):
        for u in range(unroll):
            ref[start + i * unroll + u] = value

    each(0, count // unroll, body)


def row_of(where_ref, pieces):
    first = where_ref[0] * pieces
    return jnp.where(where_ref[1] == 0, first >> 2, (first + pieces - 1) >> 2)


def neighbours_of(pattern_ref, r, cnt, used, names):
    blocks = pattern_ref.shape[1]

    def neighbour(b):
        @pl.when(used[b] == 0)
        def _():
            used[b] = 1
            n = cnt[0]
            names[n] = b
            cnt[0] = n + 1

    neighbour(r)
    for s in range(SLOTS):
        neighbour(pattern_ref[s, r])

    def incoming(a):
        hit = pattern_ref[0, a] == r
        for s in range(1, SLOTS):
            hit = hit | (pattern_ref[s, a] == r)

        @pl.when(hit)
        def _():
            neighbour(a)

    each(0, blocks, incoming)


def addressing(blocks, depth, across, length, pieces):
    low = (2 * across).bit_length() - 1
    scale = 65536 // pieces + 1
    assert all((g * scale) >> 16 == g // pieces for g in range(blocks * PIECES))
    share = length // TILE // depth

    def address(t, v):
        z = t >> low
        y = (t >> 1) & (across - 1)
        quarter = (v + z) & (QUARTERS - 1)
        before = z * share + sum(
            ((quarter + QUARTERS * i) < z).astype(I32) for i in range(depth // QUARTERS)
        )
        x = (quarter >> 1) * 2 + (t & 1)
        core = quarter & 1
        peer = jnp.where(core == 0, y * 4 + x, x * 4 + y)
        return (core * (4 * across) + peer) * length + (before + (v >> 2)) * TILE

    def split(g):
        t = (g * scale) >> 16
        return t, g - t * pieces

    def tiles_of(a, s, at_ref, n):
        for p in range(PIECES):
            t, g = split(a * PIECES + p)
            if s == SLOTS:
                at_ref[n * 4 + p] = address(t, g * PARTS + SLOTS)
            else:
                v = g * PARTS + (s // 2) * 2
                at_ref[n * 8 + 2 * p] = address(t, v)
                at_ref[n * 8 + 2 * p + 1] = address(t, v + 1)

    return tiles_of


def block_of(blocks, state, c, j, put):
    cnt, qn, cq, ql = parts_of(state, state_lengths(blocks))
    half = (blocks + 1) // 2
    q = j >> 1
    bit = 1 << (j & 1)
    word = cq[c * half + q]

    @pl.when((word & bit) == 0)
    def _():
        fresh = word == 0
        index = jnp.where(fresh, cnt[2] + 1, word >> 2)
        cnt[2] = cnt[2] + fresh.astype(I32)
        n = qn[c]
        ql[c * half + jnp.where(fresh, n, half - 1)] = jnp.where(
            fresh, q, ql[c * half + half - 1]
        )
        qn[c] = n + fresh.astype(I32)
        cq[c * half + q] = jnp.where(fresh, index * 4, word) + bit
        put(index * 2 + (j & 1))


def near_kernel(
    where_ref, pattern_ref, book, lists, state, *, depth, across, length, spare, pieces
):
    blocks = pattern_ref.shape[1]
    known, used, names = parts_of(book, book_lengths(blocks))
    meta, nat_at, nat_to, dia_at, dia_to = parts_of(lists, near_lengths(blocks))
    cnt, qn, _, _ = parts_of(state, state_lengths(blocks))
    half = (blocks + 1) // 2
    tiles_of = addressing(blocks, depth, across, length, pieces)
    clear(book, 0, 16 + blocks, 0)
    clear(state, 0, 16, 0)
    neighbours_of(pattern_ref, row_of(where_ref, pieces), known, used, names)

    def start(i):
        c = names[i]
        qn[c] = 0
        clear(state, 16 + blocks + c * half, half, 0, 8 if half % 8 == 0 else 1)

        def put_diagonal(dest):
            n = cnt[5]
            cnt[5] = n + 1
            dia_to[n] = dest
            tiles_of(c, SLOTS, dia_at, n)

        block_of(blocks, state, c, c, put_diagonal)
        for s in range(SLOTS):

            def put(dest):
                n = cnt[3]
                cnt[3] = n + 1
                nat_to[n] = dest * 2 + s % 2
                tiles_of(c, s, nat_at, n)

            block_of(blocks, state, c, pattern_ref[s, c], put)

    each(0, known[0], start)
    for u in range(UNROLL):
        nat_to[cnt[3] + u] = spare * 4
        dia_to[cnt[5] + u] = spare * 2
        for i in range(8):
            nat_at[(cnt[3] + u) * 8 + i] = 0
        for i in range(4):
            dia_at[(cnt[5] + u) * 4 + i] = 0
    meta[3] = cnt[3]
    meta[5] = cnt[5]
    meta[13] = where_ref[1]


def far_kernel(
    where_ref, pattern_ref, book, before, lists, state,
    *, depth, across, length, spare, pieces,
):
    blocks = pattern_ref.shape[1]
    known, used, names = parts_of(book, book_lengths(blocks))
    meta, tra_at, tra_to = parts_of(lists, far_lengths(blocks))
    _, qn_before, cq_before, ql_before = parts_of(before, state_lengths(blocks))
    cnt, qn, cq, ql = parts_of(state, state_lengths(blocks))
    half = (blocks + 1) // 2
    tiles_of = addressing(blocks, depth, across, length, pieces)
    clear(state, 0, 16, 0)
    cnt[2] = before[2]

    def copy(i):
        c = names[i]
        qn[c] = qn_before[c]
        unroll = 8 if half % 8 == 0 else 1

        def body(j):
            for u in range(unroll):
                at = c * half + j * unroll + u
                cq[at] = cq_before[at]
                ql[at] = ql_before[at]

        each(0, half // unroll, body)

    each(0, known[0], copy)

    def edges(a):
        ends = [pattern_ref[s, a] for s in range(SLOTS)]
        any_used = used[ends[0]]
        for b in ends[1:]:
            any_used = any_used | used[b]

        @pl.when(any_used > 0)
        def _():
            for s, b in enumerate(ends):

                @pl.when(used[b] > 0)
                def _():
                    def put(dest):
                        n = cnt[4]
                        cnt[4] = n + 1
                        tra_to[n] = dest * 2 + s % 2
                        tiles_of(a, s, tra_at, n)

                    block_of(blocks, state, b, a, put)

    each(0, blocks, edges)
    for u in range(UNROLL):
        tra_to[cnt[4] + u] = spare * 4
        for i in range(8):
            tra_at[(cnt[4] + u) * 8 + i] = 0
    meta[2] = cnt[2]
    meta[4] = cnt[4]


def move_used(source, target, used, sem):
    count = source.shape[0]

    def move(start, length):
        copy = pltpu.make_async_copy(
            source.at[pl.ds(start, length)], target.at[pl.ds(start, length)], sem
        )
        copy.start()
        copy.wait()

    move(0, min(START, count))

    @pl.when(used > START)
    def _():
        move(START, count - START)


def product_kernel(
    where_ref, book, state, lists, pairs_out, entry, cnt, pairs, sem, *, blocks, spare, pieces
):
    known, _, names = parts_of(book, book_lengths(blocks))
    _, qn, cq, ql = parts_of(state, state_lengths(blocks))
    meta, fa, fb = parts_of(lists, product_lengths(blocks))
    half = (blocks + 1) // 2
    r = row_of(where_ref, pieces)
    for i in range(16):
        cnt[i] = 0
    cnt[0] = known[0]
    for i in range(GROUP):
        pairs[i] = 0
    cnt[8] = 1

    def c_body(ci):
        c = names[ci]
        chunks = qn[c]
        mine = c == r

        def k_body(ki):
            k = names[ki]
            word = cq[c * half + (k >> 1)]
            bit = 1 << (k & 1)
            dest = (word >> 2) * 2 + (k & 1)

            @pl.when((word & bit) != 0)
            def _():
                group = cnt[8]
                base = group * GROUP

                def chunk(i, count):
                    q = ql[c * half + i]
                    a = cq[c * half + q]
                    b = cq[k * half + q]
                    at = jnp.where(mine, 1 + i, 0)
                    pairs[base + count] = (at << 20) + ((a >> 2) << 10) + (b >> 2)
                    return count + (((a & b) & 3) != 0).astype(I32)

                count = lax.fori_loop(0, chunks, chunk, 0)
                for u in range(GROUP):
                    pairs[base + count + u] = 0
                groups = (count + GROUP - 1) >> 2
                cnt[8] = group + groups
                span = group * 32 + groups
                entry[dest] = span
                code = dest * (1 << 17) + span

                @pl.when(c == k)
                def _():
                    n = cnt[6]
                    cnt[6] = n + 1
                    fa[n] = code

                @pl.when(c != k)
                def _():
                    n = cnt[7]
                    cnt[7] = n + 1
                    fb[n] = code

        each(0, cnt[0], k_body)

    each(0, cnt[0], c_body)

    for u in range(UNROLL):
        fa[cnt[6] + u] = spare * (1 << 18)
        fb[cnt[7] + u] = spare * (1 << 18)
    meta[6] = cnt[6]
    meta[7] = cnt[7]
    meta[8] = cnt[8]
    move_used(pairs, pairs_out, cnt[8] * GROUP, sem)


def result_kernel(where_ref, book, state, entry, lists, *, blocks, pieces):
    known, _, names = parts_of(book, book_lengths(blocks))
    _, qn, cq, ql = parts_of(state, state_lengths(blocks))
    meta, pp, mixl = parts_of(lists, result_lengths(blocks))
    half = (blocks + 1) // 2
    r = row_of(where_ref, pieces)

    def result(ci, n):
        c = names[ci]
        word = cq[r * half + (c >> 1)]
        code = c * (1 << 17) + entry[(word >> 2) * 2 + (c & 1)]
        pp[jnp.where(c == r, 0, n)] = code
        return jnp.where(c == r, n, n + 1)

    n = lax.fori_loop(0, known[0], result, 1)
    mixl[0] = 0

    def mix(i):
        mixl[1 + i] = cq[r * half + ql[r * half + i]] >> 2

    each(0, qn[r], mix)
    for u in range(UNROLL):
        pp[n + u] = 0
    meta[9] = n
    meta[10] = qn[r]


def two_parts(value):
    high = value.astype(BF16)
    low = (value - high.astype(F32)).astype(BF16)
    return jnp.concatenate([high, low], axis=0)


def times(lhs, rhs):
    return lax.dot_general(
        jnp.concatenate(lhs, axis=1),
        jnp.concatenate(rhs, axis=1),
        (((1,), (1,)), ((), ())),
        preferred_element_type=F32,
    )


def main_kernel(
    where_ref, near_lists, far_lists, product_lists, pairs_ref, result_lists,
    own_0, own_1, own_2, own_3, own_4, other_0, other_1, other_2, other_3, other_4,
    result,
    gathered, blocks_m, blocks_f, mixed, sums, sems, pairs, sem,
):
    blocks = result.shape[1] // BLOCK
    near, nat_at, nat_to, dia_at, dia_to = parts_of(near_lists, near_lengths(blocks))
    far, tra_at, tra_to = parts_of(far_lists, far_lengths(blocks))
    counts, fa, fb = parts_of(product_lists, product_lengths(blocks))
    extent, pp, mixl = parts_of(result_lists, result_lengths(blocks))
    core = where_ref[1]
    size = own_0.shape[0]
    half = own_3.shape[0]
    around = gathered.shape[0] // 2 // size

    def arrivals(refs, side, place, first):
        shifts = ((0, 0), (around - 1, 0), (1, 0), (2, 0), (2, half))
        return [
            pltpu.make_async_copy(
                ref,
                gathered.at[
                    pl.ds(
                        side * around * size + ((place + shift) & (around - 1)) * size + at,
                        ref.shape[0],
                    )
                ],
                sems.at[first + i],
            )
            for i, (ref, (shift, at)) in enumerate(zip(refs, shifts))
        ]

    y, x = where_ref[4], where_ref[5]
    copies = arrivals(
        (own_0, own_1, own_2, own_3, own_4), core, jnp.where(core == 0, y, x), 0
    ) + arrivals(
        (other_0, other_1, other_2, other_3, other_4), 1 - core, jnp.where(core == 0, x, y), 5
    )
    for copy in copies:
        copy.start()
    move_used(pairs_ref, pairs, counts[8] * GROUP, sem)
    right = lax.broadcasted_iota(I32, (BLOCK, LANES), 1) // BLOCK
    none = jnp.zeros((2 * BLOCK, LANES), BF16)

    def clear_blocks(i):
        blocks_m[i] = none
        blocks_f[i] = none

    each(0, far[2] + 1, clear_blocks)

    def clear_result(i):
        start = pl.multiple_of(i * LANES, LANES)
        result[:, pl.ds(start, LANES)] = jnp.zeros((result.shape[0], LANES), F32)

    each(0, result.shape[1] // LANES, clear_result)
    mixed[0] = none
    flat = gathered.reshape(gathered.shape[0] * gathered.shape[1], LANES)
    for copy in copies:
        copy.wait()

    def steps(count):
        return (count + UNROLL - 1) >> 2

    def rows_at(at_ref, n, count):
        return [
            flat[pl.ds(pl.multiple_of(at_ref[n * count + i], TILE), TILE), :]
            for i in range(count)
        ]

    def add(store, index, value):
        store[index] = store[index] + two_parts(value)

    def natural(i):
        for u in range(UNROLL):
            n = i * UNROLL + u
            to = nat_to[n]
            parity = (to >> 1) & 1
            x = jnp.concatenate(rows_at(nat_at, n, 8), axis=0)
            x = jnp.where((to & 1) == parity, x, pltpu.roll(x, BLOCK, 1))
            add(blocks_m, to >> 2, jnp.where(right == parity, x, 0.0))

    def transposed(i):
        for u in range(UNROLL):
            n = i * UNROLL + u
            to = tra_to[n]
            parity = (to >> 1) & 1
            x = jnp.concatenate(rows_at(tra_at, n, 8), axis=0).T
            x = jnp.where((to & 1) == 0, x[:BLOCK], x[BLOCK:])
            x = jnp.concatenate([x, x], axis=1)
            add(blocks_m, to >> 2, jnp.where(right == parity, x, 0.0))

    def diagonal(i):
        for u in range(UNROLL):
            n = i * UNROLL + u
            to = dia_to[n]
            parity = to & 1
            parts = []
            for x in rows_at(dia_at, n, 4):
                turned = pltpu.roll(x, BLOCK, 1)
                parts.append(jnp.where(right[:TILE] == 0, x, turned))
                parts.append(jnp.where(right[:TILE] == 0, turned, x))
            x = jnp.concatenate(parts, axis=0)
            add(blocks_m, to >> 1, jnp.where(right == parity, x, 0.0))

    each(0, steps(near[3]), natural)
    each(0, steps(far[4]), transposed)
    each(0, steps(near[5]), diagonal)

    def fold(total):
        s = total[:BLOCK] + total[BLOCK:]
        return s + pltpu.roll(s, BLOCK, 1)

    def codes_of(word, g):
        n = word & 31
        group = jnp.where(g < n, ((word >> 5) & 4095) + g, 0)
        return [pairs[group * GROUP + u] for u in range(GROUP)]

    def filtered(list_ref, static):
        def product(word, groups):
            lhs, rhs = [], []
            for g in groups:
                for code in codes_of(word, g):
                    lhs.append(blocks_m[(code >> 10) & 1023])
                    rhs.append(blocks_m[code & 1023])
            return times(lhs, rhs)

        def body(i):
            words = [list_ref[i * UNROLL + u] for u in range(UNROLL)]
            for u in range(UNROLL):
                sums[u] = product(words[u], range(static))
            most = words[0] & 31
            for word in words[1:]:
                most = jnp.maximum(most, word & 31)

            def more(g):
                for u in range(UNROLL):
                    sums[u] = sums[u] + product(words[u], [g])

            each(static, most, more)
            for u in range(UNROLL):
                dest = words[u] >> 17
                value = fold(sums[u])
                add(blocks_f, dest >> 1, jnp.where(right == (dest & 1), value, 0.0))

        return body

    each(0, steps(counts[6]), filtered(fa, 3))
    each(0, steps(counts[7]), filtered(fb, 1))

    def mix(i):
        index = mixl[1 + i]
        m = blocks_m[index].astype(F32)
        f = blocks_f[index].astype(F32)
        mixed[1 + i] = two_parts(
            m[:BLOCK] + m[BLOCK:] - 1.5 * (f[:BLOCK] + f[BLOCK:])
        )

    each(0, extent[10], mix)

    def purified(first, count, static, i):
        def product(word, groups):
            lhs, rhs = [], []
            for g in groups:
                for code in codes_of(word, g):
                    lhs += [blocks_f[(code >> 10) & 1023], mixed[code >> 20]]
                    rhs += [blocks_m[code & 1023], blocks_f[code & 1023]]
            return times(lhs, rhs)

        words = [pp[first + i * count + u] for u in range(count)]
        for u in range(count):
            sums[u] = product(words[u], range(static))
        most = words[0] & 31
        for word in words[1:]:
            most = jnp.maximum(most, word & 31)

        def more(g):
            for u in range(count):
                sums[u] = sums[u] + product(words[u], [g])

        each(static, most, more)
        for u in range(count):
            c = words[u] >> 17
            lanes = pl.ds(pl.multiple_of((c >> 1) * LANES, LANES), LANES)
            value = 2.0 * fold(sums[u])
            result[:, lanes] = result[:, lanes] + jnp.where(right == (c & 1), value, 0.0)

    purified(0, 1, 3, 0)
    each(0, steps(extent[9] - 1), lambda i: purified(1, UNROLL, 1, i))


def cases(where_ref, rows, mine, act):
    tile = where_ref[0]
    skip = tile * rows - ((tile * (rows // PIECE)) >> 2) * BLOCK
    for core in range(2):
        for cut in range(0, BLOCK, PIECE):
            if not 0 < rows - (BLOCK - cut) <= BLOCK:
                continue
            upper = (core == 0) == mine
            source = pl.ds(cut, BLOCK - cut) if upper else pl.ds(0, rows - BLOCK + cut)
            target = pl.ds(0, BLOCK - cut) if upper else pl.ds(BLOCK - cut, rows - BLOCK + cut)

            @pl.when((where_ref[1] == core) & (skip == cut))
            def _():
                act(source, target)


def place_kernel(where_ref, band_ref, out_ref, held, sem):
    load = pltpu.make_async_copy(band_ref, held, sem)
    load.start()
    load.wait()

    def act(source, target):
        copy = pltpu.make_async_copy(held.at[source, :], out_ref.at[target, :], sem)
        copy.start()
        copy.wait()

    cases(where_ref, out_ref.shape[0], True, act)


def assemble_kernel(where_ref, full_ref, other_ref, out_ref, sem):
    def act(source, target):
        copy = pltpu.make_async_copy(other_ref.at[source, :], out_ref.at[target, :], sem)
        copy.start()
        copy.wait()

    cases(where_ref, out_ref.shape[0], False, act)


def smem():
    return pl.BlockSpec(memory_space=pltpu.SMEM)


def make_pack(depth, rows, share):
    count = ceil_to(rows // PIECE * PARTS, QUARTERS)
    return pl.pallas_call(
        pack_kernel,
        out_shape=jax.ShapeDtypeStruct((depth, share, LANES), F32),
        in_specs=[smem(), smem(), pl.BlockSpec(memory_space=pltpu.VMEM)],
        out_specs=pl.BlockSpec(memory_space=pl.ANY),
        scratch_shapes=[
            pltpu.VMEM((count, TILE, LANES), F32),
            pltpu.VMEM((share, LANES), F32),
            pltpu.SemaphoreType.DMA,
        ],
        compiler_params=pltpu.CompilerParams(vmem_limit_bytes=16 << 20),
        name="pack",
    )


def make_relay(depth, share, peers, length):
    return pl.pallas_call(
        relay_kernel,
        out_shape=jax.ShapeDtypeStruct((peers, length, LANES), F32),
        in_specs=[smem(), pl.BlockSpec(memory_space=pltpu.VMEM)],
        out_specs=pl.BlockSpec(memory_space=pltpu.HBM),
        scratch_shapes=[
            pltpu.VMEM((length + TILE, LANES), F32),
            pltpu.SemaphoreType.DMA,
        ],
        compiler_params=pltpu.CompilerParams(vmem_limit_bytes=61 << 20),
        name="relay",
    )


def sizes(blocks):
    listed = blocks * (1 + 2 * SLOTS)
    triangles = blocks * (SLOTS * (SLOTS - 1) // 2 + SLOTS * SLOTS // 3 + 1)
    triples = ceil_to(4 * listed + 4 * blocks * SLOTS + 6 * triangles + 64, 1024)
    return listed, triples


def book_lengths(blocks):
    return [16, blocks, blocks]


def state_lengths(blocks):
    half = (blocks + 1) // 2
    return [16, blocks, blocks * half, blocks * half]


def near_lengths(blocks):
    edges = blocks * SLOTS + UNROLL
    diagonal = blocks + UNROLL
    return [16, edges * 8, edges, diagonal * 4, diagonal]


def far_lengths(blocks):
    edges = blocks * SLOTS + UNROLL
    return [16, edges * 8, edges]


def product_lengths(blocks):
    listed, _ = sizes(blocks)
    return [16, blocks + UNROLL, listed + UNROLL]


def result_lengths(blocks):
    return [16, blocks + 1 + UNROLL, (blocks + 1) // 2 + 1]


def scalars(lengths):
    return jax.ShapeDtypeStruct((ceil_to(sum(lengths), LANES),), I32)


def make_lists(kernel, name, inputs, outputs, scratch, outside=(), **fixed):
    def body(*refs):
        kernel(*refs, **fixed)

    return pl.pallas_call(
        body,
        out_shape=outputs,
        in_specs=[smem()] * inputs,
        out_specs=[
            pl.BlockSpec(memory_space=pltpu.HBM) if i in outside else smem()
            for i in range(len(outputs))
        ],
        scratch_shapes=[pltpu.SMEM((n,), I32) for n in scratch]
        + [pltpu.SemaphoreType.DMA] * len(outside),
        compiler_params=pltpu.CompilerParams(vmem_limit_bytes=61 << 20),
        cost_estimate=pl.CostEstimate(
            flops=10_000_000_000, bytes_accessed=25_000_000, transcendentals=0
        ),
        name=name,
    )


def make_main(width, peers, length):
    blocks = width // BLOCK
    half = (blocks + 1) // 2
    listed, triples = sizes(blocks)
    return pl.pallas_call(
        main_kernel,
        out_shape=jax.ShapeDtypeStruct((BLOCK, width), F32),
        in_specs=[smem()] * 4
        + [pl.BlockSpec(memory_space=pltpu.HBM), smem()]
        + [pl.BlockSpec(memory_space=pl.ANY)] * 10,
        out_specs=pl.BlockSpec(memory_space=pltpu.VMEM),
        scratch_shapes=[
            pltpu.VMEM((2 * peers, length, LANES), F32),
            pltpu.VMEM((listed + 2, 2 * BLOCK, LANES), BF16),
            pltpu.VMEM((listed + 2, 2 * BLOCK, LANES), BF16),
            pltpu.VMEM((half + 1, 2 * BLOCK, LANES), BF16),
            pltpu.VMEM((UNROLL, 2 * BLOCK, LANES), F32),
            pltpu.SemaphoreType.DMA((10,)),
            pltpu.SMEM((ceil_to(triples, LANES),), I32),
            pltpu.SemaphoreType.DMA,
        ],
        compiler_params=pltpu.CompilerParams(vmem_limit_bytes=58 << 20),
        name="purify",
    )


def make_place(rows, width):
    return pl.pallas_call(
        place_kernel,
        out_shape=jax.ShapeDtypeStruct((rows, width), F32),
        in_specs=[smem(), pl.BlockSpec(memory_space=pl.ANY)],
        out_specs=pl.BlockSpec(memory_space=pltpu.HBM),
        scratch_shapes=[pltpu.VMEM((BLOCK, width), F32), pltpu.SemaphoreType.DMA],
        compiler_params=pltpu.CompilerParams(vmem_limit_bytes=16 << 20),
        cost_estimate=pl.CostEstimate(
            flops=1_000_000_000, bytes_accessed=8_000_000, transcendentals=0
        ),
        name="place",
    )


def make_assemble(rows, width):
    return pl.pallas_call(
        assemble_kernel,
        out_shape=jax.ShapeDtypeStruct((rows, width), F32),
        in_specs=[
            smem(), pl.BlockSpec(memory_space=pl.ANY), pl.BlockSpec(memory_space=pltpu.VMEM)
        ],
        out_specs=pl.BlockSpec(memory_space=pl.ANY),
        scratch_shapes=[pltpu.SemaphoreType.DMA],
        input_output_aliases={1: 0},
        compiler_params=pltpu.CompilerParams(vmem_limit_bytes=16 << 20),
        name="assemble",
    )


def local(density, pattern):
    rows, width = density.shape
    layers, lines, cols = (lax.axis_size(a) for a in ("layer", "row", "col"))
    across = 4
    depth = lines // across
    pieces = rows // PIECE
    share = ceil_to(pieces * PARTS, QUARTERS) // QUARTERS * TILE
    length = pieces * PARTS * depth // QUARTERS * TILE
    assert layers // 2 * cols == across
    peers = across * across
    line, col, layer = (lax.axis_index(a) for a in ("row", "col", "layer"))
    tile = line * cols + col
    z = line // across
    where = jnp.stack(
        [tile, layer % 2, (layer - z) % QUARTERS, layer, line % across, layer // 2 * cols + col]
    ).astype(I32)
    listed = pattern.T

    blocks = width // BLOCK
    count, triples = sizes(blocks)

    packed = make_pack(depth, rows, share)(where, listed, density)
    where, packed = lax.optimization_barrier((where, packed))
    fixed = dict(depth=depth, across=across, length=length, spare=count + 1, pieces=pieces)
    book, near, state = make_lists(
        near_kernel, "near", 2,
        [scalars(f(blocks)) for f in (book_lengths, near_lengths, state_lengths)], [], **fixed,
    )(where, listed)
    along = [[z * across + y for z in range(depth)] for y in range(across)]
    got = lax.all_to_all(
        packed, "row", split_axis=0, concat_axis=0, tiled=True, axis_index_groups=along
    )
    got, book, near, state = lax.optimization_barrier((got, book, near, state))
    relayed = make_relay(depth, share, across, length)(where, got)

    def ring(core, z, fixed, over_x):
        places = [(i, fixed) if over_x else (fixed, i) for i in range(across)]
        return [
            ((x // cols * 2 + core) * lines + z * across + y) * cols + x % cols
            for x, y in places
        ]

    def rings(first):
        return [
            ring(core, z, fixed, (core == 0) == first)
            for core in range(2)
            for z in range(depth)
            for fixed in range(across)
        ]

    everywhere = ("layer", "row", "col")
    relayed, book, state = lax.optimization_barrier((relayed, book, state))
    mine = lax.all_to_all(
        relayed, everywhere, split_axis=0, concat_axis=0, tiled=True, axis_index_groups=rings(True)
    )
    far, state = make_lists(
        far_kernel, "far", 4,
        [scalars(far_lengths(blocks)), scalars(state_lengths(blocks))], [], **fixed,
    )(where, listed, book, state)
    mine, far, state = lax.optimization_barrier((mine, far, state))

    def turn(value, step):
        pairs = [
            (devices[i], devices[(i + step) % across])
            for devices in rings(False)
            for i in range(across)
        ]
        return lax.ppermute(value, everywhere, pairs)

    def swap(value):
        return lax.ppermute(value, "layer", [(i, i ^ 1) for i in range(layers)])

    middle = across // 2
    left, right = turn(mine, 1), turn(mine, -1)
    product_lists, pairs, entry = make_lists(
        product_kernel, "products", 3,
        [scalars(product_lengths(blocks)), scalars([triples]), scalars([2 * (count + 2)])],
        [16, ceil_to(triples, LANES)], outside=(1,),
        blocks=blocks, spare=count + 1, pieces=pieces,
    )(where, book, state)
    left, right, product_lists, pairs, entry = lax.optimization_barrier(
        (left, right, product_lists, pairs, entry)
    )
    own = (mine, left, right, turn(left[:middle], 1), turn(right[middle:], -1))
    other = tuple(swap(part) for part in own)
    (result_lists,) = make_lists(
        result_kernel, "results", 4, [scalars(result_lengths(blocks))], [],
        blocks=blocks, pieces=pieces,
    )(where, book, state, entry)
    band = make_main(width, peers, length)(
        where, near, far, product_lists, pairs, result_lists, *own, *other
    )
    full = make_place(rows, width)(where, band)
    return make_assemble(rows, width)(where, full, swap(band))


def solution(mesh):
    in_specs = (P(("row", "col"), None), P())
    out_specs = P(("row", "col"), None)
    return jax.shard_map(local, mesh=mesh, in_specs=in_specs, out_specs=out_specs, check_vma=False)
```
